32 devices in a mesh: rows: 32 (over z, y, x, core).
Axes of the slice: x: 2, y: 2, z: 4, core: 2. Of those that a mesh axis runs over, the one named last changes fastest.
Arguments:
- features: bfloat16 [131072, 256], P('rows'), may hold values from -6 to 6
- tile_cols: int32 [1024, 6], P('rows'), may hold values from 0 to 1023, as said below
- tile_masks: int32 [1024, 6, 128, 128], P('rows'), may hold values from 0 to 1, as said below
- degree: int32 [131072], P('rows'), may hold values from 1 to 768, as said below
- weight: bfloat16 [512, 256], replicated, may hold values from -0.25 to 0.25
Outputs:
- embedding: bfloat16 [131072, 256], P('rows')
The draws below stay inside these ranges and needn't reach their ends.
Inputs may be any that keep to these rules, and one draw needn't show every extreme that they name: `tile_cols`: each row block has exactly 2 tiles whose column block lies on the device that holds the row block (column block c lies on device c // 32); its other 4 tiles name column blocks of other devices. Over the row blocks of one device, at most 10 tiles name column blocks of any one other device, and exactly 10 for some other device; they name at most 5 distinct column blocks of any one other device, and exactly 5 for some. `tile_masks`: every item has at least one neighbour in the first tile of its row block. degree of item r * 128 + a is the number of ones in tile_masks[r, t, a, :] over all t; on every device some item reaches the most.
All inputs are finite; a program needn't handle non-finite values.
Results may differ from the reference program's by a relative error of at most 0.0027.
Values may be sent and summed in bfloat16 or wider, within the bound.
No kernel may reach another device: no remote copies, remote signals or barrier semaphores. Data moves between devices by JAX's collectives and lax.ppermute only.
A program may use at most 192 MiB of HBM per device.

```python
import jax
import jax.numpy as jnp
from jax import lax

D = 256
HID = 256
TILE = 128
RB_DEV = 32
LOC_PB = 2
REM_PB = 4
CAPU = 5
CAP = 10
TPB = 6
NB = 1024
ITEMS = 131072
N_ROWS = 32


def pattern(key):

    def one_device(device):
        base = jax.random.fold_in(key, device)
        keys = jax.random.split(base, 12)
        remote_count = RB_DEV * REM_PB
        forced = jax.random.randint(keys[0], (), 0, N_ROWS - 1)
        slot_ids = jax.random.permutation(keys[1], (N_ROWS - 2) * CAPU)[:remote_count - CAP]
        others = (slot_ids // CAPU).astype(jnp.int32)
        other_picks = (slot_ids % CAPU).astype(jnp.int32)
        others = others + (others >= forced).astype(jnp.int32)
        offsets = jnp.concatenate([jnp.full((CAP,), forced, jnp.int32), others])
        picks = jnp.concatenate([jnp.arange(CAP, dtype=jnp.int32) % CAPU, other_picks])
        shuffle = jax.random.permutation(keys[3], remote_count)
        offsets = offsets[shuffle]
        picks = picks[shuffle]
        owners = (device + 1 + offsets) % N_ROWS
        hot_first = jax.random.randint(keys[4], (N_ROWS,), 0, RB_DEV)
        stride = RB_DEV // CAPU
        chosen = (hot_first[owners] + picks * stride) % RB_DEV
        remote_cols = (owners * RB_DEV + chosen).reshape(RB_DEV, REM_PB)
        local_cols = device * RB_DEV + jax.random.randint(keys[6], (RB_DEV, LOC_PB), 0, RB_DEV)
        columns = jnp.concatenate([local_cols, remote_cols], axis=1)
        rotate = jax.random.randint(keys[7], (RB_DEV, 1), 0, TPB)
        where_from = (jnp.arange(TPB, dtype=jnp.int32)[None, :] + rotate) % TPB
        columns = jnp.take_along_axis(columns, where_from, axis=1).astype(jnp.int32)
        rates = jax.random.randint(keys[8], (RB_DEV, 1, TILE, 1), 4, 64)
        noise = jax.random.randint(keys[9], (RB_DEV, TPB, TILE, TILE), 0, 1024)
        bitmap = (noise < rates).astype(jnp.int32)
        anchor = jax.random.randint(keys[10], (RB_DEV, TILE), 0, TILE)
        hit = (jnp.arange(TILE, dtype=jnp.int32)[None, None, :] == anchor[:, :, None]).astype(jnp.int32)
        bitmap = bitmap.at[:, 0].set(jnp.maximum(bitmap[:, 0], hit))
        dense_item = jax.random.randint(keys[11], (), 0, RB_DEV * TILE)
        item_ids = jnp.arange(RB_DEV * TILE, dtype=jnp.int32).reshape(RB_DEV, 1, TILE, 1)
        bitmap = jnp.maximum(bitmap, (item_ids == dense_item).astype(jnp.int32))
        counts = jnp.sum(bitmap, axis=(1, 3)).reshape(RB_DEV * TILE).astype(jnp.int32)
        return (columns, bitmap, counts)
    columns, bitmap, counts = lax.map(one_device, jnp.arange(N_ROWS, dtype=jnp.int32))
    return (columns.reshape(NB, TPB), bitmap.reshape(NB, TPB, TILE, TILE), counts.reshape(ITEMS))


def draw_tile_cols(key, part):
    return pattern(key)[0]


def draw_tile_masks(key, part):
    return pattern(key)[1]


def draw_degree(key, part):
    return pattern(key)[2]


def steps_of(stream_key, shape, cuts, least, largest):
    def one(axis_at, blocks):
        steps = jax.random.uniform(jax.random.fold_in(jax.random.fold_in(stream_key, 6), axis_at), (blocks,), jnp.float32, least / len(cuts), largest / len(cuts))
        return jnp.repeat(jnp.exp(steps), shape[axis_at] // blocks).reshape((-1,) + (1,) * (len(shape) - axis_at - 1))

    factor_of = one(*cuts[0])
    for cut in cuts[1:]:
        factor_of = factor_of * one(*cut)
    return factor_of


def scatter_about(own_key, dims, width, most, shards=(), held_as=jnp.bfloat16):
    drawn = jax.random.normal(own_key, dims, jnp.float32) * width
    if len(shards) > 0:
        drawn = steps_of(own_key, dims, shards, -0.22, 0.18) * drawn
    return jnp.clip(drawn, min=-most, max=most).astype(held_as)


def setup_inputs(seed: int = 0) -> dict:
    splits = jax.random.split(jax.random.key(seed), 6)
    features = scatter_about(splits[0], (ITEMS, D), 1.0, 6.0, ((0, 32),))
    tile_cols = draw_tile_cols(jax.random.fold_in(splits[5], 71), 0)
    tile_masks = draw_tile_masks(jax.random.fold_in(splits[5], 71), 0)
    degree = draw_degree(jax.random.fold_in(splits[5], 71), 0)
    weight = scatter_about(splits[4], (2 * D, HID), (2 * D) ** -0.5, 0.25)
    return dict(features=features, tile_cols=tile_cols, tile_masks=tile_masks, degree=degree, weight=weight)


def reference(features, tile_cols, tile_masks, degree, weight):
    blocks = features.reshape(NB, TILE, D)

    def one_block(inputs):
        columns, pattern_masks = inputs
        picked = blocks[columns].astype(jnp.float32)
        return jnp.einsum('tij,tjd->id', pattern_masks.astype(jnp.float32), picked)
    sums = lax.map(one_block, (tile_cols, tile_masks)).reshape(ITEMS, D)
    mean = (sums / degree.astype(jnp.float32)[:, None]).astype(jnp.bfloat16)
    joined = jnp.concatenate([features, mean], axis=1)
    hidden = jnp.maximum(jnp.dot(joined, weight, preferred_element_type=jnp.float32), 0.0)
    scale = lax.rsqrt(lax.optimization_barrier(jnp.sum(hidden * hidden, axis=1, keepdims=True)) + 1e-06)
    return (hidden * scale).astype(jnp.bfloat16)
```

```python
import functools

import jax
import jax.numpy as jnp
from jax import lax
from jax.experimental import pallas as pl
from jax.experimental.pallas import tpu as pltpu
from jax.sharding import PartitionSpec as P

REM_PB = 4
PLANES = 4


def arrival_order(planes):
    order = []
    for z in range(planes):
        mine = [(0, 0)]
        for step in range(1, planes):
            if z + step < planes:
                mine.append((step, -1))
            if z - step >= 0:
                mine.append((step, 1))
        order.append(mine)
    return order


def pick_row(table, z):
    return jnp.sum(jnp.where(jnp.arange(table.shape[0])[:, None] == z, table, 0), axis=0)


def choose_kernel(which, ids, *refs, sources, outputs, capacity):
    froms, tos, sems = refs[:sources], refs[sources : sources + outputs], refs[-1]
    for j, source in enumerate(froms):

        @pl.when(which[0] == j)
        def _():
            copies = []
            for o, out in enumerate(tos):
                for s in range(capacity):
                    n = o * capacity + s
                    copies.append(pltpu.make_async_copy(source.at[ids[n]], out.at[s], sems.at[n]))
            for copy in copies:
                copy.start()
            for copy in copies:
                copy.wait()


def choose(which, ids, froms, outputs, capacity):
    block = froms[0].shape[1:]
    moved = outputs * capacity * block[0] * block[1] * 2
    return pl.pallas_call(
        functools.partial(choose_kernel, sources=len(froms), outputs=outputs, capacity=capacity),
        grid_spec=pltpu.PrefetchScalarGridSpec(
            num_scalar_prefetch=2,
            grid=(1,),
            in_specs=[pl.BlockSpec(memory_space=pl.ANY)] * len(froms),
            out_specs=[pl.BlockSpec(memory_space=pl.ANY)] * outputs,
            scratch_shapes=[pltpu.SemaphoreType.DMA((outputs * capacity,))],
        ),
        out_shape=[jax.ShapeDtypeStruct((capacity,) + block, froms[0].dtype)] * outputs,
        cost_estimate=pl.CostEstimate(flops=0, bytes_accessed=2 * moved, transcendentals=0),
        name="choose_blocks",
    )(which, ids, *froms)


def layer_kernel(slots, *refs, pieces, starts, per_block):
    froms = refs[:pieces]
    masks, degree, weight, out, table, sems = refs[pieces:]
    row = pl.program_id(0)
    tile, width = table.shape[1:]

    @pl.when(row == 0)
    def _():
        copies = [
            pltpu.make_async_copy(piece, table.at[pl.ds(at, piece.shape[0])], sems.at[n])
            for n, (piece, at) in enumerate(zip(froms, starts))
        ]
        for copy in copies:
            copy.start()
        for copy in copies:
            copy.wait()

    sums = jnp.zeros((tile, width), jnp.float32)
    for t in range(per_block):
        mask = masks[0, t].astype(jnp.float32).astype(jnp.bfloat16)
        picked = table[slots[row * per_block + t]]
        sums = sums + jnp.dot(mask, picked, preferred_element_type=jnp.float32)
    count = jnp.broadcast_to(degree[pl.ds(row, 1), :].astype(jnp.float32), (tile, tile)).T
    count = jnp.concatenate([count] * (width // tile), axis=1)
    mean = (sums / count).astype(jnp.bfloat16)
    hidden = jnp.dot(table[row], weight[:width], preferred_element_type=jnp.float32)
    hidden = hidden + jnp.dot(mean, weight[width:], preferred_element_type=jnp.float32)
    hidden = jnp.maximum(hidden, 0.0)
    scale = lax.rsqrt(jnp.sum(hidden * hidden, axis=1, keepdims=True) + 1e-06)
    out[...] = (hidden * scale).astype(jnp.bfloat16)


def layer(slots, froms, starts, blocks_in_table, tile_masks, degree, weight):
    rows, per_block, tile, _ = tile_masks.shape
    width = weight.shape[0] // 2
    out_width = weight.shape[1]
    return pl.pallas_call(
        functools.partial(layer_kernel, pieces=len(froms), starts=starts, per_block=per_block),
        grid_spec=pltpu.PrefetchScalarGridSpec(
            num_scalar_prefetch=1,
            grid=(rows,),
            in_specs=[pl.BlockSpec(memory_space=pl.ANY)] * len(froms)
            + [
                pl.BlockSpec((1, per_block, tile, tile), lambda r, s: (r, 0, 0, 0)),
                pl.BlockSpec((rows, tile), lambda r, s: (0, 0)),
                pl.BlockSpec((2 * width, out_width), lambda r, s: (0, 0)),
            ],
            out_specs=pl.BlockSpec((tile, out_width), lambda r, s: (r, 0)),
            scratch_shapes=[
                pltpu.VMEM((blocks_in_table, tile, width), jnp.bfloat16),
                pltpu.SemaphoreType.DMA((len(froms),)),
            ],
        ),
        out_shape=jax.ShapeDtypeStruct((rows * tile, out_width), jnp.bfloat16),
        compiler_params=pltpu.CompilerParams(vmem_limit_bytes=40 * 1024 * 1024),
        cost_estimate=pl.CostEstimate(
            flops=2 * rows * tile * (per_block * tile + 2 * width) * width,
            bytes_accessed=rows * per_block * tile * tile * 4 + blocks_in_table * tile * width * 2,
            transcendentals=rows * tile,
        ),
        name="sage_layer",
    )(slots, *froms, tile_masks, degree, weight)


def on_device(features, tile_cols, tile_masks, degree, weight):
    blocks_here, per_block = tile_cols.shape
    tile = tile_masks.shape[2]
    width = features.shape[1]
    peers = lax.axis_size("rows")
    planes = PLANES if peers % PLANES == 0 else 1
    plane = peers // planes
    myself = lax.axis_index("rows")
    z, p = myself // plane, myself % plane
    capacity = max(2, (REM_PB * blocks_here + peers - 2) // (peers - 1))
    order = arrival_order(planes)
    local = features.reshape(blocks_here, tile, width)

    arrived = {(0, 0): local}
    for step in range(1, planes):
        for way in (-1, 1):
            held = arrived[(step - 1, way)] if step > 1 else local
            pairs = [
                (a * plane + q, (a + way) * plane + q)
                for a in range(planes)
                if 0 <= a + way < planes and 0 <= a - way * (step - 1) < planes
                for q in range(plane)
            ]
            arrived[(step, way)] = lax.ppermute(held, "rows", pairs)

    columns = tile_cols.reshape(-1)
    all_columns = lax.all_gather(columns, "rows")
    partners = p ^ jnp.arange(plane, dtype=jnp.int32)
    asked = all_columns[z * plane + partners]
    plane_at = jnp.array(
        [[a - way * step for step, way in order[a]] for a in range(planes)], jnp.int32
    )
    sources = pick_row(plane_at, z)
    line = sources * plane + p
    blocks = jnp.arange(blocks_here, dtype=jnp.int32)
    wanted = (line[:, None] * blocks_here + blocks[None, :]).reshape(-1)
    need = jnp.any(asked[:, :, None] == wanted[None, None, :], axis=1)
    need = need.reshape(plane, planes, blocks_here).astype(jnp.int32)
    below = blocks[:, None] > blocks[None, :]
    place = jnp.sum(jnp.where(below, need[:, :, None, :], 0), axis=3)
    seat = jnp.arange(capacity, dtype=jnp.int32)
    chosen = jnp.sum(
        jnp.where(
            (need[:, :, None, :] == 1) & (place[:, :, None, :] == seat[:, None]), blocks, 0
        ),
        axis=3,
    )

    owners, within = columns // blocks_here, columns % blocks_here
    positions = jnp.arange(columns.shape[0], dtype=jnp.int32)
    same = columns[:, None] == columns[None, :]
    first = ~jnp.any(same & (positions[None, :] < positions[:, None]), axis=1)
    ahead = (owners[:, None] == owners[None, :]) & (columns[None, :] < columns[:, None])
    ranks = jnp.sum(ahead & first[None, :], axis=1, dtype=jnp.int32)
    stage_at = jnp.array(
        [
            [[a - way * step for step, way in order[a]].index(b) for b in range(planes)]
            for a in range(planes)
        ],
        jnp.int32,
    )
    stages = pick_row(stage_at, z)
    their_plane = owners // plane
    stage = jnp.sum(
        jnp.where(their_plane[:, None] == jnp.arange(planes), stages[None, :], 0), axis=1
    )
    partner = (owners % plane) ^ p
    slots = jnp.where(
        owners == myself,
        within,
        blocks_here + (stage * plane + partner) * capacity + ranks,
    )

    froms, starts = [local], [0]
    for k in range(planes):
        kinds = sorted(set(order[a][k] for a in range(planes)))
        which_at = jnp.array([[kinds.index(order[a][k])] for a in range(planes)], jnp.int32)
        skip = 1 if k == 0 else 0
        ids = chosen[skip:, k, :].reshape(-1)
        picked = choose(
            pick_row(which_at, z), ids, [arrived[kind] for kind in kinds], plane - skip, capacity
        )
        for m in range(skip, plane):
            part = picked[m - skip]
            if m > 0:
                pairs = [
                    (a * plane + q, a * plane + (q ^ m)) for a in range(planes) for q in range(plane)
                ]
                part = lax.ppermute(part, "rows", pairs)
            froms.append(part)
            starts.append(blocks_here + (k * plane + m) * capacity)

    return layer(
        slots,
        froms,
        tuple(starts),
        blocks_here + peers * capacity,
        tile_masks,
        degree.reshape(blocks_here, tile),
        weight,
    )


def solution(mesh):
    in_specs = (P("rows", None), P("rows", None), P("rows", None, None, None), P("rows"), P())
    out_specs = P("rows", None)
    return jax.shard_map(
        on_device, mesh=mesh, in_specs=in_specs, out_specs=out_specs, check_vma=False
    )
```

```python
import functools

import jax
import jax.numpy as jnp
from jax import lax
from jax.experimental import pallas as pl
from jax.experimental.pallas import tpu as pltpu
from jax.sharding import PartitionSpec as P

REM_PB = 4
PLANES = 4


def arrival_order(planes):
    order = []
    for z in range(planes):
        mine = [(0, 0)]
        for step in range(1, planes):
            if z + step < planes:
                mine.append((step, -1))
            if z - step >= 0:
                mine.append((step, 1))
        order.append(mine)
    return order


def pick_row(table, z):
    return jnp.sum(jnp.where(jnp.arange(table.shape[0])[:, None] == z, table, 0), axis=0)


def choose_kernel(which, ids, *refs, sources):
    froms, out, sem = refs[:sources], refs[sources], refs[-1]
    count = out.shape[0]
    for j, source in enumerate(froms):

        @pl.when(which[0] == j)
        def _():
            copies = [
                pltpu.make_async_copy(source.at[ids[n]], out.at[n], sem.at[n]) for n in range(count)
            ]
            for copy in copies:
                copy.start()
            for copy in copies:
                copy.wait()


def choose(which, ids, froms):
    block = froms[0].shape[1:]
    count = ids.shape[0]
    moved = count * block[0] * block[1] * 2
    return pl.pallas_call(
        functools.partial(choose_kernel, sources=len(froms)),
        grid_spec=pltpu.PrefetchScalarGridSpec(
            num_scalar_prefetch=2,
            grid=(1,),
            in_specs=[pl.BlockSpec(memory_space=pltpu.HBM)] * len(froms),
            out_specs=pl.BlockSpec((count,) + block, lambda i, w, s: (0, 0, 0)),
            scratch_shapes=[pltpu.SemaphoreType.DMA((count,))],
        ),
        out_shape=jax.ShapeDtypeStruct((count,) + block, froms[0].dtype),
        compiler_params=pltpu.CompilerParams(vmem_limit_bytes=32 * 1024 * 1024),
        cost_estimate=pl.CostEstimate(flops=0, bytes_accessed=2 * moved, transcendentals=0),
        name="choose_blocks",
    )(which, ids, *froms)


def layer_kernel(slots, *refs, pieces, starts):
    froms = refs[:pieces]
    masks, degree, weight, out, table, means, sems = refs[pieces:]
    step = pl.program_id(0)
    rows, per_block = masks.shape[:2]
    tile, width = table.shape[1:]

    @pl.when(step == 0)
    def _():
        copies = [
            pltpu.make_async_copy(piece, table.at[pl.ds(at, piece.shape[0])], sems.at[n])
            for n, (piece, at) in enumerate(zip(froms, starts))
        ]
        for copy in copies:
            copy.start()
        for copy in copies:
            copy.wait()

    for r in range(rows):
        row = step * rows + r
        mask = jnp.concatenate(
            [masks[r, t].astype(jnp.float32).astype(jnp.bfloat16) for t in range(per_block)], axis=1
        )
        picked = jnp.concatenate(
            [table[slots[row * per_block + t]] for t in range(per_block)], axis=0
        )
        sums = jnp.dot(mask, picked, preferred_element_type=jnp.float32)
        count = jnp.broadcast_to(degree[pl.ds(row, 1), :].astype(jnp.float32), (tile, tile)).T
        count = jnp.concatenate([count] * (width // tile), axis=1)
        means[pl.ds(r * tile, tile), :] = (sums / count).astype(jnp.bfloat16)
    own = table[pl.ds(step * rows, rows)].reshape(rows * tile, width)
    hidden = jnp.dot(own, weight[:width], preferred_element_type=jnp.float32)
    hidden = hidden + jnp.dot(means[...], weight[width:], preferred_element_type=jnp.float32)
    hidden = jnp.maximum(hidden, 0.0)
    scale = lax.rsqrt(jnp.sum(hidden * hidden, axis=1, keepdims=True) + 1e-06)
    out[...] = (hidden * scale).astype(jnp.bfloat16)


def layer(slots, froms, starts, blocks_in_table, tile_masks, degree, weight):
    blocks_here, per_block, tile, _ = tile_masks.shape
    width = weight.shape[0] // 2
    out_width = weight.shape[1]
    rows = 4 if blocks_here % 4 == 0 else 1
    return pl.pallas_call(
        functools.partial(layer_kernel, pieces=len(froms), starts=starts),
        grid_spec=pltpu.PrefetchScalarGridSpec(
            num_scalar_prefetch=1,
            grid=(blocks_here // rows,),
            in_specs=[pl.BlockSpec(memory_space=pltpu.HBM)] * len(froms)
            + [
                pl.BlockSpec((rows, per_block, tile, tile), lambda r, s: (r, 0, 0, 0)),
                pl.BlockSpec((blocks_here, tile), lambda r, s: (0, 0)),
                pl.BlockSpec((2 * width, out_width), lambda r, s: (0, 0)),
            ],
            out_specs=pl.BlockSpec((rows * tile, out_width), lambda r, s: (r, 0)),
            scratch_shapes=[
                pltpu.VMEM((blocks_in_table, tile, width), jnp.bfloat16),
                pltpu.VMEM((rows * tile, width), jnp.bfloat16),
                pltpu.SemaphoreType.DMA((len(froms),)),
            ],
        ),
        out_shape=jax.ShapeDtypeStruct((blocks_here * tile, out_width), jnp.bfloat16),
        compiler_params=pltpu.CompilerParams(vmem_limit_bytes=48 * 1024 * 1024),
        cost_estimate=pl.CostEstimate(
            flops=2 * blocks_here * tile * (per_block * tile + 2 * width) * width,
            bytes_accessed=blocks_here * per_block * tile * tile * 4 + blocks_in_table * tile * width * 2,
            transcendentals=blocks_here * tile,
        ),
        name="sage_layer",
    )(slots, *froms, tile_masks, degree, weight)


def on_device(features, tile_cols, tile_masks, degree, weight):
    blocks_here, per_block = tile_cols.shape
    tile = tile_masks.shape[2]
    width = features.shape[1]
    peers = lax.axis_size("rows")
    planes = PLANES if peers % PLANES == 0 else 1
    plane = peers // planes
    myself = lax.axis_index("rows")
    z, p = myself // plane, myself % plane
    capacity = max(2, (REM_PB * blocks_here + peers - 2) // (peers - 1))
    order = arrival_order(planes)

    columns = tile_cols.reshape(-1)
    shifted = [columns]
    for m in range(1, plane):
        pairs = [
            (a * plane + q, a * plane + (q ^ m)) for a in range(planes) for q in range(plane)
        ]
        shifted.append(lax.ppermute(columns, "rows", pairs))
    features, asked = lax.optimization_barrier((features, jnp.stack(shifted)))
    local = features.reshape(blocks_here, tile, width)

    arrived = {(0, 0): local}
    for step in range(1, planes):
        for way in (-1, 1):
            held = arrived[(step - 1, way)] if step > 1 else local
            pairs = [
                (a * plane + q, (a + way) * plane + q)
                for a in range(planes)
                if 0 <= a + way < planes and 0 <= a - way * (step - 1) < planes
                for q in range(plane)
            ]
            arrived[(step, way)] = lax.ppermute(held, "rows", pairs)

    plane_at = jnp.array(
        [[a - way * step for step, way in order[a]] for a in range(planes)], jnp.int32
    )
    sources = pick_row(plane_at, z)
    line = sources * plane + p
    blocks = jnp.arange(blocks_here, dtype=jnp.int32)
    wanted = (line[:, None] * blocks_here + blocks[None, :]).reshape(-1)
    need = jnp.any(asked[:, :, None] == wanted[None, None, :], axis=1)
    need = need.reshape(plane, planes, blocks_here).astype(jnp.int32)
    below = blocks[:, None] > blocks[None, :]
    place = jnp.sum(jnp.where(below, need[:, :, None, :], 0), axis=3)
    seat = jnp.arange(capacity, dtype=jnp.int32)
    chosen = jnp.sum(
        jnp.where(
            (need[:, :, None, :] == 1) & (place[:, :, None, :] == seat[:, None]), blocks, 0
        ),
        axis=3,
    )

    owners, within = columns // blocks_here, columns % blocks_here
    positions = jnp.arange(columns.shape[0], dtype=jnp.int32)
    same = columns[:, None] == columns[None, :]
    first = ~jnp.any(same & (positions[None, :] < positions[:, None]), axis=1)
    ahead = (owners[:, None] == owners[None, :]) & (columns[None, :] < columns[:, None])
    ranks = jnp.sum(ahead & first[None, :], axis=1, dtype=jnp.int32)
    stage_at = jnp.array(
        [
            [[a - way * step for step, way in order[a]].index(b) for b in range(planes)]
            for a in range(planes)
        ],
        jnp.int32,
    )
    stages = pick_row(stage_at, z)
    their_plane = owners // plane
    stage = jnp.sum(
        jnp.where(their_plane[:, None] == jnp.arange(planes), stages[None, :], 0), axis=1
    )
    slots = jnp.where(
        owners == myself,
        within,
        blocks_here + (stage * plane + owners % plane) * capacity + ranks,
    )

    others = jnp.arange(plane, dtype=jnp.int32)
    swap = (others[:, None] ^ p) == others[None, :]
    chosen = jnp.sum(jnp.where(swap[:, :, None, None], chosen[None], 0), axis=1)
    groups = [[a * plane + q for q in range(plane)] for a in range(planes)]
    froms, starts = [local], [0]
    for k in range(planes):
        kinds = sorted(set(order[a][k] for a in range(planes)))
        which_at = jnp.array([[kinds.index(order[a][k])] for a in range(planes)], jnp.int32)
        ids = chosen[:, k, :].reshape(-1)
        picked = choose(pick_row(which_at, z), ids, [arrived[kind] for kind in kinds])
        froms.append(
            lax.all_to_all(
                picked, "rows", split_axis=0, concat_axis=0, axis_index_groups=groups, tiled=True
            )
        )
        starts.append(blocks_here + k * plane * capacity)

    return layer(
        slots,
        froms,
        tuple(starts),
        blocks_here + peers * capacity,
        tile_masks,
        degree.reshape(blocks_here, tile),
        weight,
    )


def solution(mesh):
    in_specs = (P("rows", None), P("rows", None), P("rows", None, None, None), P("rows"), P())
    out_specs = P("rows", None)
    return jax.shard_map(
        on_device, mesh=mesh, in_specs=in_specs, out_specs=out_specs, check_vma=False
    )
```

```python
import functools

import jax
import jax.numpy as jnp
from jax import lax
from jax.experimental import pallas as pl
from jax.experimental.pallas import tpu as pltpu
from jax.sharding import PartitionSpec as P

REM_PB = 4
PLANES = 4
HALVES = 2
CHOOSE_WEIGHT = 200


def arrival_order(planes):
    order = []
    for z in range(planes):
        mine = [(0, 0)]
        for step in range(1, planes):
            if z + step < planes:
                mine.append((step, -1))
            if z - step >= 0:
                mine.append((step, 1))
        order.append(mine)
    return order


def pick_row(table, z):
    return jnp.sum(jnp.where(jnp.arange(table.shape[0])[:, None] == z, table, 0), axis=0)


def choose_kernel(which, ids, *refs, kinds, parts):
    froms, out, held, in_sems, out_sems = refs[: kinds * parts], *refs[kinds * parts :]
    count = out.shape[0]
    tall = out.shape[1] // parts

    def arrival(source, n, h):
        here = held.at[n, pl.ds(h * tall, tall)]
        return pltpu.make_async_copy(source.at[ids[n]], here, in_sems.at[n, h])

    for j in range(kinds):

        @pl.when(which[0] == j)
        def _():
            for n in range(count):
                for h in range(parts):
                    arrival(froms[j * parts + h], n, h).start()

    leaving = []
    for n in range(count):
        for h in range(parts):
            arrival(froms[h], n, h).wait()
        leaving.append(pltpu.make_async_copy(held.at[n], out.at[n], out_sems.at[n]))
        leaving[-1].start()
    for copy in leaving:
        copy.wait()


def choose(which, ids, froms):
    parts = len(froms[0])
    _, tall, width = froms[0][0].shape
    block = (parts * tall, width)
    count = ids.shape[0]
    moved = count * block[0] * block[1] * 2
    return pl.pallas_call(
        functools.partial(choose_kernel, kinds=len(froms), parts=parts),
        grid_spec=pltpu.PrefetchScalarGridSpec(
            num_scalar_prefetch=2,
            grid=(1,),
            in_specs=[pl.BlockSpec(memory_space=pltpu.HBM)] * (parts * len(froms)),
            out_specs=pl.BlockSpec(memory_space=pltpu.HBM),
            scratch_shapes=[
                pltpu.VMEM((count,) + block, froms[0][0].dtype),
                pltpu.SemaphoreType.DMA((count, parts)),
                pltpu.SemaphoreType.DMA((count,)),
            ],
        ),
        out_shape=jax.ShapeDtypeStruct((count,) + block, froms[0][0].dtype),
        compiler_params=pltpu.CompilerParams(vmem_limit_bytes=32 * 1024 * 1024),
        cost_estimate=pl.CostEstimate(
            flops=0, bytes_accessed=CHOOSE_WEIGHT * moved, transcendentals=0
        ),
        name="choose_blocks",
    )(which, ids, *[part for source in froms for part in source])


def layer_kernel(slots, *refs, pieces, starts):
    froms = refs[:pieces]
    masks, degree, weight, out, table, means, sems = refs[pieces:]
    step = pl.program_id(0)
    rows, per_block = masks.shape[:2]
    tile, width = table.shape[1:]

    @pl.when(step == 0)
    def _():
        copies = [
            pltpu.make_async_copy(
                piece,
                table.at[pl.ds(at, piece.shape[0]), pl.ds(top, piece.shape[1])],
                sems.at[n],
            )
            for n, (piece, (at, top)) in enumerate(zip(froms, starts))
        ]
        for copy in copies:
            copy.start()
        for copy in copies:
            copy.wait()

    for r in range(rows):
        row = step * rows + r
        mask = jnp.concatenate(
            [masks[r, t].astype(jnp.float32).astype(jnp.bfloat16) for t in range(per_block)], axis=1
        )
        picked = jnp.concatenate(
            [table[slots[row * per_block + t]] for t in range(per_block)], axis=0
        )
        sums = jnp.dot(mask, picked, preferred_element_type=jnp.float32)
        count = jnp.broadcast_to(degree[pl.ds(row, 1), :].astype(jnp.float32), (tile, tile)).T
        count = jnp.concatenate([count] * (width // tile), axis=1)
        means[pl.ds(r * tile, tile), :] = (sums / count).astype(jnp.bfloat16)
    own = table[pl.ds(step * rows, rows)].reshape(rows * tile, width)
    hidden = jnp.dot(own, weight[:width], preferred_element_type=jnp.float32)
    hidden = hidden + jnp.dot(means[...], weight[width:], preferred_element_type=jnp.float32)
    hidden = jnp.maximum(hidden, 0.0)
    scale = lax.rsqrt(jnp.sum(hidden * hidden, axis=1, keepdims=True) + 1e-06)
    out[...] = (hidden * scale).astype(jnp.bfloat16)


def layer(slots, froms, starts, blocks_in_table, tile_masks, degree, weight):
    blocks_here, per_block, tile, _ = tile_masks.shape
    width = weight.shape[0] // 2
    out_width = weight.shape[1]
    rows = 4 if blocks_here % 4 == 0 else 1
    return pl.pallas_call(
        functools.partial(layer_kernel, pieces=len(froms), starts=starts),
        grid_spec=pltpu.PrefetchScalarGridSpec(
            num_scalar_prefetch=1,
            grid=(blocks_here // rows,),
            in_specs=[pl.BlockSpec(memory_space=pltpu.HBM)] * len(froms)
            + [
                pl.BlockSpec((rows, per_block, tile, tile), lambda r, s: (r, 0, 0, 0)),
                pl.BlockSpec((blocks_here, tile), lambda r, s: (0, 0)),
                pl.BlockSpec((2 * width, out_width), lambda r, s: (0, 0)),
            ],
            out_specs=pl.BlockSpec((rows * tile, out_width), lambda r, s: (r, 0)),
            scratch_shapes=[
                pltpu.VMEM((blocks_in_table, tile, width), jnp.bfloat16),
                pltpu.VMEM((rows * tile, width), jnp.bfloat16),
                pltpu.SemaphoreType.DMA((len(froms),)),
            ],
        ),
        out_shape=jax.ShapeDtypeStruct((blocks_here * tile, out_width), jnp.bfloat16),
        compiler_params=pltpu.CompilerParams(vmem_limit_bytes=48 * 1024 * 1024),
        cost_estimate=pl.CostEstimate(
            flops=2 * blocks_here * tile * (per_block * tile + 2 * width) * width,
            bytes_accessed=blocks_here * per_block * tile * tile * 4 + blocks_in_table * tile * width * 2,
            transcendentals=blocks_here * tile,
        ),
        name="sage_layer",
    )(slots, *froms, tile_masks, degree, weight)


def on_device(features, tile_cols, tile_masks, degree, weight):
    blocks_here, per_block = tile_cols.shape
    tile = tile_masks.shape[2]
    width = features.shape[1]
    peers = lax.axis_size("rows")
    planes = PLANES if peers % PLANES == 0 else 1
    plane = peers // planes
    myself = lax.axis_index("rows")
    z, p = myself // plane, myself % plane
    capacity = max(2, (REM_PB * blocks_here + peers - 2) // (peers - 1))
    order = arrival_order(planes)

    local = features.reshape(blocks_here, tile, width)
    groups = [[a * plane + q for q in range(plane)] for a in range(planes)]

    columns = tile_cols.reshape(-1)
    asked = lax.all_to_all(
        jnp.broadcast_to(columns, (plane,) + columns.shape),
        "rows",
        split_axis=0,
        concat_axis=0,
        axis_index_groups=groups,
        tiled=True,
    )

    tall = tile // HALVES
    held = [local[:, :tall], local[:, tall:]]
    held[1], asked = lax.optimization_barrier((held[1], asked))
    arrived = [{} for _ in range(HALVES)]
    for step in range(1, planes):
        for h in range(HALVES):
            for way in (-1, 1):
                pairs = [
                    (a * plane + q, (a + way) * plane + q)
                    for a in range(planes)
                    if 0 <= a + way < planes and 0 <= a - way * (step - 1) < planes
                    for q in range(plane)
                ]
                source = held[h] if step == 1 else arrived[h][step - 1, way]
                arrived[h][step, way] = lax.ppermute(source, "rows", pairs)

    plane_at = jnp.array(
        [[a - way * step for step, way in order[a]] for a in range(planes)], jnp.int32
    )
    sources = pick_row(plane_at, z)
    line = sources * plane + p
    blocks = jnp.arange(blocks_here, dtype=jnp.int32)
    wanted = (line[:, None] * blocks_here + blocks[None, :]).reshape(-1)
    need = jnp.any(asked[:, :, None] == wanted[None, None, :], axis=1)
    need = need.reshape(plane, planes, blocks_here).astype(jnp.int32)
    below = blocks[:, None] > blocks[None, :]
    place = jnp.sum(jnp.where(below, need[:, :, None, :], 0), axis=3)
    seat = jnp.arange(capacity, dtype=jnp.int32)
    chosen = jnp.sum(
        jnp.where(
            (need[:, :, None, :] == 1) & (place[:, :, None, :] == seat[:, None]), blocks, 0
        ),
        axis=3,
    )

    owners, within = columns // blocks_here, columns % blocks_here
    positions = jnp.arange(columns.shape[0], dtype=jnp.int32)
    same = columns[:, None] == columns[None, :]
    first = ~jnp.any(same & (positions[None, :] < positions[:, None]), axis=1)
    ahead = (owners[:, None] == owners[None, :]) & (columns[None, :] < columns[:, None])
    ranks = jnp.sum(ahead & first[None, :], axis=1, dtype=jnp.int32)
    stage_at = jnp.array(
        [
            [[a - way * step for step, way in order[a]].index(b) for b in range(planes)]
            for a in range(planes)
        ],
        jnp.int32,
    )
    stages = pick_row(stage_at, z)
    their_plane = owners // plane
    stage = jnp.sum(
        jnp.where(their_plane[:, None] == jnp.arange(planes), stages[None, :], 0), axis=1
    )
    slots = jnp.where(
        owners == myself,
        within,
        blocks_here + (stage * plane + owners % plane) * capacity + ranks,
    )

    froms, starts = [local], [(0, 0)]
    for k in range(planes):
        kinds = sorted(set(order[a][k] for a in range(planes)))
        which_at = jnp.array([[kinds.index(order[a][k])] for a in range(planes)], jnp.int32)
        which = pick_row(which_at, z)
        ids = chosen[:, k, :].reshape(-1)
        if k == 0:
            lots = [(0, [[local]])]
        elif k < planes - 1:
            lots = [(0, [[arrived[h][kind] for h in range(HALVES)] for kind in kinds])]
        else:
            lots = [(h * tall, [[arrived[h][kind]] for kind in kinds]) for h in range(HALVES)]
        for top, sources_k in lots:
            picked = choose(which, ids, sources_k)
            froms.append(
                lax.all_to_all(
                    picked, "rows", split_axis=0, concat_axis=0, axis_index_groups=groups, tiled=True
                )
            )
            starts.append((blocks_here + k * plane * capacity, top))

    return layer(
        slots,
        froms,
        tuple(starts),
        blocks_here + peers * capacity,
        tile_masks,
        degree.reshape(blocks_here, tile),
        weight,
    )


def solution(mesh):
    in_specs = (P("rows", None), P("rows", None), P("rows", None, None, None), P("rows"), P())
    out_specs = P("rows", None)
    return jax.shard_map(
        on_device, mesh=mesh, in_specs=in_specs, out_specs=out_specs, check_vma=False
    )
```

```python
import functools

import jax
import jax.numpy as jnp
from jax import lax
from jax.experimental import pallas as pl
from jax.experimental.pallas import tpu as pltpu
from jax.sharding import PartitionSpec as P

REM_PB = 4
PLANES = 4
CHUNKS = 4
VMEM_LIMIT = 60 * 1024 * 1024


def choose_kernel(ids, blocks, out, held, in_sem, out_sem):
    count = out.shape[0]
    for n in range(count):
        pltpu.make_async_copy(blocks.at[ids[n]], held.at[n], in_sem).start()
    pltpu.make_async_copy(out, held, in_sem).wait()
    leaving = pltpu.make_async_copy(held, out, out_sem)
    leaving.start()
    leaving.wait()


def choose(ids, blocks):
    out = (ids.shape[0],) + blocks.shape[1:]
    moved = out[0] * out[1] * out[2] * 2
    return pl.pallas_call(
        choose_kernel,
        grid_spec=pltpu.PrefetchScalarGridSpec(
            num_scalar_prefetch=1,
            grid=(1,),
            in_specs=[pl.BlockSpec(memory_space=pltpu.HBM)],
            out_specs=pl.BlockSpec(memory_space=pltpu.HBM),
            scratch_shapes=[
                pltpu.VMEM(out, blocks.dtype),
                pltpu.SemaphoreType.DMA,
                pltpu.SemaphoreType.DMA,
            ],
        ),
        out_shape=jax.ShapeDtypeStruct(out, blocks.dtype),
        compiler_params=pltpu.CompilerParams(vmem_limit_bytes=VMEM_LIMIT),
        cost_estimate=pl.CostEstimate(flops=0, bytes_accessed=4 * moved, transcendentals=0),
        name="choose_blocks",
    )(ids, blocks)


def layer_kernel(slots, *refs, pieces, starts):
    froms = refs[:pieces]
    masks, degree, weight, out, table, means, sems = refs[pieces:]
    step = pl.program_id(0)
    rows, per_block = masks.shape[:2]
    tile, width = table.shape[1:]

    @pl.when(step == 0)
    def _():
        copies = [
            pltpu.make_async_copy(
                piece,
                table.at[pl.ds(at, piece.shape[0]), pl.ds(top, piece.shape[1])],
                sems.at[n],
            )
            for n, (piece, (at, top)) in enumerate(zip(froms, starts))
        ]
        for copy in copies:
            copy.start()
        for copy in copies:
            copy.wait()

    for r in range(rows):
        row = step * rows + r
        mask = jnp.concatenate(
            [masks[r, t].astype(jnp.float32).astype(jnp.bfloat16) for t in range(per_block)], axis=1
        )
        picked = jnp.concatenate(
            [table[slots[row * per_block + t]] for t in range(per_block)], axis=0
        )
        sums = jnp.dot(mask, picked, preferred_element_type=jnp.float32)
        count = jnp.broadcast_to(degree[pl.ds(row, 1), :].astype(jnp.float32), (tile, tile)).T
        count = jnp.concatenate([count] * (width // tile), axis=1)
        means[pl.ds(r * tile, tile), :] = (sums / count).astype(jnp.bfloat16)
    own = table[pl.ds(step * rows, rows)].reshape(rows * tile, width)
    hidden = jnp.dot(own, weight[:width], preferred_element_type=jnp.float32)
    hidden = hidden + jnp.dot(means[...], weight[width:], preferred_element_type=jnp.float32)
    hidden = jnp.maximum(hidden, 0.0)
    scale = lax.rsqrt(jnp.sum(hidden * hidden, axis=1, keepdims=True) + 1e-06)
    out[...] = (hidden * scale).astype(jnp.bfloat16)


def layer(slots, froms, starts, blocks_in_table, tile_masks, degree, weight):
    blocks_here, per_block, tile, _ = tile_masks.shape
    width = weight.shape[0] // 2
    out_width = weight.shape[1]
    rows = 4 if blocks_here % 4 == 0 else 1
    return pl.pallas_call(
        functools.partial(layer_kernel, pieces=len(froms), starts=starts),
        grid_spec=pltpu.PrefetchScalarGridSpec(
            num_scalar_prefetch=1,
            grid=(blocks_here // rows,),
            in_specs=[pl.BlockSpec(memory_space=pltpu.HBM)] * len(froms)
            + [
                pl.BlockSpec((rows, per_block, tile, tile), lambda r, s: (r, 0, 0, 0)),
                pl.BlockSpec((blocks_here, tile), lambda r, s: (0, 0)),
                pl.BlockSpec((2 * width, out_width), lambda r, s: (0, 0)),
            ],
            out_specs=pl.BlockSpec((rows * tile, out_width), lambda r, s: (r, 0)),
            scratch_shapes=[
                pltpu.VMEM((blocks_in_table, tile, width), jnp.bfloat16),
                pltpu.VMEM((rows * tile, width), jnp.bfloat16),
                pltpu.SemaphoreType.DMA((len(froms),)),
            ],
        ),
        out_shape=jax.ShapeDtypeStruct((blocks_here * tile, out_width), jnp.bfloat16),
        compiler_params=pltpu.CompilerParams(vmem_limit_bytes=VMEM_LIMIT),
        cost_estimate=pl.CostEstimate(
            flops=2 * blocks_here * tile * (per_block * tile + 2 * width) * width,
            bytes_accessed=blocks_here * per_block * tile * tile * 4 + blocks_in_table * tile * width * 2,
            transcendentals=blocks_here * tile,
        ),
        name="sage_layer",
    )(slots, *froms, tile_masks, degree, weight)


def on_device(features, tile_cols, tile_masks, degree, weight):
    blocks_here, per_block = tile_cols.shape
    tile = tile_masks.shape[2]
    width = features.shape[1]
    peers = lax.axis_size("rows")
    planes = PLANES if peers % PLANES == 0 else 1
    plane = peers // planes
    myself = lax.axis_index("rows")
    p = myself % plane
    capacity = max(2, (REM_PB * blocks_here + peers - 2) // (peers - 1))
    local = features.reshape(blocks_here, tile, width)
    groups = [[a * plane + q for q in range(plane)] for a in range(planes)]
    lines = [[a * plane + q for a in range(planes)] for q in range(plane)]

    tall = tile // CHUNKS
    spread = [
        lax.all_gather(
            local[:, c * tall : (c + 1) * tall], "rows", axis_index_groups=lines, tiled=True
        )
        for c in range(CHUNKS)
    ]

    columns = tile_cols.reshape(-1)
    asked = lax.all_to_all(
        jnp.broadcast_to(columns, (plane,) + columns.shape),
        "rows",
        split_axis=0,
        concat_axis=0,
        axis_index_groups=groups,
        tiled=True,
    )
    blocks = jnp.arange(blocks_here, dtype=jnp.int32)
    line = jnp.arange(planes, dtype=jnp.int32) * plane + p
    wanted = (line[:, None] * blocks_here + blocks[None, :]).reshape(-1)
    need = jnp.any(asked[:, :, None] == wanted[None, None, :], axis=1)
    need = need.reshape(plane, planes, blocks_here).astype(jnp.int32)
    below = blocks[:, None] > blocks[None, :]
    place = jnp.sum(jnp.where(below, need[:, :, None, :], 0), axis=3)
    seat = jnp.arange(capacity, dtype=jnp.int32)
    taken = (need[:, :, None, :] == 1) & (place[:, :, None, :] == seat[:, None])
    chosen = jnp.sum(jnp.where(taken, blocks, 0), axis=3)
    ids = (chosen + jnp.arange(planes, dtype=jnp.int32)[:, None] * blocks_here).reshape(-1)

    owners, within = columns // blocks_here, columns % blocks_here
    positions = jnp.arange(columns.shape[0], dtype=jnp.int32)
    same = columns[:, None] == columns[None, :]
    first = ~jnp.any(same & (positions[None, :] < positions[:, None]), axis=1)
    ahead = (owners[:, None] == owners[None, :]) & (columns[None, :] < columns[:, None])
    ranks = jnp.sum(ahead & first[None, :], axis=1, dtype=jnp.int32)
    place_of = (owners % plane) * planes + owners // plane
    slots = jnp.where(owners == myself, within, blocks_here + place_of * capacity + ranks)

    froms, starts = [local], [(0, 0)]
    for c in range(CHUNKS):
        froms.append(
            lax.all_to_all(
                choose(ids, spread[c]),
                "rows",
                split_axis=0,
                concat_axis=0,
                axis_index_groups=groups,
                tiled=True,
            )
        )
        starts.append((blocks_here, c * tall))

    return layer(
        slots,
        froms,
        tuple(starts),
        blocks_here + peers * capacity,
        tile_masks,
        degree.reshape(blocks_here, tile),
        weight,
    )


def solution(mesh):
    in_specs = (P("rows", None), P("rows", None), P("rows", None, None, None), P("rows"), P())
    out_specs = P("rows", None)
    return jax.shard_map(
        on_device, mesh=mesh, in_specs=in_specs, out_specs=out_specs, check_vma=False
    )
```

```python
import functools

import jax
import jax.numpy as jnp
from jax import lax
from jax.experimental import pallas as pl
from jax.experimental.pallas import tpu as pltpu
from jax.sharding import PartitionSpec as P

REM_PB = 4
PLANES = 4
CHUNKS = 1

VMEM_LIMIT = 60 * 1024 * 1024


def arrival_order(planes):
    order = []
    for z in range(planes):
        mine = [(0, 0)]
        for step in range(1, planes):
            if z + step < planes:
                mine.append((step, -1))
            if z - step >= 0:
                mine.append((step, 1))
        order.append(mine)
    return order


def pick_row(table, z):
    return jnp.sum(jnp.where(jnp.arange(table.shape[0])[:, None] == z, table, 0), axis=0)


def choose_kernel(which, ids, *refs, top):
    *froms, out, held, in_sem, out_sem = refs
    count, tall = out.shape[:2]
    for j, source in enumerate(froms):

        @pl.when(which[0] == j)
        def _():
            for n in range(count):
                block = source.at[ids[n], pl.ds(top, tall)]
                pltpu.make_async_copy(block, held.at[n], in_sem).start()

    pltpu.make_async_copy(out, held, in_sem).wait()
    leaving = pltpu.make_async_copy(held, out, out_sem)
    leaving.start()
    leaving.wait()


def choose(which, ids, froms, tall, top=0):
    out = (ids.shape[0], tall, froms[0].shape[2])
    moved = out[0] * out[1] * out[2] * 2
    return pl.pallas_call(
        functools.partial(choose_kernel, top=top),
        grid_spec=pltpu.PrefetchScalarGridSpec(
            num_scalar_prefetch=2,
            grid=(1,),
            in_specs=[pl.BlockSpec(memory_space=pltpu.HBM)] * len(froms),
            out_specs=pl.BlockSpec(memory_space=pltpu.HBM),
            scratch_shapes=[
                pltpu.VMEM(out, froms[0].dtype),
                pltpu.SemaphoreType.DMA,
                pltpu.SemaphoreType.DMA,
            ],
        ),
        out_shape=jax.ShapeDtypeStruct(out, froms[0].dtype),
        compiler_params=pltpu.CompilerParams(vmem_limit_bytes=VMEM_LIMIT),
        cost_estimate=pl.CostEstimate(flops=0, bytes_accessed=2 * moved, transcendentals=0),
        name="choose_blocks",
    )(which, ids, *froms)


def layer_kernel(slots, *refs, pieces, starts):
    froms = refs[:pieces]
    masks, degree, weight, out, table, means, sems = refs[pieces:]
    step = pl.program_id(0)
    rows, per_block = masks.shape[:2]
    tile, width = table.shape[1:]

    @pl.when(step == 0)
    def _():
        copies = [
            pltpu.make_async_copy(
                piece,
                table.at[pl.ds(at, piece.shape[0]), pl.ds(top, piece.shape[1])],
                sems.at[n],
            )
            for n, (piece, (at, top)) in enumerate(zip(froms, starts))
        ]
        for copy in copies:
            copy.start()
        for copy in copies:
            copy.wait()

    for r in range(rows):
        row = step * rows + r
        mask = jnp.concatenate(
            [masks[r, t].astype(jnp.float32).astype(jnp.bfloat16) for t in range(per_block)], axis=1
        )
        picked = jnp.concatenate(
            [table[slots[row * per_block + t]] for t in range(per_block)], axis=0
        )
        sums = jnp.dot(mask, picked, preferred_element_type=jnp.float32)
        count = jnp.broadcast_to(degree[pl.ds(row, 1), :].astype(jnp.float32), (tile, tile)).T
        count = jnp.concatenate([count] * (width // tile), axis=1)
        means[pl.ds(r * tile, tile), :] = (sums / count).astype(jnp.bfloat16)
    own = table[pl.ds(step * rows, rows)].reshape(rows * tile, width)
    hidden = jnp.dot(own, weight[:width], preferred_element_type=jnp.float32)
    hidden = hidden + jnp.dot(means[...], weight[width:], preferred_element_type=jnp.float32)
    hidden = jnp.maximum(hidden, 0.0)
    scale = lax.rsqrt(jnp.sum(hidden * hidden, axis=1, keepdims=True) + 1e-06)
    out[...] = (hidden * scale).astype(jnp.bfloat16)


def layer(slots, froms, starts, blocks_in_table, tile_masks, degree, weight):
    blocks_here, per_block, tile, _ = tile_masks.shape
    width = weight.shape[0] // 2
    out_width = weight.shape[1]
    rows = 4 if blocks_here % 4 == 0 else 1
    return pl.pallas_call(
        functools.partial(layer_kernel, pieces=len(froms), starts=starts),
        grid_spec=pltpu.PrefetchScalarGridSpec(
            num_scalar_prefetch=1,
            grid=(blocks_here // rows,),
            in_specs=[pl.BlockSpec(memory_space=pltpu.HBM)] * len(froms)
            + [
                pl.BlockSpec((rows, per_block, tile, tile), lambda r, s: (r, 0, 0, 0)),
                pl.BlockSpec((blocks_here, tile), lambda r, s: (0, 0)),
                pl.BlockSpec((2 * width, out_width), lambda r, s: (0, 0)),
            ],
            out_specs=pl.BlockSpec((rows * tile, out_width), lambda r, s: (r, 0)),
            scratch_shapes=[
                pltpu.VMEM((blocks_in_table, tile, width), jnp.bfloat16),
                pltpu.VMEM((rows * tile, width), jnp.bfloat16),
                pltpu.SemaphoreType.DMA((len(froms),)),
            ],
        ),
        out_shape=jax.ShapeDtypeStruct((blocks_here * tile, out_width), jnp.bfloat16),
        compiler_params=pltpu.CompilerParams(vmem_limit_bytes=VMEM_LIMIT),
        cost_estimate=pl.CostEstimate(
            flops=2 * blocks_here * tile * (per_block * tile + 2 * width) * width,
            bytes_accessed=blocks_here * per_block * tile * tile * 4 + blocks_in_table * tile * width * 2,
            transcendentals=blocks_here * tile,
        ),
        name="sage_layer",
    )(slots, *froms, tile_masks, degree, weight)


def on_device(features, tile_cols, tile_masks, degree, weight):
    blocks_here, per_block = tile_cols.shape
    tile = tile_masks.shape[2]
    width = features.shape[1]
    peers = lax.axis_size("rows")
    planes = PLANES if peers % PLANES == 0 else 1
    plane = peers // planes
    myself = lax.axis_index("rows")
    z, p = myself // plane, myself % plane
    capacity = max(2, (REM_PB * blocks_here + peers - 2) // (peers - 1))
    local = features.reshape(blocks_here, tile, width)
    groups = [[a * plane + q for q in range(plane)] for a in range(planes)]
    order = arrival_order(planes)

    tall = tile // CHUNKS
    arrived = [{} for _ in range(CHUNKS)]
    for step in range(1, planes):
        for c in range(CHUNKS):
            for way in (-1, 1):
                pairs = [
                    (a * plane + q, (a + way) * plane + q)
                    for a in range(planes)
                    if 0 <= a + way < planes and 0 <= a - way * (step - 1) < planes
                    for q in range(plane)
                ]
                held = local[:, c * tall : (c + 1) * tall] if step == 1 else arrived[c][step - 1, way]
                arrived[c][step, way] = lax.ppermute(held, "rows", pairs)

    columns = tile_cols.reshape(-1)
    asked = lax.all_to_all(
        jnp.broadcast_to(columns, (plane,) + columns.shape),
        "rows",
        split_axis=0,
        concat_axis=0,
        axis_index_groups=groups,
        tiled=True,
    )
    blocks = jnp.arange(blocks_here, dtype=jnp.int32)
    plane_at = jnp.array(
        [[a - way * step for step, way in order[a]] for a in range(planes)], jnp.int32
    )
    line = pick_row(plane_at, z) * plane + p
    wanted = (line[:, None] * blocks_here + blocks[None, :]).reshape(-1)
    need = jnp.any(asked[:, :, None] == wanted[None, None, :], axis=1)
    need = need.reshape(plane, planes, blocks_here).astype(jnp.int32)
    below = blocks[:, None] > blocks[None, :]
    place = jnp.sum(jnp.where(below, need[:, :, None, :], 0), axis=3)
    seat = jnp.arange(capacity, dtype=jnp.int32)
    taken = (need[:, :, None, :] == 1) & (place[:, :, None, :] == seat[:, None])
    chosen = jnp.sum(jnp.where(taken, blocks, 0), axis=3)

    owners, within = columns // blocks_here, columns % blocks_here
    positions = jnp.arange(columns.shape[0], dtype=jnp.int32)
    same = columns[:, None] == columns[None, :]
    first = ~jnp.any(same & (positions[None, :] < positions[:, None]), axis=1)
    ahead = (owners[:, None] == owners[None, :]) & (columns[None, :] < columns[:, None])
    ranks = jnp.sum(ahead & first[None, :], axis=1, dtype=jnp.int32)
    stage_at = jnp.array(
        [
            [[a - way * step for step, way in order[a]].index(b) for b in range(planes)]
            for a in range(planes)
        ],
        jnp.int32,
    )
    stages = pick_row(stage_at, z)
    their_plane = owners // plane
    stage = jnp.sum(
        jnp.where(their_plane[:, None] == jnp.arange(planes), stages[None, :], 0), axis=1
    )
    place_of = (stage * plane + owners % plane) * capacity
    slots = jnp.where(owners == myself, within, blocks_here + place_of + ranks)

    froms, starts = [local], [(0, 0)]
    for k in range(planes):
        kinds = sorted(set(order[a][k] for a in range(planes)))
        which_at = jnp.array([[kinds.index(order[a][k])] for a in range(planes)], jnp.int32)
        which = pick_row(which_at, z)
        for c in range(CHUNKS):
            ids = chosen[:, k, :].reshape(-1)
            if k == 0:
                picked = choose(which, ids, [local], tall, c * tall)
            else:
                picked = choose(which, ids, [arrived[c][kind] for kind in kinds], tall)
            used = jnp.any(taken[:, k], axis=2).reshape(-1)
            picked = jnp.where(used[:, None, None], picked, 0)
            received = lax.all_to_all(
                picked, "rows", split_axis=0, concat_axis=0, axis_index_groups=groups, tiled=True
            )
            froms.append(received)
            starts.append((blocks_here + k * plane * capacity, c * tall))

    return layer(
        slots,
        froms,
        tuple(starts),
        blocks_here + peers * capacity,
        tile_masks,
        degree.reshape(blocks_here, tile),
        weight,
    )


def solution(mesh):
    in_specs = (P("rows", None), P("rows", None), P("rows", None, None, None), P("rows"), P())
    out_specs = P("rows", None)
    return jax.shard_map(
        on_device, mesh=mesh, in_specs=in_specs, out_specs=out_specs, check_vma=False
    )
```

```python
import functools

import jax
import jax.numpy as jnp
from jax import lax
from jax.experimental import pallas as pl
from jax.experimental.pallas import tpu as pltpu
from jax.sharding import PartitionSpec as P

REM_PB = 4
PLANES = 4
LAST = 1

VMEM_LIMIT = 60 * 1024 * 1024


def arrival_order(planes):
    order = []
    for z in range(planes):
        mine = [(0, 0)]
        for step in range(1, planes):
            if z + step < planes:
                mine.append((step, -1))
            if z - step >= 0:
                mine.append((step, 1))
        order.append(mine)
    return order


def pick_row(table, z):
    return jnp.sum(jnp.where(jnp.arange(table.shape[0])[:, None] == z, table, 0), axis=0)


def choose_kernel(ids, *refs):
    *froms, out, held, in_sem, out_sem = refs
    count = out.shape[0]
    tall = froms[0].shape[1]
    for n in range(count):
        for h, source in enumerate(froms):
            pltpu.make_async_copy(source.at[ids[n]], held.at[n, pl.ds(h * tall, tall)], in_sem).start()
    pltpu.make_async_copy(out, held, in_sem).wait()
    leaving = pltpu.make_async_copy(held, out, out_sem)
    leaving.start()
    leaving.wait()


def choose(ids, froms):
    out = (ids.shape[0], len(froms) * froms[0].shape[1], froms[0].shape[2])
    moved = out[0] * out[1] * out[2] * 2
    return pl.pallas_call(
        choose_kernel,
        grid_spec=pltpu.PrefetchScalarGridSpec(
            num_scalar_prefetch=1,
            grid=(1,),
            in_specs=[pl.BlockSpec(memory_space=pltpu.HBM)] * len(froms),
            out_specs=pl.BlockSpec(memory_space=pltpu.HBM),
            scratch_shapes=[
                pltpu.VMEM(out, froms[0].dtype),
                pltpu.SemaphoreType.DMA,
                pltpu.SemaphoreType.DMA,
            ],
        ),
        out_shape=jax.ShapeDtypeStruct(out, froms[0].dtype),
        compiler_params=pltpu.CompilerParams(vmem_limit_bytes=VMEM_LIMIT),
        cost_estimate=pl.CostEstimate(flops=0, bytes_accessed=2 * moved, transcendentals=0),
        name="choose_blocks",
    )(ids, *froms)


def early_kernel(slots, late, counts, *refs, pieces, starts):
    froms = refs[:pieces]
    masks, sums, left, table, sems = refs[pieces:]
    step = pl.program_id(0)
    rows, per_block = masks.shape[:2]
    tile, width = table.shape[1:]
    spare = left.shape[2] // tile

    @pl.when(step == 0)
    def _():
        copies = [
            pltpu.make_async_copy(piece, table.at[pl.ds(at, piece.shape[0])], sems.at[n])
            for n, (piece, at) in enumerate(zip(froms, starts))
        ]
        for copy in copies:
            copy.start()
        table[table.shape[0] - 1] = jnp.zeros((tile, width), table.dtype)
        for copy in copies:
            copy.wait()

    for r in range(rows):
        row = step * rows + r
        mask = jnp.concatenate(
            [masks[r, t].astype(jnp.float32).astype(jnp.bfloat16) for t in range(per_block)], axis=1
        )
        picked = jnp.concatenate(
            [table[slots[row * per_block + t]] for t in range(per_block)], axis=0
        )
        sums[pl.ds(r * tile, tile), :] = jnp.dot(mask, picked, preferred_element_type=jnp.float32)
        for t in range(spare):
            kept = masks[r, late[row * spare + t]].astype(jnp.float32)
            kept = jnp.where(t < counts[row], kept, 0.0).astype(jnp.bfloat16)
            left[r, :, t * tile : (t + 1) * tile] = kept


def early(slots, late, counts, froms, starts, blocks_in_table, tile_masks, width):
    blocks_here, per_block, tile, _ = tile_masks.shape
    spare = late.shape[0] // blocks_here
    rows = 4 if blocks_here % 4 == 0 else 1
    return pl.pallas_call(
        functools.partial(early_kernel, pieces=len(froms), starts=starts),
        grid_spec=pltpu.PrefetchScalarGridSpec(
            num_scalar_prefetch=3,
            grid=(blocks_here // rows,),
            in_specs=[pl.BlockSpec(memory_space=pltpu.HBM)] * len(froms)
            + [pl.BlockSpec((rows, per_block, tile, tile), lambda r, *_: (r, 0, 0, 0))],
            out_specs=[
                pl.BlockSpec((rows * tile, width), lambda r, *_: (r, 0)),
                pl.BlockSpec((rows, tile, spare * tile), lambda r, *_: (r, 0, 0)),
            ],
            scratch_shapes=[
                pltpu.VMEM((blocks_in_table, tile, width), jnp.bfloat16),
                pltpu.SemaphoreType.DMA((len(froms),)),
            ],
        ),
        out_shape=[
            jax.ShapeDtypeStruct((blocks_here * tile, width), jnp.float32),
            jax.ShapeDtypeStruct((blocks_here, tile, spare * tile), jnp.bfloat16),
        ],
        compiler_params=pltpu.CompilerParams(vmem_limit_bytes=VMEM_LIMIT),
        cost_estimate=pl.CostEstimate(
            flops=2 * blocks_here * tile * per_block * tile * width,
            bytes_accessed=blocks_here * per_block * tile * tile * 6 + blocks_in_table * tile * width * 2,
            transcendentals=0,
        ),
        name="early_sums",
    )(slots, late, counts, *froms, tile_masks)


def layer_kernel(slots, counts, *refs, pieces, starts):
    froms = refs[:pieces]
    sums, left, features, degree, weight, out, table, totals, means, sems = refs[pieces:]
    step = pl.program_id(0)
    rows, tile = left.shape[:2]
    width = table.shape[2]
    spare = left.shape[2] // tile

    @pl.when(step == 0)
    def _():
        copies = [
            pltpu.make_async_copy(piece, table.at[:, pl.ds(top, piece.shape[1])], sems.at[n])
            for n, (piece, top) in enumerate(zip(froms, starts))
        ]
        for copy in copies:
            copy.start()
        for copy in copies:
            copy.wait()

    for r in range(rows):
        row = step * rows + r
        here = pl.ds(r * tile, tile)

        def add(base, first, count):
            picked = jnp.concatenate(
                [table[slots[row * spare + t]] for t in range(first, first + count)], axis=0
            )
            mask = left[r, :, first * tile : (first + count) * tile]
            totals[here, :] = base[here, :] + jnp.dot(mask, picked, preferred_element_type=jnp.float32)

        pair = min(2, spare)
        add(sums, 0, pair)
        for first in range(pair, spare, pair):
            pl.when(counts[row] > first)(functools.partial(add, totals, first, min(pair, spare - first)))
        count = jnp.broadcast_to(degree[pl.ds(row, 1), :].astype(jnp.float32), (tile, tile)).T
        count = jnp.concatenate([count] * (width // tile), axis=1)
        means[here, :] = (totals[here, :] / count).astype(jnp.bfloat16)
    hidden = jnp.dot(features[...], weight[:width], preferred_element_type=jnp.float32)
    hidden = hidden + jnp.dot(means[...], weight[width:], preferred_element_type=jnp.float32)
    hidden = jnp.maximum(hidden, 0.0)
    scale = lax.rsqrt(jnp.sum(hidden * hidden, axis=1, keepdims=True) + 1e-06)
    out[...] = (hidden * scale).astype(jnp.bfloat16)


def layer(slots, counts, froms, starts, sums, left, features, degree, weight):
    blocks_here, tile, across = left.shape
    width = features.shape[1]
    out_width = weight.shape[1]
    rows = 4 if blocks_here % 4 == 0 else 1
    items = (rows * tile, width)
    return pl.pallas_call(
        functools.partial(layer_kernel, pieces=len(froms), starts=starts),
        grid_spec=pltpu.PrefetchScalarGridSpec(
            num_scalar_prefetch=2,
            grid=(blocks_here // rows,),
            in_specs=[pl.BlockSpec(memory_space=pltpu.HBM)] * len(froms)
            + [
                pl.BlockSpec(items, lambda r, *_: (r, 0)),
                pl.BlockSpec((rows, tile, across), lambda r, *_: (r, 0, 0)),
                pl.BlockSpec(items, lambda r, *_: (r, 0)),
                pl.BlockSpec((blocks_here, tile), lambda r, *_: (0, 0)),
                pl.BlockSpec((2 * width, out_width), lambda r, *_: (0, 0)),
            ],
            out_specs=pl.BlockSpec((rows * tile, out_width), lambda r, *_: (r, 0)),
            scratch_shapes=[
                pltpu.VMEM((froms[0].shape[0], tile, width), jnp.bfloat16),
                pltpu.VMEM(items, jnp.float32),
                pltpu.VMEM(items, jnp.bfloat16),
                pltpu.SemaphoreType.DMA((len(froms),)),
            ],
        ),
        out_shape=jax.ShapeDtypeStruct((blocks_here * tile, out_width), jnp.bfloat16),
        compiler_params=pltpu.CompilerParams(vmem_limit_bytes=VMEM_LIMIT),
        cost_estimate=pl.CostEstimate(
            flops=2 * blocks_here * tile * (across + 2 * width) * out_width,
            bytes_accessed=blocks_here * tile * (4 * width + 2 * across + 2 * width + 2 * out_width),
            transcendentals=blocks_here * tile,
        ),
        name="sage_layer",
    )(slots, counts, *froms, sums, left, features, degree, weight)


def on_device(features, tile_cols, tile_masks, degree, weight):
    blocks_here, per_block = tile_cols.shape
    tile = tile_masks.shape[2]
    width = features.shape[1]
    peers = lax.axis_size("rows")
    planes = PLANES if peers % PLANES == 0 else 1
    plane = peers // planes
    myself = lax.axis_index("rows")
    z, p = myself // plane, myself % plane
    capacity = max(2, (REM_PB * blocks_here + peers - 2) // (peers - 1))
    local = features.reshape(blocks_here, tile, width)
    groups = [[a * plane + q for q in range(plane)] for a in range(planes)]
    order = arrival_order(planes)

    columns = tile_cols.reshape(-1)
    asked = lax.all_to_all(
        jnp.broadcast_to(columns, (plane,) + columns.shape),
        "rows",
        split_axis=0,
        concat_axis=0,
        axis_index_groups=groups,
        tiled=True,
    )
    blocks = jnp.arange(blocks_here, dtype=jnp.int32)
    plane_at = jnp.array(
        [[a - way * step for step, way in order[a]] for a in range(planes)], jnp.int32
    )
    line = pick_row(plane_at, z) * plane + p
    wanted = (line[:, None] * blocks_here + blocks[None, :]).reshape(-1)
    need = jnp.any(asked[:, :, None] == wanted[None, None, :], axis=1)
    need = need.reshape(plane, planes, blocks_here).astype(jnp.int32)
    below = blocks[:, None] > blocks[None, :]
    place = jnp.sum(jnp.where(below, need[:, :, None, :], 0), axis=3)
    seat = jnp.arange(capacity, dtype=jnp.int32)
    taken = (need[:, :, None, :] == 1) & (place[:, :, None, :] == seat[:, None])
    chosen = jnp.sum(jnp.where(taken, blocks, 0), axis=3)

    owners, within = columns // blocks_here, columns % blocks_here
    positions = jnp.arange(columns.shape[0], dtype=jnp.int32)
    same = columns[:, None] == columns[None, :]
    first = ~jnp.any(same & (positions[None, :] < positions[:, None]), axis=1)
    ahead = (owners[:, None] == owners[None, :]) & (columns[None, :] < columns[:, None])
    ranks = jnp.sum(ahead & first[None, :], axis=1, dtype=jnp.int32)
    stage_at = jnp.array(
        [
            [[a - way * step for step, way in order[a]].index(b) for b in range(planes)]
            for a in range(planes)
        ],
        jnp.int32,
    )
    stages = pick_row(stage_at, z)
    their_plane = owners // plane
    stage = jnp.sum(
        jnp.where(their_plane[:, None] == jnp.arange(planes), stages[None, :], 0), axis=1
    )
    seats = (owners % plane) * capacity + ranks
    here = planes - 1 if planes > 1 else 1
    nothing = blocks_here + here * plane * capacity
    slots = blocks_here + stage * plane * capacity + seats
    slots = jnp.where(owners == myself, within, jnp.where(stage < here, slots, nothing))

    last = ((stage >= here) & (owners != myself)).reshape(blocks_here, per_block)
    counts = jnp.sum(last, axis=1, dtype=jnp.int32)
    order_in = jnp.cumsum(last, axis=1) - 1
    spots = jnp.arange(REM_PB, dtype=jnp.int32)
    chair = last[:, None, :] & (order_in[:, None, :] == spots[:, None])
    late = jnp.sum(jnp.where(chair, jnp.arange(per_block, dtype=jnp.int32), 0), axis=2, dtype=jnp.int32)
    late_slots = jnp.sum(
        jnp.where(chair, seats.reshape(blocks_here, 1, per_block), 0), axis=2, dtype=jnp.int32
    )

    arrived = {(0, -1): local, (0, 1): local}
    froms, starts, sums = [local], [0], None
    picked = received = None
    for k in range(planes):
        finish = k == planes - 1 and k > 0
        kinds = sorted(set(order[a][k] for a in range(planes)))
        which_at = jnp.array([[kinds.index(order[a][k])] for a in range(planes)], jnp.int32)
        which = pick_row(which_at, z)[0]
        if k > 0:
            pairs = {
                way: [
                    (a * plane + q, (a + way) * plane + q)
                    for a in range(planes)
                    if 0 <= a + way < planes and 0 <= a - way * (k - 1) < planes
                    for q in range(plane)
                ]
                for way in (-1, 1)
            }
        if finish:
            through = jnp.where(z < planes // 2, arrived[k - 1, -1], arrived[k - 1, 1])
            tall = tile // LAST
            cut = [through[:, c * tall : (c + 1) * tall] for c in range(LAST)]
            ended = [lax.ppermute(part, "rows", pairs[-1] + pairs[1]) for part in cut]
            outer = (z == 0) | (z == planes - 1)
            lots = []
            for c in range(LAST):
                end, _ = lax.optimization_barrier((ended[c], picked))
                lots.append([jnp.where(outer, end, cut[c])])
        elif k > 0:
            for way in (-1, 1):
                arrived[k, way] = lax.ppermute(arrived[k - 1, way], "rows", pairs[way])
            arrived[k, -1], arrived[k, 1], _ = lax.optimization_barrier(
                (arrived[k, -1], arrived[k, 1], picked)
            )
            source = arrived[kinds[0]]
            for j, kind in enumerate(kinds):
                if j > 0:
                    source = jnp.where(which == j, arrived[kind], source)
            lots = [[source]]
        else:
            lots = [[local]]
        ids = chosen[:, k, :].reshape(-1)
        parts = []
        for sources in lots:
            if received is not None:
                ids, _ = lax.optimization_barrier((ids, received))
            picked = choose(ids, sources)
            received = lax.all_to_all(
                picked, "rows", split_axis=0, concat_axis=0, axis_index_groups=groups, tiled=True
            )
            parts.append(received)
        if k < here:
            froms += parts
            starts.append(blocks_here + k * plane * capacity)

    sums, left = early(
        slots, late.reshape(-1), counts, froms, tuple(starts), nothing + 1, tile_masks, width
    )
    tops = tuple(c * (tile // len(parts)) for c in range(len(parts)))
    return layer(
        late_slots.reshape(-1),
        counts,
        parts,
        tops,
        sums,
        left,
        features,
        degree.reshape(blocks_here, tile),
        weight,
    )


def solution(mesh):
    in_specs = (P("rows", None), P("rows", None), P("rows", None, None, None), P("rows"), P())
    out_specs = P("rows", None)
    return jax.shard_map(
        on_device, mesh=mesh, in_specs=in_specs, out_specs=out_specs, check_vma=False
    )
```

```python
import functools

import jax
import jax.numpy as jnp
from jax import lax
from jax.experimental import pallas as pl
from jax.experimental.pallas import tpu as pltpu
from jax.sharding import PartitionSpec as P

REM_PB = 4
PLANES = 4
CHOOSE_FLOPS = 10**10
EARLY_FLOPS = 2 * 10**10

VMEM_LIMIT = 60 * 1024 * 1024


def pick_row(table, z):
    return jnp.sum(jnp.where(jnp.arange(table.shape[0])[:, None] == z, table, 0), axis=0)


def choose_kernel(which, ids, *refs):
    *froms, out, held, in_sem, out_sem = refs
    count = out.shape[0]
    for j, source in enumerate(froms):

        @pl.when(which[0] == j)
        def _():
            for n in range(count):
                pltpu.make_async_copy(source.at[ids[n]], held.at[n], in_sem).start()

    pltpu.make_async_copy(out, held, in_sem).wait()
    leaving = pltpu.make_async_copy(held, out, out_sem)
    leaving.start()
    leaving.wait()


def choose(which, ids, froms):
    out = (ids.shape[0],) + froms[0].shape[1:]
    moved = out[0] * out[1] * out[2] * 2
    return pl.pallas_call(
        choose_kernel,
        grid_spec=pltpu.PrefetchScalarGridSpec(
            num_scalar_prefetch=2,
            grid=(1,),
            in_specs=[pl.BlockSpec(memory_space=pltpu.HBM)] * len(froms),
            out_specs=pl.BlockSpec(memory_space=pltpu.HBM),
            scratch_shapes=[
                pltpu.VMEM(out, froms[0].dtype),
                pltpu.SemaphoreType.DMA,
                pltpu.SemaphoreType.DMA,
            ],
        ),
        out_shape=jax.ShapeDtypeStruct(out, froms[0].dtype),
        compiler_params=pltpu.CompilerParams(vmem_limit_bytes=VMEM_LIMIT),
        cost_estimate=pl.CostEstimate(flops=CHOOSE_FLOPS, bytes_accessed=2 * moved, transcendentals=0),
        name="choose_blocks",
    )(which, ids, *froms)


def fill(pieces, table, sems):
    copies, at = [], 0
    for n, piece in enumerate(pieces):
        here = table.at[pl.ds(at, piece.shape[0])]
        copies.append(pltpu.make_async_copy(piece, here, sems.at[n]))
        at += piece.shape[0]
    for copy in copies:
        copy.start()
    for copy in copies:
        copy.wait()


def early_kernel(slots, late, counts, *refs):
    *froms, masks, degree, sums, left, share, table, sems = refs
    step = pl.program_id(0)
    rows, per_block = masks.shape[:2]
    tile, width = table.shape[1:]
    spare = left.shape[2] // tile

    @pl.when(step == 0)
    def _():
        table[table.shape[0] - 1] = jnp.zeros((tile, width), table.dtype)
        fill(froms, table, sems)

    for r in range(rows):
        row = step * rows + r
        here = pl.ds(r * tile, tile)
        mask = jnp.concatenate(
            [masks[r, t].astype(jnp.float32).astype(jnp.bfloat16) for t in range(per_block)], axis=1
        )
        picked = jnp.concatenate(
            [table[slots[row * per_block + t]] for t in range(per_block)], axis=0
        )
        sums[here, :] = jnp.dot(mask, picked, preferred_element_type=jnp.float32)
        for t in range(spare):
            kept = masks[r, late[row * spare + t]].astype(jnp.float32)
            kept = jnp.where(t < counts[row], kept, 0.0).astype(jnp.bfloat16)
            left[r, :, t * tile : (t + 1) * tile] = kept
        count = degree[pl.ds(row, 1), :].astype(jnp.float32)
        share[here, :] = 1.0 / jnp.broadcast_to(count, (tile, tile)).T


def early(slots, late, counts, froms, tile_masks, degree):
    blocks_here, per_block, tile, _ = tile_masks.shape
    width = froms[0].shape[2]
    spare = late.shape[0] // blocks_here
    rows = 4 if blocks_here % 4 == 0 else 1
    blocks_in_table = sum(piece.shape[0] for piece in froms) + 1
    return pl.pallas_call(
        early_kernel,
        grid_spec=pltpu.PrefetchScalarGridSpec(
            num_scalar_prefetch=3,
            grid=(blocks_here // rows,),
            in_specs=[pl.BlockSpec(memory_space=pl.ANY)] * len(froms)
            + [
                pl.BlockSpec((rows, per_block, tile, tile), lambda r, *_: (r, 0, 0, 0)),
                pl.BlockSpec((blocks_here, tile), lambda r, *_: (0, 0)),
            ],
            out_specs=[
                pl.BlockSpec((rows * tile, width), lambda r, *_: (r, 0)),
                pl.BlockSpec((rows, tile, spare * tile), lambda r, *_: (r, 0, 0)),
                pl.BlockSpec((rows * tile, tile), lambda r, *_: (r, 0)),
            ],
            scratch_shapes=[
                pltpu.VMEM((blocks_in_table, tile, width), jnp.bfloat16),
                pltpu.SemaphoreType.DMA((len(froms),)),
            ],
        ),
        out_shape=[
            jax.ShapeDtypeStruct((blocks_here * tile, width), jnp.float32),
            jax.ShapeDtypeStruct((blocks_here, tile, spare * tile), jnp.bfloat16),
            jax.ShapeDtypeStruct((blocks_here * tile, tile), jnp.float32),
        ],
        compiler_params=pltpu.CompilerParams(vmem_limit_bytes=VMEM_LIMIT),
        cost_estimate=pl.CostEstimate(
            flops=EARLY_FLOPS,
            bytes_accessed=blocks_here * per_block * tile * tile * 6 + blocks_in_table * tile * width * 2,
            transcendentals=0,
        ),
        name="early_sums",
    )(slots, late, counts, *froms, tile_masks, degree)


def layer_kernel(slots, counts, *refs):
    *froms, sums, left, share, features, weight, out, table, totals, sems = refs
    step = pl.program_id(0)
    rows, tile = left.shape[:2]
    width = table.shape[2]
    spare = left.shape[2] // tile
    pair = min(2, spare)
    pl.when(step == 0)(functools.partial(fill, froms, table, sems))

    def added(r, first):
        ends = min(first + pair, spare)
        picked = [table[slots[(step * rows + r) * spare + t]] for t in range(first, ends)]
        mask = left[r, :, first * tile : ends * tile]
        return jnp.dot(mask, jnp.concatenate(picked, axis=0), preferred_element_type=jnp.float32)

    for r in range(rows):
        here = pl.ds(r * tile, tile)
        totals[here, :] = sums[here, :] + added(r, 0)
    for r in range(rows):
        here = pl.ds(r * tile, tile)
        for first in range(pair, spare, pair):

            @pl.when(counts[step * rows + r] > first)
            def _():
                totals[here, :] += added(r, first)

    for r in range(rows):
        here = pl.ds(r * tile, tile)
        part = jnp.concatenate([share[here, :]] * (width // tile), axis=1)
        mean = (totals[here, :] * part).astype(jnp.bfloat16)
        joined = jnp.concatenate([features[here, :], mean], axis=1)
        hidden = jnp.dot(joined, weight[...], preferred_element_type=jnp.float32)
        hidden = jnp.maximum(hidden, 0.0)
        scale = lax.rsqrt(jnp.sum(hidden * hidden, axis=1, keepdims=True) + 1e-06)
        out[here, :] = (hidden * scale).astype(jnp.bfloat16)


def layer(slots, counts, froms, sums, left, share, features, weight):
    blocks_here, tile, across = left.shape
    width = features.shape[1]
    out_width = weight.shape[1]
    rows = 4 if blocks_here % 4 == 0 else 1
    items = rows * tile
    blocks_in_table = sum(piece.shape[0] for piece in froms)
    return pl.pallas_call(
        layer_kernel,
        grid_spec=pltpu.PrefetchScalarGridSpec(
            num_scalar_prefetch=2,
            grid=(blocks_here // rows,),
            in_specs=[pl.BlockSpec(memory_space=pl.ANY)] * len(froms)
            + [
                pl.BlockSpec((items, width), lambda r, *_: (r, 0)),
                pl.BlockSpec((rows, tile, across), lambda r, *_: (r, 0, 0)),
                pl.BlockSpec((items, tile), lambda r, *_: (r, 0)),
                pl.BlockSpec((items, width), lambda r, *_: (r, 0)),
                pl.BlockSpec((2 * width, out_width), lambda r, *_: (0, 0)),
            ],
            out_specs=pl.BlockSpec((items, out_width), lambda r, *_: (r, 0)),
            scratch_shapes=[
                pltpu.VMEM((blocks_in_table, tile, width), jnp.bfloat16),
                pltpu.VMEM((items, width), jnp.float32),
                pltpu.SemaphoreType.DMA((len(froms),)),
            ],
        ),
        out_shape=jax.ShapeDtypeStruct((blocks_here * tile, out_width), jnp.bfloat16),
        compiler_params=pltpu.CompilerParams(vmem_limit_bytes=VMEM_LIMIT),
        cost_estimate=pl.CostEstimate(
            flops=2 * blocks_here * tile * (across + 2 * width) * out_width,
            bytes_accessed=blocks_here * tile * (4 * width + 2 * across + 2 * width + 2 * out_width),
            transcendentals=blocks_here * tile,
        ),
        name="sage_layer",
    )(slots, counts, *froms, sums, left, share, features, weight)


def on_device(features, tile_cols, tile_masks, degree, weight):
    blocks_here, per_block = tile_cols.shape
    tile = tile_masks.shape[2]
    width = features.shape[1]
    peers = lax.axis_size("rows")
    plane = peers // PLANES
    myself = lax.axis_index("rows")
    z, p = myself // plane, myself % plane
    end = (z == 0) | (z == PLANES - 1)
    capacity = max(2, (REM_PB * blocks_here + peers - 2) // (peers - 1))
    seats_all = plane * capacity
    local = features.reshape(blocks_here, tile, width)
    columns = tile_cols.reshape(-1)
    groups = [[a * plane + q for q in range(plane)] for a in range(PLANES)]

    def exchange(x):
        return lax.all_to_all(
            x, "rows", split_axis=0, concat_axis=0, axis_index_groups=groups, tiled=True
        )

    def shift(x, moves):
        pairs = [(a * plane + q, b * plane + q) for a, b in moves for q in range(plane)]
        return lax.ppermute(x, "rows", pairs)

    across = shift(columns, [(0, PLANES - 1), (PLANES - 1, 0)])
    both = jnp.stack([columns, across])
    asked = exchange(jnp.broadcast_to(both[None], (plane,) + both.shape))
    down = [(a, a - 1) for a in range(1, PLANES)]
    up = [(a - 1, a) for a in range(1, PLANES)]
    first, _ = lax.optimization_barrier((local, across))
    from_above, from_below = shift(first, down), shift(first, up)

    rounds = jnp.array([[0, 0, 1, 2], [1, 2, 0, 3], [2, 3, 1, 0], [3, 3, 2, 1]], jnp.int32)
    line = pick_row(rounds, z) * plane + p
    blocks = jnp.arange(blocks_here, dtype=jnp.int32)
    wanted = line[:, None] * blocks_here + blocks[None, :]
    far = end & (jnp.arange(PLANES) == 1)
    asking = jnp.where(far[None, :, None], asked[:, 1, None, :], asked[:, 0, None, :])
    need = jnp.any(asking[:, :, :, None] == wanted[None, :, None, :], axis=2).astype(jnp.int32)
    below = blocks[:, None] > blocks[None, :]
    place = jnp.sum(jnp.where(below, need[:, :, None, :], 0), axis=3)
    seat = jnp.arange(capacity, dtype=jnp.int32)
    taken = (need[:, :, None, :] == 1) & (place[:, :, None, :] == seat[:, None])
    chosen = jnp.sum(jnp.where(taken, blocks, 0), axis=3)
    ids = [chosen[:, k, :].reshape(-1) for k in range(PLANES)]

    owners, within = columns // blocks_here, columns % blocks_here
    positions = jnp.arange(columns.shape[0], dtype=jnp.int32)
    same = columns[:, None] == columns[None, :]
    repeated = jnp.any(same & (positions[None, :] < positions[:, None]), axis=1)
    ahead = (owners[:, None] == owners[None, :]) & (columns[None, :] < columns[:, None])
    ranks = jnp.sum(ahead & ~repeated[None, :], axis=1, dtype=jnp.int32)
    rounds_of = jnp.array([[0, 2, 3, 1], [2, 0, 1, 3], [3, 2, 0, 1], [1, 3, 2, 0]], jnp.int32)
    their_plane = owners // plane
    among = their_plane[:, None] == jnp.arange(PLANES)
    turn = jnp.sum(jnp.where(among, pick_row(rounds_of, z)[None, :], 0), axis=1)
    seats = (owners % plane) * capacity + ranks
    nothing = blocks_here + 3 * seats_all
    final = (turn == 3) | (end & (turn == 1))
    slots = jnp.where(final, nothing, blocks_here + turn * seats_all + seats)
    slots = jnp.where(owners == myself, within, slots)
    seats = jnp.where(turn == 3, seats + seats_all, seats)

    last = final.reshape(blocks_here, per_block)
    counts = jnp.sum(last, axis=1, dtype=jnp.int32)
    order_in = jnp.cumsum(last, axis=1) - 1
    spots = jnp.arange(REM_PB, dtype=jnp.int32)
    chair = last[:, None, :] & (order_in[:, None, :] == spots[:, None])
    late = jnp.sum(jnp.where(chair, jnp.arange(per_block, dtype=jnp.int32), 0), axis=2, dtype=jnp.int32)
    late_slots = jnp.sum(
        jnp.where(chair, seats.reshape(blocks_here, 1, per_block), 0), axis=2, dtype=jnp.int32
    )

    always = jnp.zeros((1,), jnp.int32)
    inner = (~end).astype(jnp.int32)[None]
    picked = choose(always, ids[0], [local])
    got = [exchange(picked)]
    ids[1], _, _ = lax.optimization_barrier((ids[1], picked, from_below))
    picked = choose(inner, ids[1], [local, from_above])
    got.append(exchange(picked))
    second_down = shift(from_above, down[:-1])
    second_up = shift(from_below, up[1:])
    crossed = shift(got[1], [(0, PLANES - 1), (PLANES - 1, 0)])
    ids[2], _ = lax.optimization_barrier((ids[2], picked))
    picked = choose((z > 0).astype(jnp.int32)[None], ids[2], [from_above, from_below])
    got.append(exchange(picked))
    beyond = (z >= PLANES // 2).astype(jnp.int32)[None]
    got.append(exchange(choose(beyond, ids[3], [second_down, second_up])))

    sums, left, share = early(
        slots, late.reshape(-1), counts, [local] + got[:3], tile_masks, degree.reshape(blocks_here, tile)
    )
    return layer(late_slots.reshape(-1), counts, [crossed, got[3]], sums, left, share, features, weight)


def solution(mesh):
    in_specs = (P("rows", None), P("rows", None), P("rows", None, None, None), P("rows"), P())
    out_specs = P("rows", None)
    return jax.shard_map(
        on_device, mesh=mesh, in_specs=in_specs, out_specs=out_specs, check_vma=False
    )
```

```python
import functools

import jax
import jax.numpy as jnp
from jax import lax
from jax.experimental import pallas as pl
from jax.experimental.pallas import tpu as pltpu
from jax.sharding import PartitionSpec as P

REM_PB = 4
PLANES = 4
HEAVY = 3 * 10**10
LIGHT = 10**10

VMEM_LIMIT = 62 * 1024 * 1024


def pick_row(table, z):
    return jnp.sum(jnp.where(jnp.arange(table.shape[0])[:, None] == z, table, 0), axis=0)


def choose_kernel(which, ids, *refs):
    *froms, out, held, in_sem, out_sem = refs
    count = out.shape[0]
    for j, source in enumerate(froms):

        @pl.when(which[0] == j)
        def _():
            for n in range(count):
                pltpu.make_async_copy(source.at[ids[n]], held.at[n], in_sem).start()

    pltpu.make_async_copy(out, held, in_sem).wait()
    leaving = pltpu.make_async_copy(held, out, out_sem)
    leaving.start()
    leaving.wait()


def choose(which, ids, froms, flops):
    out = (ids.shape[0],) + froms[0].shape[1:]
    moved = out[0] * out[1] * out[2] * 2
    return pl.pallas_call(
        choose_kernel,
        grid_spec=pltpu.PrefetchScalarGridSpec(
            num_scalar_prefetch=2,
            grid=(1,),
            in_specs=[pl.BlockSpec(memory_space=pltpu.HBM)] * len(froms),
            out_specs=pl.BlockSpec(memory_space=pltpu.HBM),
            scratch_shapes=[
                pltpu.VMEM(out, froms[0].dtype),
                pltpu.SemaphoreType.DMA,
                pltpu.SemaphoreType.DMA,
            ],
        ),
        out_shape=jax.ShapeDtypeStruct(out, froms[0].dtype),
        compiler_params=pltpu.CompilerParams(vmem_limit_bytes=VMEM_LIMIT),
        cost_estimate=pl.CostEstimate(flops=flops, bytes_accessed=2 * moved, transcendentals=0),
        name="choose_blocks",
    )(which, ids, *froms)


def either_kernel(second, a, b, out):
    out[...] = jnp.where(second[0] == 1, b[...], a[...])


def either(second, a, b):
    whole = pl.BlockSpec(a.shape, lambda i, s: (0, 0))
    return pl.pallas_call(
        either_kernel,
        grid_spec=pltpu.PrefetchScalarGridSpec(
            num_scalar_prefetch=1, grid=(1,), in_specs=[whole, whole], out_specs=whole
        ),
        out_shape=jax.ShapeDtypeStruct(a.shape, a.dtype),
        cost_estimate=pl.CostEstimate(flops=HEAVY, bytes_accessed=0, transcendentals=0),
        name="either_ids",
    )(second, a, b)


def fill(pieces, table, sems):
    copies, at = [], 0
    for n, piece in enumerate(pieces):
        here = table.at[pl.ds(at, piece.shape[0])]
        copies.append(pltpu.make_async_copy(piece, here, sems.at[n]))
        at += piece.shape[0]
    for copy in copies:
        copy.start()
    for copy in copies:
        copy.wait()


def early_kernel(slots, late, counts, *refs):
    *froms, masks, sums, left, table, sems = refs
    step = pl.program_id(0)
    rows, per_block = masks.shape[:2]
    tile, width = table.shape[1:]
    spare = left.shape[2] // tile

    @pl.when(step == 0)
    def _():
        table[table.shape[0] - 1] = jnp.zeros((tile, width), table.dtype)
        fill(froms, table, sems)

    for r in range(rows):
        row = step * rows + r
        here = pl.ds(r * tile, tile)
        mask = jnp.concatenate(
            [masks[r, t].astype(jnp.float32).astype(jnp.bfloat16) for t in range(per_block)], axis=1
        )
        picked = jnp.concatenate(
            [table[slots[row * per_block + t]] for t in range(per_block)], axis=0
        )
        sums[here, :] = jnp.dot(mask, picked, preferred_element_type=jnp.float32)
        for t in range(spare):
            kept = jnp.where(t < counts[row], masks[r, late[row * spare + t]], 0)
            left[r, :, t * tile : (t + 1) * tile] = kept.astype(jnp.int8)


def early(slots, late, counts, froms, tile_masks):
    blocks_here, per_block, tile, _ = tile_masks.shape
    width = froms[0].shape[2]
    spare = late.shape[0] // blocks_here
    rows = 4 if blocks_here % 4 == 0 else 1
    blocks_in_table = sum(piece.shape[0] for piece in froms) + 1
    return pl.pallas_call(
        early_kernel,
        grid_spec=pltpu.PrefetchScalarGridSpec(
            num_scalar_prefetch=3,
            grid=(blocks_here // rows,),
            in_specs=[pl.BlockSpec(memory_space=pl.ANY)] * len(froms)
            + [pl.BlockSpec((rows, per_block, tile, tile), lambda r, *_: (r, 0, 0, 0))],
            out_specs=[
                pl.BlockSpec((rows * tile, width), lambda r, *_: (r, 0)),
                pl.BlockSpec((rows, tile, spare * tile), lambda r, *_: (r, 0, 0)),
            ],
            scratch_shapes=[
                pltpu.VMEM((blocks_in_table, tile, width), jnp.bfloat16),
                pltpu.SemaphoreType.DMA((len(froms),)),
            ],
        ),
        out_shape=[
            jax.ShapeDtypeStruct((blocks_here * tile, width), jnp.float32),
            jax.ShapeDtypeStruct((blocks_here, tile, spare * tile), jnp.int8),
        ],
        compiler_params=pltpu.CompilerParams(vmem_limit_bytes=VMEM_LIMIT),
        cost_estimate=pl.CostEstimate(
            flops=2 * LIGHT,
            bytes_accessed=blocks_here * per_block * tile * tile * 6 + blocks_in_table * tile * width * 2,
            transcendentals=0,
        ),
        name="early_sums",
    )(slots, late, counts, *froms, tile_masks)


def layer_kernel(slots, counts, *refs):
    *froms, sums, left, degree, features, weight, out, table, totals, sems = refs
    step = pl.program_id(0)
    rows, tile = left.shape[:2]
    width = table.shape[2]
    spare = left.shape[2] // tile
    pair = min(2, spare)
    pl.when(step == 0)(functools.partial(fill, froms, table, sems))

    def added(r, first):
        ends = min(first + pair, spare)
        picked = [table[slots[(step * rows + r) * spare + t]] for t in range(first, ends)]
        mask = left[r, :, first * tile : ends * tile].astype(jnp.int32)
        mask = mask.astype(jnp.float32).astype(jnp.bfloat16)
        return jnp.dot(mask, jnp.concatenate(picked, axis=0), preferred_element_type=jnp.float32)

    for r in range(rows):
        here = pl.ds(r * tile, tile)
        totals[here, :] = sums[here, :] + added(r, 0)
    for r in range(rows):
        here = pl.ds(r * tile, tile)
        for first in range(pair, spare, pair):

            @pl.when(counts[step * rows + r] > first)
            def _():
                totals[here, :] += added(r, first)

    across = lax.broadcasted_iota(jnp.int32, (tile, tile), 1)
    diagonal = lax.broadcasted_iota(jnp.int32, (tile, tile), 0) == across
    ones = jnp.ones((2 * tile, tile), jnp.bfloat16)
    for r in range(rows):
        here = pl.ds(r * tile, tile)
        count = degree[pl.ds(step * rows + r, 1), :]
        small = count & 7
        halves = [
            jnp.where(diagonal, part.astype(jnp.float32), 0.0).astype(jnp.bfloat16)
            for part in (count - small, small)
        ]
        count = jnp.dot(jnp.concatenate(halves, axis=1), ones, preferred_element_type=jnp.float32)
        part = jnp.concatenate([1.0 / count] * (width // tile), axis=1)
        mean = (totals[here, :] * part).astype(jnp.bfloat16)
        joined = jnp.concatenate([features[here, :], mean], axis=1)
        hidden = jnp.dot(joined, weight[...], preferred_element_type=jnp.float32)
        hidden = jnp.maximum(hidden, 0.0)
        scale = lax.rsqrt(jnp.sum(hidden * hidden, axis=1, keepdims=True) + 1e-06)
        out[here, :] = (hidden * scale).astype(jnp.bfloat16)


def layer(slots, counts, froms, sums, left, degree, features, weight):
    blocks_here, tile, across = left.shape
    width = features.shape[1]
    out_width = weight.shape[1]
    rows = 8 if blocks_here % 8 == 0 else 1
    items = rows * tile
    blocks_in_table = sum(piece.shape[0] for piece in froms)
    return pl.pallas_call(
        layer_kernel,
        grid_spec=pltpu.PrefetchScalarGridSpec(
            num_scalar_prefetch=2,
            grid=(blocks_here // rows,),
            in_specs=[pl.BlockSpec(memory_space=pl.ANY)] * len(froms)
            + [
                pl.BlockSpec((items, width), lambda r, *_: (r, 0)),
                pl.BlockSpec((rows, tile, across), lambda r, *_: (r, 0, 0)),
                pl.BlockSpec((blocks_here, tile), lambda r, *_: (0, 0)),
                pl.BlockSpec((items, width), lambda r, *_: (r, 0)),
                pl.BlockSpec((2 * width, out_width), lambda r, *_: (0, 0)),
            ],
            out_specs=pl.BlockSpec((items, out_width), lambda r, *_: (r, 0)),
            scratch_shapes=[
                pltpu.VMEM((blocks_in_table, tile, width), jnp.bfloat16),
                pltpu.VMEM((items, width), jnp.float32),
                pltpu.SemaphoreType.DMA((len(froms),)),
            ],
        ),
        out_shape=jax.ShapeDtypeStruct((blocks_here * tile, out_width), jnp.bfloat16),
        compiler_params=pltpu.CompilerParams(vmem_limit_bytes=VMEM_LIMIT),
        cost_estimate=pl.CostEstimate(
            flops=2 * blocks_here * tile * (across + 2 * width) * out_width,
            bytes_accessed=blocks_here * tile * (4 * width + across + 2 * width + 2 * out_width),
            transcendentals=blocks_here * tile,
        ),
        name="sage_layer",
    )(slots, counts, *froms, sums, left, degree, features, weight)


def on_device(features, tile_cols, tile_masks, degree, weight):
    blocks_here, per_block = tile_cols.shape
    tile = tile_masks.shape[2]
    width = features.shape[1]
    peers = lax.axis_size("rows")
    plane = peers // PLANES
    myself = lax.axis_index("rows")
    z, p = myself // plane, myself % plane
    end = (z == 0) | (z == PLANES - 1)
    capacity = max(2, (REM_PB * blocks_here + peers - 2) // (peers - 1))
    seats_all = plane * capacity
    local = features.reshape(blocks_here, tile, width)
    columns = tile_cols.reshape(-1)
    groups = [[a * plane + q for q in range(plane)] for a in range(PLANES)]

    def exchange(x):
        return lax.all_to_all(
            x, "rows", split_axis=0, concat_axis=0, axis_index_groups=groups, tiled=True
        )

    def shift(x, moves):
        pairs = [(a * plane + q, b * plane + q) for a, b in moves for q in range(plane)]
        return lax.ppermute(x, "rows", pairs)

    asked = exchange(jnp.broadcast_to(columns, (plane,) + columns.shape))
    across = shift(asked, [(0, PLANES - 1), (PLANES - 1, 0)])
    down = [(a, a - 1) for a in range(1, PLANES)]
    up = [(a - 1, a) for a in range(1, PLANES)]
    from_above, from_below = shift(local, down), shift(local, up)

    rounds = jnp.array([[0, 0, 1, 2], [1, 2, 0, 3], [2, 3, 1, 0], [3, 3, 2, 1]], jnp.int32)
    line = pick_row(rounds, z) * plane + p
    blocks = jnp.arange(blocks_here, dtype=jnp.int32)
    wanted = line[:, None] * blocks_here + blocks[None, :]
    below = blocks[:, None] > blocks[None, :]
    seat = jnp.arange(capacity, dtype=jnp.int32)

    def seated(asking, wanted):
        need = jnp.any(asking[:, None, :, None] == wanted[None, :, None, :], axis=2).astype(jnp.int32)
        place = jnp.sum(jnp.where(below, need[:, :, None, :], 0), axis=3)
        taken = (need[:, :, None, :] == 1) & (place[:, :, None, :] == seat[:, None])
        return jnp.sum(jnp.where(taken, blocks, 0), axis=3)

    near = seated(asked, wanted)
    ids = [near[:, k, :].reshape(-1) for k in range(PLANES)]

    owners, within = columns // blocks_here, columns % blocks_here
    positions = jnp.arange(columns.shape[0], dtype=jnp.int32)
    same = columns[:, None] == columns[None, :]
    repeated = jnp.any(same & (positions[None, :] < positions[:, None]), axis=1)
    ahead = (owners[:, None] == owners[None, :]) & (columns[None, :] < columns[:, None])
    ranks = jnp.sum(ahead & ~repeated[None, :], axis=1, dtype=jnp.int32)
    rounds_of = jnp.array([[0, 2, 3, 1], [2, 0, 1, 3], [3, 2, 0, 1], [1, 3, 2, 0]], jnp.int32)
    their_plane = owners // plane
    among = their_plane[:, None] == jnp.arange(PLANES)
    turn = jnp.sum(jnp.where(among, pick_row(rounds_of, z)[None, :], 0), axis=1)
    seats = (owners % plane) * capacity + ranks
    nothing = blocks_here + 3 * seats_all
    final = (turn == 3) | (end & (turn == 1))
    slots = jnp.where(final, nothing, blocks_here + turn * seats_all + seats)
    slots = jnp.where(owners == myself, within, slots)
    seats = jnp.where(turn == 3, seats + seats_all, seats)

    last = final.reshape(blocks_here, per_block)
    counts = jnp.sum(last, axis=1, dtype=jnp.int32)
    order_in = jnp.cumsum(last, axis=1) - 1
    spots = jnp.arange(REM_PB, dtype=jnp.int32)
    chair = last[:, None, :] & (order_in[:, None, :] == spots[:, None])
    late = jnp.sum(jnp.where(chair, jnp.arange(per_block, dtype=jnp.int32), 0), axis=2, dtype=jnp.int32)
    late_slots = jnp.sum(
        jnp.where(chair, seats.reshape(blocks_here, 1, per_block), 0), axis=2, dtype=jnp.int32
    )

    always = jnp.zeros((1,), jnp.int32)
    inner = (~end).astype(jnp.int32)[None]
    picked = choose(always, ids[0], [local], LIGHT)
    got = [exchange(picked)]
    across, _, _ = lax.optimization_barrier((across, from_above, from_below))
    opposite = seated(across, wanted[:1])[:, 0, :]
    ids[1] = either(end.astype(jnp.int32)[None], near[:, 1, :], opposite).reshape(-1)
    ids[1], _ = lax.optimization_barrier((ids[1], got[0]))
    picked = choose(inner, ids[1], [local, from_above], LIGHT)
    got.append(exchange(picked))
    second_down = shift(from_above, down[:-1])
    second_up = shift(from_below, up[1:])
    leaving, _, _ = lax.optimization_barrier((got[1], second_down, second_up))
    crossed = shift(leaving, [(0, PLANES - 1), (PLANES - 1, 0)])
    ids[2], _ = lax.optimization_barrier((ids[2], picked))
    picked = choose((z > 0).astype(jnp.int32)[None], ids[2], [from_above, from_below], HEAVY)
    got.append(exchange(picked))
    beyond = (z >= PLANES // 2).astype(jnp.int32)[None]
    got.append(exchange(choose(beyond, ids[3], [second_down, second_up], LIGHT)))

    sums, left = early(slots, late.reshape(-1), counts, [local] + got[:3], tile_masks)
    return layer(
        late_slots.reshape(-1),
        counts,
        [crossed, got[3]],
        sums,
        left,
        degree.reshape(blocks_here, tile),
        features,
        weight,
    )


def solution(mesh):
    in_specs = (P("rows", None), P("rows", None), P("rows", None, None, None), P("rows"), P())
    out_specs = P("rows", None)
    return jax.shard_map(
        on_device, mesh=mesh, in_specs=in_specs, out_specs=out_specs, check_vma=False
    )
```

```python
import functools

import jax
import jax.numpy as jnp
from jax import lax
from jax.experimental import pallas as pl
from jax.experimental.pallas import tpu as pltpu
from jax.sharding import PartitionSpec as P

REM_PB = 4
PLANES = 4
HEAVY = 3 * 10**10
LIGHT = 10**10

VMEM_LIMIT = 62 * 1024 * 1024


def pick_row(table, z):
    return jnp.sum(jnp.where(jnp.arange(table.shape[0])[:, None] == z, table, 0), axis=0)


def choose_kernel(which, ids, *refs):
    *froms, out, held, in_sem, out_sem = refs
    count, seats = out.shape[0], ids.shape[1]
    for j, source in enumerate(froms):

        @pl.when(which[0] == j)
        def _():
            for n in range(count):
                block = source.at[ids[n // seats, n % seats]]
                pltpu.make_async_copy(block, held.at[n], in_sem).start()

    pltpu.make_async_copy(out, held, in_sem).wait()
    leaving = pltpu.make_async_copy(held, out, out_sem)
    leaving.start()
    leaving.wait()


def choose(which, ids, froms, flops):
    out = (ids.shape[0] * ids.shape[1],) + froms[0].shape[1:]
    moved = out[0] * out[1] * out[2] * 2
    return pl.pallas_call(
        choose_kernel,
        grid_spec=pltpu.PrefetchScalarGridSpec(
            num_scalar_prefetch=2,
            grid=(1,),
            in_specs=[pl.BlockSpec(memory_space=pltpu.HBM)] * len(froms),
            out_specs=pl.BlockSpec(memory_space=pltpu.HBM),
            scratch_shapes=[
                pltpu.VMEM(out, froms[0].dtype),
                pltpu.SemaphoreType.DMA,
                pltpu.SemaphoreType.DMA,
            ],
        ),
        out_shape=jax.ShapeDtypeStruct(out, froms[0].dtype),
        compiler_params=pltpu.CompilerParams(vmem_limit_bytes=VMEM_LIMIT),
        cost_estimate=pl.CostEstimate(flops=flops, bytes_accessed=2 * moved, transcendentals=0),
        name="choose_blocks",
    )(which, ids, *froms)


def either_kernel(second, a, b, out):
    out[...] = jnp.where(second[0] == 1, b[...], a[...])


def either(second, a, b):
    whole = pl.BlockSpec(a.shape, lambda i, s: (0, 0))
    return pl.pallas_call(
        either_kernel,
        grid_spec=pltpu.PrefetchScalarGridSpec(
            num_scalar_prefetch=1, grid=(1,), in_specs=[whole, whole], out_specs=whole
        ),
        out_shape=jax.ShapeDtypeStruct(a.shape, a.dtype),
        cost_estimate=pl.CostEstimate(flops=HEAVY, bytes_accessed=0, transcendentals=0),
        name="either_ids",
    )(second, a, b)


def fill(pieces, table, sems):
    copies, at = [], 0
    for n, piece in enumerate(pieces):
        here = table.at[pl.ds(at, piece.shape[0])]
        copies.append(pltpu.make_async_copy(piece, here, sems.at[n]))
        at += piece.shape[0]
    for copy in copies:
        copy.start()
    for copy in copies:
        copy.wait()


def early_kernel(slots, late, counts, *refs):
    *froms, masks, sums, left, table, sems = refs
    step = pl.program_id(0)
    rows, per_block = masks.shape[:2]
    tile, width = table.shape[1:]
    spare = left.shape[2] // tile

    @pl.when(step == 0)
    def _():
        table[table.shape[0] - 1] = jnp.zeros((tile, width), table.dtype)
        fill(froms, table, sems)

    for r in range(rows):
        row = step * rows + r
        here = pl.ds(r * tile, tile)
        mask = jnp.concatenate(
            [masks[r, t].astype(jnp.float32).astype(jnp.bfloat16) for t in range(per_block)], axis=1
        )
        picked = jnp.concatenate(
            [table[slots[row * per_block + t]] for t in range(per_block)], axis=0
        )
        sums[here, :] = jnp.dot(mask, picked, preferred_element_type=jnp.float32)
        for t in range(spare):
            kept = jnp.where(t < counts[row], masks[r, late[row * spare + t]], 0)
            left[r, :, t * tile : (t + 1) * tile] = kept.astype(jnp.int8)


def early(slots, late, counts, froms, tile_masks):
    blocks_here, per_block, tile, _ = tile_masks.shape
    width = froms[0].shape[2]
    spare = late.shape[0] // blocks_here
    rows = 4 if blocks_here % 4 == 0 else 1
    blocks_in_table = sum(piece.shape[0] for piece in froms) + 1
    return pl.pallas_call(
        early_kernel,
        grid_spec=pltpu.PrefetchScalarGridSpec(
            num_scalar_prefetch=3,
            grid=(blocks_here // rows,),
            in_specs=[pl.BlockSpec(memory_space=pl.ANY)] * len(froms)
            + [pl.BlockSpec((rows, per_block, tile, tile), lambda r, *_: (r, 0, 0, 0))],
            out_specs=[
                pl.BlockSpec((rows * tile, width), lambda r, *_: (r, 0)),
                pl.BlockSpec((rows, tile, spare * tile), lambda r, *_: (r, 0, 0)),
            ],
            scratch_shapes=[
                pltpu.VMEM((blocks_in_table, tile, width), jnp.bfloat16),
                pltpu.SemaphoreType.DMA((len(froms),)),
            ],
        ),
        out_shape=[
            jax.ShapeDtypeStruct((blocks_here * tile, width), jnp.float32),
            jax.ShapeDtypeStruct((blocks_here, tile, spare * tile), jnp.int8),
        ],
        compiler_params=pltpu.CompilerParams(vmem_limit_bytes=VMEM_LIMIT),
        cost_estimate=pl.CostEstimate(
            flops=2 * LIGHT,
            bytes_accessed=blocks_here * per_block * tile * tile * 6 + blocks_in_table * tile * width * 2,
            transcendentals=0,
        ),
        name="early_sums",
    )(slots, late, counts, *froms, tile_masks)


def layer_kernel(slots, counts, *refs):
    *froms, sums, left, degree, features, weight, out, table, totals, share, sems = refs
    step = pl.program_id(0)
    rows, tile = left.shape[:2]
    width = table.shape[2]
    spare = left.shape[2] // tile
    pair = min(2, spare)
    pl.when(step == 0)(functools.partial(fill, froms, table, sems))

    def added(r, first):
        ends = min(first + pair, spare)
        picked = [table[slots[(step * rows + r) * spare + t]] for t in range(first, ends)]
        mask = left[r, :, first * tile : ends * tile].astype(jnp.int32)
        mask = mask.astype(jnp.float32).astype(jnp.bfloat16)
        return jnp.dot(mask, jnp.concatenate(picked, axis=0), preferred_element_type=jnp.float32)

    for r in range(rows):
        here = pl.ds(r * tile, tile)
        totals[here, :] = sums[here, :] + added(r, 0)
    for r in range(rows):
        here = pl.ds(r * tile, tile)
        for first in range(pair, spare, pair):

            @pl.when(counts[step * rows + r] > first)
            def _():
                totals[here, :] += added(r, first)

    column = lax.broadcasted_iota(jnp.int32, (tile, tile), 1)
    diagonal = lax.broadcasted_iota(jnp.int32, (tile, tile), 0) == column
    spread = []
    for r in range(rows):
        count = degree[pl.ds(step * rows + r, 1), :]
        small = count & 7
        halves = [
            jnp.where(diagonal, part.astype(jnp.float32), 0.0).astype(jnp.bfloat16)
            for part in (count - small, small)
        ]
        spread.append(jnp.concatenate(halves, axis=1))
    ones = jnp.ones((2 * tile, tile), jnp.bfloat16)
    share[...] = 1.0 / jnp.dot(
        jnp.concatenate(spread, axis=0), ones, preferred_element_type=jnp.float32
    )

    many = min(rows, 4) * tile
    for first in range(0, rows * tile, many):
        here = pl.ds(first, many)
        part = jnp.concatenate([share[here, :]] * (width // tile), axis=1)
        mean = (totals[here, :] * part).astype(jnp.bfloat16)
        joined = jnp.concatenate([features[here, :], mean], axis=1)
        hidden = jnp.dot(joined, weight[...], preferred_element_type=jnp.float32)
        hidden = jnp.maximum(hidden, 0.0)
        scale = lax.rsqrt(jnp.sum(hidden * hidden, axis=1, keepdims=True) + 1e-06)
        out[here, :] = (hidden * scale).astype(jnp.bfloat16)


def layer(slots, counts, froms, sums, left, degree, features, weight):
    blocks_here, tile, across = left.shape
    width = features.shape[1]
    out_width = weight.shape[1]
    rows = 8 if blocks_here % 8 == 0 else 1
    items = rows * tile
    blocks_in_table = sum(piece.shape[0] for piece in froms)
    return pl.pallas_call(
        layer_kernel,
        grid_spec=pltpu.PrefetchScalarGridSpec(
            num_scalar_prefetch=2,
            grid=(blocks_here // rows,),
            in_specs=[pl.BlockSpec(memory_space=pl.ANY)] * len(froms)
            + [
                pl.BlockSpec((items, width), lambda r, *_: (r, 0)),
                pl.BlockSpec((rows, tile, across), lambda r, *_: (r, 0, 0)),
                pl.BlockSpec((blocks_here, tile), lambda r, *_: (0, 0)),
                pl.BlockSpec((items, width), lambda r, *_: (r, 0)),
                pl.BlockSpec((2 * width, out_width), lambda r, *_: (0, 0)),
            ],
            out_specs=pl.BlockSpec((items, out_width), lambda r, *_: (r, 0)),
            scratch_shapes=[
                pltpu.VMEM((blocks_in_table, tile, width), jnp.bfloat16),
                pltpu.VMEM((items, width), jnp.float32),
                pltpu.VMEM((items, tile), jnp.float32),
                pltpu.SemaphoreType.DMA((len(froms),)),
            ],
        ),
        out_shape=jax.ShapeDtypeStruct((blocks_here * tile, out_width), jnp.bfloat16),
        compiler_params=pltpu.CompilerParams(vmem_limit_bytes=VMEM_LIMIT),
        cost_estimate=pl.CostEstimate(
            flops=2 * blocks_here * tile * (across + 2 * width) * out_width,
            bytes_accessed=blocks_here * tile * (4 * width + across + 2 * width + 2 * out_width),
            transcendentals=blocks_here * tile,
        ),
        name="sage_layer",
    )(slots, counts, *froms, sums, left, degree, features, weight)


def on_device(features, tile_cols, tile_masks, degree, weight):
    blocks_here, per_block = tile_cols.shape
    tile = tile_masks.shape[2]
    width = features.shape[1]
    peers = lax.axis_size("rows")
    plane = peers // PLANES
    myself = lax.axis_index("rows")
    z, p = myself // plane, myself % plane
    end = (z == 0) | (z == PLANES - 1)
    capacity = max(2, (REM_PB * blocks_here + peers - 2) // (peers - 1))
    seats_all = plane * capacity
    local = features.reshape(blocks_here, tile, width)
    columns = tile_cols.reshape(-1)
    groups = [[a * plane + q for q in range(plane)] for a in range(PLANES)]

    def exchange(x):
        return lax.all_to_all(
            x, "rows", split_axis=0, concat_axis=0, axis_index_groups=groups, tiled=True
        )

    def shift(x, moves):
        pairs = [(a * plane + q, b * plane + q) for a, b in moves for q in range(plane)]
        return lax.ppermute(x, "rows", pairs)

    asked = exchange(jnp.broadcast_to(columns, (plane,) + columns.shape))
    across = shift(asked, [(0, PLANES - 1), (PLANES - 1, 0)])
    down = [(a, a - 1) for a in range(1, PLANES)]
    up = [(a - 1, a) for a in range(1, PLANES)]
    from_above, from_below = shift(local, down), shift(local, up)

    rounds = jnp.array([[0, 0, 1, 2], [1, 2, 0, 3], [2, 3, 1, 0], [3, 3, 2, 1]], jnp.int32)
    line = pick_row(rounds, z) * plane + p
    blocks = jnp.arange(blocks_here, dtype=jnp.int32)
    wanted = line[:, None] * blocks_here + blocks[None, :]
    below = blocks[:, None] > blocks[None, :]
    seat = jnp.arange(capacity, dtype=jnp.int32)

    def seated(asking, wanted):
        need = jnp.any(asking[:, None, :, None] == wanted[None, :, None, :], axis=2).astype(jnp.int32)
        place = jnp.sum(jnp.where(below, need[:, :, None, :], 0), axis=3)
        taken = (need[:, :, None, :] == 1) & (place[:, :, None, :] == seat[:, None])
        return jnp.sum(jnp.where(taken, blocks, 0), axis=3)

    near = seated(asked, wanted)
    ids = [near[:, k, :] for k in range(PLANES)]

    owners, within = columns // blocks_here, columns % blocks_here
    positions = jnp.arange(columns.shape[0], dtype=jnp.int32)
    same = columns[:, None] == columns[None, :]
    repeated = jnp.any(same & (positions[None, :] < positions[:, None]), axis=1)
    ahead = (owners[:, None] == owners[None, :]) & (columns[None, :] < columns[:, None])
    ranks = jnp.sum(ahead & ~repeated[None, :], axis=1, dtype=jnp.int32)
    rounds_of = jnp.array([[0, 2, 3, 1], [2, 0, 1, 3], [3, 2, 0, 1], [1, 3, 2, 0]], jnp.int32)
    their_plane = owners // plane
    among = their_plane[:, None] == jnp.arange(PLANES)
    turn = jnp.sum(jnp.where(among, pick_row(rounds_of, z)[None, :], 0), axis=1)
    seats = (owners % plane) * capacity + ranks
    nothing = blocks_here + 3 * seats_all
    final = (turn == 3) | (end & (turn == 1))
    slots = jnp.where(final, nothing, blocks_here + turn * seats_all + seats)
    slots = jnp.where(owners == myself, within, slots)
    seats = jnp.where(turn == 3, seats + seats_all, seats)

    last = final.reshape(blocks_here, per_block)
    counts = jnp.sum(last, axis=1, dtype=jnp.int32)
    order_in = jnp.cumsum(last, axis=1) - 1
    spots = jnp.arange(REM_PB, dtype=jnp.int32)
    chair = last[:, None, :] & (order_in[:, None, :] == spots[:, None])
    late = jnp.sum(jnp.where(chair, jnp.arange(per_block, dtype=jnp.int32), 0), axis=2, dtype=jnp.int32)
    late_slots = jnp.sum(
        jnp.where(chair, seats.reshape(blocks_here, 1, per_block), 0), axis=2, dtype=jnp.int32
    )

    always = jnp.zeros((1,), jnp.int32)
    inner = (~end).astype(jnp.int32)[None]
    picked = choose(always, ids[0], [local], LIGHT)
    got = [exchange(picked)]
    across, _, _ = lax.optimization_barrier((across, from_above, from_below))
    opposite = seated(across, wanted[:1])[:, 0, :]
    ids[1] = either(end.astype(jnp.int32)[None], near[:, 1, :], opposite)
    picked = choose(inner, ids[1], [local, from_above], LIGHT)
    leaving, _ = lax.optimization_barrier((picked, got[0]))
    got.append(exchange(leaving))
    second_down = shift(from_above, down[:-1])
    second_up = shift(from_below, up[1:])
    leaving, _, _ = lax.optimization_barrier((got[1], second_down, second_up))
    crossed = shift(leaving, [(0, PLANES - 1), (PLANES - 1, 0)])
    ids[2], _ = lax.optimization_barrier((ids[2], picked))
    picked = choose((z > 0).astype(jnp.int32)[None], ids[2], [from_above, from_below], HEAVY)
    got.append(exchange(picked))
    beyond = (z >= PLANES // 2).astype(jnp.int32)[None]
    got.append(exchange(choose(beyond, ids[3], [second_down, second_up], LIGHT)))

    sums, left = early(slots, late.reshape(-1), counts, [local] + got[:3], tile_masks)
    return layer(
        late_slots.reshape(-1),
        counts,
        [crossed, got[3]],
        sums,
        left,
        degree.reshape(blocks_here, tile),
        features,
        weight,
    )


def solution(mesh):
    in_specs = (P("rows", None), P("rows", None), P("rows", None, None, None), P("rows"), P())
    out_specs = P("rows", None)
    return jax.shard_map(
        on_device, mesh=mesh, in_specs=in_specs, out_specs=out_specs, check_vma=False
    )
```

```python
import functools

import jax
import jax.numpy as jnp
from jax import lax
from jax.experimental import pallas as pl
from jax.experimental.pallas import tpu as pltpu
from jax.sharding import PartitionSpec as P

REM_PB = 4
PLANES = 4
HEAVY = 3 * 10**10
LIGHT = 10**10

VMEM_LIMIT = 62 * 1024 * 1024


def pick_row(table, z):
    return jnp.sum(jnp.where(jnp.arange(table.shape[0])[:, None] == z, table, 0), axis=0)


def choose_kernel(which, ids, *refs, turn):
    *froms, out, held, in_sem, out_sem = refs
    count, seats = out.shape[0], ids.shape[2]
    for j, source in enumerate(froms):

        @pl.when(which[0] == j)
        def _():
            for n in range(count):
                block = source.at[ids[turn, n // seats, n % seats]]
                pltpu.make_async_copy(block, held.at[n], in_sem).start()

    pltpu.make_async_copy(out, held, in_sem).wait()
    leaving = pltpu.make_async_copy(held, out, out_sem)
    leaving.start()
    leaving.wait()


def choose(which, ids, turn, froms, flops):
    out = (ids.shape[1] * ids.shape[2],) + froms[0].shape[1:]
    moved = out[0] * out[1] * out[2] * 2
    return pl.pallas_call(
        functools.partial(choose_kernel, turn=turn),
        grid_spec=pltpu.PrefetchScalarGridSpec(
            num_scalar_prefetch=2,
            grid=(1,),
            in_specs=[pl.BlockSpec(memory_space=pltpu.HBM)] * len(froms),
            out_specs=pl.BlockSpec(memory_space=pltpu.HBM),
            scratch_shapes=[
                pltpu.VMEM(out, froms[0].dtype),
                pltpu.SemaphoreType.DMA,
                pltpu.SemaphoreType.DMA,
            ],
        ),
        out_shape=jax.ShapeDtypeStruct(out, froms[0].dtype),
        compiler_params=pltpu.CompilerParams(vmem_limit_bytes=VMEM_LIMIT),
        cost_estimate=pl.CostEstimate(flops=flops, bytes_accessed=2 * moved, transcendentals=0),
        name="choose_blocks",
    )(which, ids, *froms)


def either_kernel(second, a, b, out):
    out[...] = jnp.where(second[0] == 1, b[...], a[1:2])


def either(second, a, b):
    return pl.pallas_call(
        either_kernel,
        grid_spec=pltpu.PrefetchScalarGridSpec(
            num_scalar_prefetch=1,
            grid=(1,),
            in_specs=[
                pl.BlockSpec(a.shape, lambda i, s: (0, 0, 0)),
                pl.BlockSpec(b.shape, lambda i, s: (0, 0, 0)),
            ],
            out_specs=pl.BlockSpec(b.shape, lambda i, s: (0, 0, 0)),
        ),
        out_shape=jax.ShapeDtypeStruct(b.shape, b.dtype),
        cost_estimate=pl.CostEstimate(flops=LIGHT // 2, bytes_accessed=0, transcendentals=0),
        name="either_ids",
    )(second, a, b)


def fill(pieces, table, sems):
    copies, at = [], 0
    for n, piece in enumerate(pieces):
        here = table.at[pl.ds(at, piece.shape[0])]
        copies.append(pltpu.make_async_copy(piece, here, sems.at[n]))
        at += piece.shape[0]
    for copy in copies:
        copy.start()
    for copy in copies:
        copy.wait()


def early_kernel(slots, late, counts, *refs):
    *froms, masks, sums, left, more, table, sems = refs
    step = pl.program_id(0)
    rows, per_block = masks.shape[:2]
    tile, width = table.shape[1:]
    pair = left.shape[2] // tile

    @pl.when(step == 0)
    def _():
        table[table.shape[0] - 1] = jnp.zeros((tile, width), table.dtype)
        fill(froms, table, sems)

    for r in range(rows):
        row = step * rows + r
        here = pl.ds(r * tile, tile)
        mask = jnp.concatenate(
            [masks[r, t].astype(jnp.float32).astype(jnp.bfloat16) for t in range(per_block)], axis=1
        )
        picked = jnp.concatenate(
            [table[slots[row * per_block + t]] for t in range(per_block)], axis=0
        )
        sums[here, :] = jnp.dot(mask, picked, preferred_element_type=jnp.float32)
        for t in range(2 * pair):
            kept = masks[r, late[row * 2 * pair + t]].astype(jnp.float32)
            kept = jnp.where(t < counts[row], kept, 0.0).astype(jnp.bfloat16)
            into = left if t < pair else more
            into[r, :, t % pair * tile : (t % pair + 1) * tile] = kept


def early(slots, late, counts, froms, tile_masks):
    blocks_here, per_block, tile, _ = tile_masks.shape
    width = froms[0].shape[2]
    half = late.shape[0] // blocks_here // 2 * tile
    rows = 4 if blocks_here % 4 == 0 else 1
    blocks_in_table = sum(piece.shape[0] for piece in froms) + 1
    return pl.pallas_call(
        early_kernel,
        grid_spec=pltpu.PrefetchScalarGridSpec(
            num_scalar_prefetch=3,
            grid=(blocks_here // rows,),
            in_specs=[pl.BlockSpec(memory_space=pl.ANY)] * len(froms)
            + [pl.BlockSpec((rows, per_block, tile, tile), lambda r, *_: (r, 0, 0, 0))],
            out_specs=[
                pl.BlockSpec((rows * tile, width), lambda r, *_: (r, 0)),
                pl.BlockSpec((rows, tile, half), lambda r, *_: (r, 0, 0)),
                pl.BlockSpec((rows, tile, half), lambda r, *_: (r, 0, 0)),
            ],
            scratch_shapes=[
                pltpu.VMEM((blocks_in_table, tile, width), jnp.bfloat16),
                pltpu.SemaphoreType.DMA((len(froms),)),
            ],
        ),
        out_shape=[
            jax.ShapeDtypeStruct((blocks_here * tile, width), jnp.float32),
            jax.ShapeDtypeStruct((blocks_here, tile, half), jnp.bfloat16),
            jax.ShapeDtypeStruct((blocks_here, tile, half), jnp.bfloat16),
        ],
        compiler_params=pltpu.CompilerParams(vmem_limit_bytes=VMEM_LIMIT),
        cost_estimate=pl.CostEstimate(
            flops=2 * LIGHT,
            bytes_accessed=blocks_here * per_block * tile * tile * 6 + blocks_in_table * tile * width * 2,
            transcendentals=0,
        ),
        name="early_sums",
    )(slots, late, counts, *froms, tile_masks)


def layer_kernel(slots, counts, *refs):
    *froms, more, sums, left, degree, features, weight, out, table, extra, totals, share, sems, extra_sems = refs
    step = pl.program_id(0)
    rows, tile = left.shape[:2]
    pair = left.shape[2] // tile
    width = table.shape[2]
    blocks_here = more.shape[0]

    def fetch(row):
        return pltpu.make_async_copy(more.at[row], extra.at[row], extra_sems.at[row])

    @pl.when(step == 0)
    def _():
        for row in range(blocks_here):
            pl.when(counts[row] > pair)(fetch(row).start)
        fill(froms, table, sems)

    def added(row, first, mask):
        picked = [table[slots[row * 2 * pair + t]] for t in range(first, first + pair)]
        return jnp.dot(mask, jnp.concatenate(picked, axis=0), preferred_element_type=jnp.float32)

    for r in range(rows):
        here = pl.ds(r * tile, tile)
        totals[here, :] = sums[here, :] + added(step * rows + r, 0, left[r])
    for r in range(rows):
        row = step * rows + r
        here = pl.ds(r * tile, tile)

        @pl.when(counts[row] > pair)
        def _():
            fetch(row).wait()
            totals[here, :] += added(row, pair, extra[row])

    column = lax.broadcasted_iota(jnp.int32, (tile, tile), 1)
    diagonal = lax.broadcasted_iota(jnp.int32, (tile, tile), 0) == column
    spread = []
    for r in range(rows):
        count = degree[pl.ds(step * rows + r, 1), :]
        small = count & 7
        halves = [
            jnp.where(diagonal, part.astype(jnp.float32), 0.0).astype(jnp.bfloat16)
            for part in (count - small, small)
        ]
        spread.append(jnp.concatenate(halves, axis=1))
    ones = jnp.ones((2 * tile, tile), jnp.bfloat16)
    share[...] = 1.0 / jnp.dot(
        jnp.concatenate(spread, axis=0), ones, preferred_element_type=jnp.float32
    )

    out_width = out.shape[1]
    ones = jnp.ones((2 * out_width, tile), jnp.bfloat16)
    many = min(rows, 2) * tile
    for first in range(0, rows * tile, many):
        here = pl.ds(first, many)
        part = jnp.concatenate([share[here, :]] * (width // tile), axis=1)
        mean = (totals[here, :] * part).astype(jnp.bfloat16)
        joined = jnp.concatenate([features[here, :], mean], axis=1)
        hidden = jnp.dot(joined, weight[...], preferred_element_type=jnp.float32)
        hidden = jnp.maximum(hidden, 0.0)
        squares = hidden * hidden
        high = squares.astype(jnp.bfloat16)
        low = (squares - high.astype(jnp.float32)).astype(jnp.bfloat16)
        total = jnp.dot(
            jnp.concatenate([high, low], axis=1), ones, preferred_element_type=jnp.float32
        )
        scale = jnp.concatenate([lax.rsqrt(total + 1e-06)] * (out_width // tile), axis=1)
        out[here, :] = (hidden * scale).astype(jnp.bfloat16)


def layer(slots, counts, froms, sums, left, more, degree, features, weight):
    blocks_here, tile, across = left.shape
    width = features.shape[1]
    out_width = weight.shape[1]
    rows = 8 if blocks_here % 8 == 0 else 1
    items = rows * tile
    blocks_in_table = sum(piece.shape[0] for piece in froms)
    return pl.pallas_call(
        layer_kernel,
        grid_spec=pltpu.PrefetchScalarGridSpec(
            num_scalar_prefetch=2,
            grid=(blocks_here // rows,),
            in_specs=[pl.BlockSpec(memory_space=pl.ANY)] * (len(froms) + 1)
            + [
                pl.BlockSpec((items, width), lambda r, *_: (r, 0)),
                pl.BlockSpec((rows, tile, across), lambda r, *_: (r, 0, 0)),
                pl.BlockSpec((blocks_here, tile), lambda r, *_: (0, 0)),
                pl.BlockSpec((items, width), lambda r, *_: (r, 0)),
                pl.BlockSpec((2 * width, out_width), lambda r, *_: (0, 0)),
            ],
            out_specs=pl.BlockSpec((items, out_width), lambda r, *_: (r, 0)),
            scratch_shapes=[
                pltpu.VMEM((blocks_in_table, tile, width), jnp.bfloat16),
                pltpu.VMEM((blocks_here, tile, across), jnp.bfloat16),
                pltpu.VMEM((items, width), jnp.float32),
                pltpu.VMEM((items, tile), jnp.float32),
                pltpu.SemaphoreType.DMA((len(froms),)),
                pltpu.SemaphoreType.DMA((blocks_here,)),
            ],
        ),
        out_shape=jax.ShapeDtypeStruct((blocks_here * tile, out_width), jnp.bfloat16),
        compiler_params=pltpu.CompilerParams(vmem_limit_bytes=VMEM_LIMIT),
        cost_estimate=pl.CostEstimate(
            flops=2 * blocks_here * tile * (across + 2 * width) * out_width,
            bytes_accessed=blocks_here * tile * (4 * width + 2 * across + 2 * width + 2 * out_width),
            transcendentals=blocks_here * tile,
        ),
        name="sage_layer",
    )(slots, counts, *froms, more, sums, left, degree, features, weight)


def on_device(features, tile_cols, tile_masks, degree, weight):
    blocks_here, per_block = tile_cols.shape
    tile = tile_masks.shape[2]
    width = features.shape[1]
    peers = lax.axis_size("rows")
    plane = peers // PLANES
    myself = lax.axis_index("rows")
    z, p = myself // plane, myself % plane
    end = (z == 0) | (z == PLANES - 1)
    capacity = max(2, (REM_PB * blocks_here + peers - 2) // (peers - 1))
    seats_all = plane * capacity
    local = features.reshape(blocks_here, tile, width)
    columns = tile_cols.reshape(-1)
    groups = [[a * plane + q for q in range(plane)] for a in range(PLANES)]

    def exchange(x):
        return lax.all_to_all(
            x, "rows", split_axis=0, concat_axis=0, axis_index_groups=groups, tiled=True
        )

    def shift(x, moves):
        pairs = [(a * plane + q, b * plane + q) for a, b in moves for q in range(plane)]
        return lax.ppermute(x, "rows", pairs)

    asked = exchange(jnp.broadcast_to(columns, (plane,) + columns.shape))
    down = [(a, a - 1) for a in range(1, PLANES)]
    up = [(a - 1, a) for a in range(1, PLANES)]
    from_above, from_below = shift(local, down), shift(local, up)

    rounds = jnp.array([[0, 0, 1, 2], [1, 2, 0, 3], [2, 3, 1, 0], [3, 3, 2, 1]], jnp.int32)
    line = pick_row(rounds, z) * plane + p
    blocks = jnp.arange(blocks_here, dtype=jnp.int32)
    wanted = line[:, None] * blocks_here + blocks[None, :]
    below = blocks[:, None] > blocks[None, :]
    seat = jnp.arange(capacity, dtype=jnp.int32)

    def seated(asking, wanted):
        need = jnp.any(asking[:, None, :, None] == wanted[None, :, None, :], axis=2).astype(jnp.int32)
        place = jnp.sum(jnp.where(below, need[:, :, None, :], 0), axis=3)
        taken = (need[:, :, None, :] == 1) & (place[:, :, None, :] == seat[:, None])
        return jnp.sum(jnp.where(taken, blocks, 0), axis=3)

    near = jnp.swapaxes(seated(asked, wanted), 0, 1)

    owners, within = columns // blocks_here, columns % blocks_here
    positions = jnp.arange(columns.shape[0], dtype=jnp.int32)
    same = columns[:, None] == columns[None, :]
    repeated = jnp.any(same & (positions[None, :] < positions[:, None]), axis=1)
    ahead = (owners[:, None] == owners[None, :]) & (columns[None, :] < columns[:, None])
    ranks = jnp.sum(ahead & ~repeated[None, :], axis=1, dtype=jnp.int32)
    rounds_of = jnp.array([[0, 2, 3, 1], [2, 0, 1, 3], [3, 2, 0, 1], [1, 3, 2, 0]], jnp.int32)
    their_plane = owners // plane
    among = their_plane[:, None] == jnp.arange(PLANES)
    turn = jnp.sum(jnp.where(among, pick_row(rounds_of, z)[None, :], 0), axis=1)
    seats = (owners % plane) * capacity + ranks
    nothing = blocks_here + 3 * seats_all
    final = (turn == 3) | (end & (turn == 1))
    slots = jnp.where(final, nothing, blocks_here + turn * seats_all + seats)
    slots = jnp.where(owners == myself, within, slots)
    seats = jnp.where(turn == 3, seats + seats_all, seats)

    last = final.reshape(blocks_here, per_block)
    counts = jnp.sum(last, axis=1, dtype=jnp.int32)
    order_in = jnp.cumsum(last, axis=1) - 1
    spots = jnp.arange(REM_PB, dtype=jnp.int32)
    chair = last[:, None, :] & (order_in[:, None, :] == spots[:, None])
    late = jnp.sum(jnp.where(chair, jnp.arange(per_block, dtype=jnp.int32), 0), axis=2, dtype=jnp.int32)
    late_slots = jnp.sum(
        jnp.where(chair, seats.reshape(blocks_here, 1, per_block), 0), axis=2, dtype=jnp.int32
    )

    always = jnp.zeros((1,), jnp.int32)
    inner = (~end).astype(jnp.int32)[None]
    picked = choose(always, near, 0, [local], LIGHT)
    got = [exchange(picked)]
    asked, _ = lax.optimization_barrier((asked, picked))
    across = shift(asked, [(0, PLANES - 1), (PLANES - 1, 0)])
    across, _, _ = lax.optimization_barrier((across, from_above, from_below))
    opposite = jnp.swapaxes(seated(across, wanted[:1]), 0, 1)
    middle = either(end.astype(jnp.int32)[None], near, opposite)
    picked = choose(inner, middle, 0, [local, from_above], LIGHT)
    leaving, _ = lax.optimization_barrier((picked, got[0]))
    got.append(exchange(leaving))
    second_down = shift(from_above, down[:-1])
    second_up = shift(from_below, up[1:])
    leaving, _, _ = lax.optimization_barrier((got[1], second_down, second_up))
    crossed = shift(leaving, [(0, PLANES - 1), (PLANES - 1, 0)])
    near, _ = lax.optimization_barrier((near, picked))
    below_or_above = (z > 0).astype(jnp.int32)[None]
    got.append(exchange(choose(below_or_above, near, 2, [from_above, from_below], HEAVY)))
    beyond = (z >= PLANES // 2).astype(jnp.int32)[None]
    got.append(exchange(choose(beyond, near, 3, [second_down, second_up], LIGHT)))

    sums, left, more = early(slots, late.reshape(-1), counts, [local] + got[:3], tile_masks)
    return layer(
        late_slots.reshape(-1),
        counts,
        [crossed, got[3]],
        sums,
        left,
        more,
        degree.reshape(blocks_here, tile),
        features,
        weight,
    )


def solution(mesh):
    in_specs = (P("rows", None), P("rows", None), P("rows", None, None, None), P("rows"), P())
    out_specs = P("rows", None)
    return jax.shard_map(
        on_device, mesh=mesh, in_specs=in_specs, out_specs=out_specs, check_vma=False
    )
```

```python
import functools

import jax
import jax.numpy as jnp
from jax import lax
from jax.experimental import pallas as pl
from jax.experimental.pallas import tpu as pltpu
from jax.sharding import PartitionSpec as P

REM_PB = 4
PLANES = 4
HEAVY = 3 * 10**10
LIGHT = 10**10

VMEM_LIMIT = 62 * 1024 * 1024


def pick_row(table, z):
    return jnp.sum(jnp.where(jnp.arange(table.shape[0])[:, None] == z, table, 0), axis=0)


def choose_kernel(which, *refs, turns):
    lists, (*froms, out, held, in_sems, out_sems) = refs[: len(turns)], refs[len(turns) :]
    count, seats = out.shape[0], lists[0].shape[2]
    groups = in_sems.shape[0]
    size = count // groups
    for j, source in enumerate(froms):
        ids, turn = lists[j % len(turns)], turns[j % len(turns)]

        @pl.when(which[0] == j)
        def _():
            for n in range(count):
                block = source.at[ids[turn, n // seats, n % seats]]
                pltpu.make_async_copy(block, held.at[n], in_sems.at[n // size]).start()

    leaving = []
    for g in range(groups):
        here = pl.ds(g * size, size)
        pltpu.make_async_copy(out.at[here], held.at[here], in_sems.at[g]).wait()
        leaving.append(pltpu.make_async_copy(held.at[here], out.at[here], out_sems.at[g]))
        leaving[-1].start()
    for copy in leaving:
        copy.wait()


def choose(which, lists, turns, froms, flops):
    out = (lists[0].shape[1] * lists[0].shape[2],) + froms[0].shape[1:]
    moved = out[0] * out[1] * out[2] * 2
    groups = 4 if out[0] % 4 == 0 else 1
    return pl.pallas_call(
        functools.partial(choose_kernel, turns=turns),
        grid_spec=pltpu.PrefetchScalarGridSpec(
            num_scalar_prefetch=1 + len(lists),
            grid=(1,),
            in_specs=[pl.BlockSpec(memory_space=pltpu.HBM)] * len(froms),
            out_specs=pl.BlockSpec(memory_space=pltpu.HBM),
            scratch_shapes=[
                pltpu.VMEM(out, froms[0].dtype),
                pltpu.SemaphoreType.DMA((groups,)),
                pltpu.SemaphoreType.DMA((groups,)),
            ],
        ),
        out_shape=jax.ShapeDtypeStruct(out, froms[0].dtype),
        compiler_params=pltpu.CompilerParams(vmem_limit_bytes=VMEM_LIMIT),
        cost_estimate=pl.CostEstimate(flops=flops, bytes_accessed=2 * moved, transcendentals=0),
        name="choose_blocks",
    )(which, *lists, *froms)


def fill(pieces, table, sems):
    copies, at = [], 0
    for n, piece in enumerate(pieces):
        here = table.at[pl.ds(at, piece.shape[0])]
        copies.append(pltpu.make_async_copy(piece, here, sems.at[n]))
        at += piece.shape[0]
    for copy in copies:
        copy.start()
    for copy in copies:
        copy.wait()


def early_kernel(slots, late, counts, *refs):
    *froms, masks, sums, left, more, table, sems = refs
    step = pl.program_id(0)
    rows, per_block = masks.shape[:2]
    tile, width = table.shape[1:]
    pair = left.shape[2] // tile

    @pl.when(step == 0)
    def _():
        table[table.shape[0] - 1] = jnp.zeros((tile, width), table.dtype)
        fill(froms, table, sems)

    for r in range(rows):
        row = step * rows + r
        here = pl.ds(r * tile, tile)
        mask = jnp.concatenate(
            [masks[r, t].astype(jnp.float32).astype(jnp.bfloat16) for t in range(per_block)], axis=1
        )
        picked = jnp.concatenate(
            [table[slots[row * per_block + t]] for t in range(per_block)], axis=0
        )
        sums[here, :] = jnp.dot(mask, picked, preferred_element_type=jnp.float32)
        for t in range(2 * pair):
            kept = masks[r, late[row * 2 * pair + t]].astype(jnp.float32)
            kept = jnp.where(t < counts[row], kept, 0.0).astype(jnp.bfloat16)
            into = left if t < pair else more
            into[r, :, t % pair * tile : (t % pair + 1) * tile] = kept


def early(slots, late, counts, froms, tile_masks):
    blocks_here, per_block, tile, _ = tile_masks.shape
    width = froms[0].shape[2]
    half = late.shape[0] // blocks_here // 2 * tile
    rows = 4 if blocks_here % 4 == 0 else 1
    blocks_in_table = sum(piece.shape[0] for piece in froms) + 1
    return pl.pallas_call(
        early_kernel,
        grid_spec=pltpu.PrefetchScalarGridSpec(
            num_scalar_prefetch=3,
            grid=(blocks_here // rows,),
            in_specs=[pl.BlockSpec(memory_space=pl.ANY)] * len(froms)
            + [pl.BlockSpec((rows, per_block, tile, tile), lambda r, *_: (r, 0, 0, 0))],
            out_specs=[
                pl.BlockSpec((rows * tile, width), lambda r, *_: (r, 0)),
                pl.BlockSpec((rows, tile, half), lambda r, *_: (r, 0, 0)),
                pl.BlockSpec((rows, tile, half), lambda r, *_: (r, 0, 0)),
            ],
            scratch_shapes=[
                pltpu.VMEM((blocks_in_table, tile, width), jnp.bfloat16),
                pltpu.SemaphoreType.DMA((len(froms),)),
            ],
        ),
        out_shape=[
            jax.ShapeDtypeStruct((blocks_here * tile, width), jnp.float32),
            jax.ShapeDtypeStruct((blocks_here, tile, half), jnp.bfloat16),
            jax.ShapeDtypeStruct((blocks_here, tile, half), jnp.bfloat16),
        ],
        compiler_params=pltpu.CompilerParams(vmem_limit_bytes=VMEM_LIMIT),
        cost_estimate=pl.CostEstimate(
            flops=2 * LIGHT,
            bytes_accessed=blocks_here * per_block * tile * tile * 6 + blocks_in_table * tile * width * 2,
            transcendentals=0,
        ),
        name="early_sums",
    )(slots, late, counts, *froms, tile_masks)


def layer_kernel(slots, counts, *refs, many):
    *froms, more, sums, left, features, degree, weight, out = refs[:-11]
    table, extra, totals, masks, own, share, done, table_sems, extra_sems, in_sems, out_sems = refs[-11:]
    blocks_here, tile, across = masks.shape
    pair = across // tile
    width, out_width = table.shape[2], done.shape[1]
    chunks = blocks_here // many
    items = many * tile

    def table_copies():
        at = 0
        for n, piece in enumerate(froms):
            cut = table_sems.shape[1]
            size = piece.shape[0] // cut
            for c in range(cut):
                here = table.at[pl.ds(at + c * size, size)]
                yield pltpu.make_async_copy(piece.at[pl.ds(c * size, size)], here, table_sems.at[n, c])
            at += piece.shape[0]

    def chunk_copies(c):
        here, there = pl.ds(c * items, items), pl.ds(c * many, many)
        return [
            pltpu.make_async_copy(left.at[there], masks.at[there], in_sems.at[c, 0]),
            pltpu.make_async_copy(sums.at[here], totals.at[here], in_sems.at[c, 1]),
            pltpu.make_async_copy(features.at[here], own.at[here], in_sems.at[c, 2]),
        ]

    def fetch(row):
        return pltpu.make_async_copy(more.at[row], extra.at[row], extra_sems.at[row])

    def leave(c):
        here = pl.ds(c * items, items)
        return pltpu.make_async_copy(done.at[here], out.at[here], out_sems.at[c])

    for copy in table_copies():
        copy.start()
    for c in range(chunks):
        for copy in chunk_copies(c):
            copy.start()
        for row in range(c * many, (c + 1) * many):
            pl.when(counts[row] > pair)(fetch(row).start)

    column = lax.broadcasted_iota(jnp.int32, (tile, tile), 1)
    diagonal = lax.broadcasted_iota(jnp.int32, (tile, tile), 0) == column
    ones = jnp.ones((2 * tile, tile), jnp.bfloat16)
    for row in range(blocks_here):
        count = degree[row : row + 1, :]
        small = count & 7
        halves = [
            jnp.where(diagonal, part.astype(jnp.float32), 0.0).astype(jnp.bfloat16)
            for part in (count - small, small)
        ]
        spread = jnp.concatenate(halves, axis=1)
        share[row * tile : (row + 1) * tile, :] = 1.0 / jnp.dot(
            spread, ones, preferred_element_type=jnp.float32
        )

    for copy in table_copies():
        copy.wait()
    ones = jnp.ones((2 * out_width, tile), jnp.bfloat16)

    def chunk(c, carry):
        for copy in chunk_copies(c):
            copy.wait()

        def added(row, first, mask):
            picked = [table[slots[row * 2 * pair + t]] for t in range(first, first + pair)]
            return jnp.dot(mask, jnp.concatenate(picked, axis=0), preferred_element_type=jnp.float32)

        def rows_of(row):
            return pl.ds(pl.multiple_of(row * tile, tile), tile)

        for r in range(many):
            row = c * many + r
            totals[rows_of(row), :] += added(row, 0, masks[row])
        for r in range(many):
            row = c * many + r

            @pl.when(counts[row] > pair)
            def _():
                fetch(row).wait()
                totals[rows_of(row), :] += added(row, pair, extra[row])

        here = pl.ds(pl.multiple_of(c * items, items), items)
        part = jnp.concatenate([share[here, :]] * (width // tile), axis=1)
        mean = (totals[here, :] * part).astype(jnp.bfloat16)
        joined = jnp.concatenate([own[here, :], mean], axis=1)
        hidden = jnp.dot(joined, weight[...], preferred_element_type=jnp.float32)
        hidden = jnp.maximum(hidden, 0.0)
        squares = hidden * hidden
        high = squares.astype(jnp.bfloat16)
        low = (squares - high.astype(jnp.float32)).astype(jnp.bfloat16)
        total = jnp.dot(
            jnp.concatenate([high, low], axis=1), ones, preferred_element_type=jnp.float32
        )
        scale = jnp.concatenate([lax.rsqrt(total + 1e-06)] * (out_width // tile), axis=1)
        done[here, :] = (hidden * scale).astype(jnp.bfloat16)
        leave(c).start()
        return carry

    lax.fori_loop(0, chunks, chunk, 0)
    for c in range(chunks):
        leave(c).wait()


def layer(slots, counts, froms, sums, left, more, degree, features, weight):
    blocks_here, tile, across = left.shape
    items, width = features.shape
    out_width = weight.shape[1]
    many = 4 if blocks_here % 4 == 0 else 1
    chunks = blocks_here // many
    blocks_in_table = sum(piece.shape[0] for piece in froms)
    cut = 4 if froms[0].shape[0] % 4 == 0 else 1
    return pl.pallas_call(
        functools.partial(layer_kernel, many=many),
        grid_spec=pltpu.PrefetchScalarGridSpec(
            num_scalar_prefetch=2,
            grid=(1,),
            in_specs=[pl.BlockSpec(memory_space=pl.ANY)] * (len(froms) + 4)
            + [
                pl.BlockSpec((blocks_here, tile), lambda i, *_: (0, 0)),
                pl.BlockSpec((2 * width, out_width), lambda i, *_: (0, 0)),
            ],
            out_specs=pl.BlockSpec(memory_space=pl.ANY),
            scratch_shapes=[
                pltpu.VMEM((blocks_in_table, tile, width), jnp.bfloat16),
                pltpu.VMEM((blocks_here, tile, across), jnp.bfloat16),
                pltpu.VMEM((items, width), jnp.float32),
                pltpu.VMEM((blocks_here, tile, across), jnp.bfloat16),
                pltpu.VMEM((items, width), jnp.bfloat16),
                pltpu.VMEM((items, tile), jnp.float32),
                pltpu.VMEM((items, out_width), jnp.bfloat16),
                pltpu.SemaphoreType.DMA((len(froms), cut)),
                pltpu.SemaphoreType.DMA((blocks_here,)),
                pltpu.SemaphoreType.DMA((chunks, 3)),
                pltpu.SemaphoreType.DMA((chunks,)),
            ],
        ),
        out_shape=jax.ShapeDtypeStruct((items, out_width), jnp.bfloat16),
        compiler_params=pltpu.CompilerParams(vmem_limit_bytes=VMEM_LIMIT),
        cost_estimate=pl.CostEstimate(
            flops=2 * items * (across + 2 * width) * out_width,
            bytes_accessed=items * (4 * width + 2 * across + 2 * width + 2 * out_width),
            transcendentals=items,
        ),
        name="sage_layer",
    )(slots, counts, *froms, more, sums, left, features, degree, weight)


def on_device(features, tile_cols, tile_masks, degree, weight):
    blocks_here, per_block = tile_cols.shape
    tile = tile_masks.shape[2]
    width = features.shape[1]
    peers = lax.axis_size("rows")
    plane = peers // PLANES
    myself = lax.axis_index("rows")
    z, p = myself // plane, myself % plane
    end = (z == 0) | (z == PLANES - 1)
    capacity = max(2, (REM_PB * blocks_here + peers - 2) // (peers - 1))
    seats_all = plane * capacity
    local = features.reshape(blocks_here, tile, width)
    columns = tile_cols.reshape(-1)
    groups = [[a * plane + q for q in range(plane)] for a in range(PLANES)]

    def exchange(x):
        return lax.all_to_all(
            x, "rows", split_axis=0, concat_axis=0, axis_index_groups=groups, tiled=True
        )

    def shift(x, moves):
        pairs = [(a * plane + q, b * plane + q) for a, b in moves for q in range(plane)]
        return lax.ppermute(x, "rows", pairs)

    asked = exchange(jnp.broadcast_to(columns, (plane,) + columns.shape))
    down = [(a, a - 1) for a in range(1, PLANES)]
    up = [(a - 1, a) for a in range(1, PLANES)]
    from_above, from_below = shift(local, down), shift(local, up)

    rounds = jnp.array([[0, 0, 1, 2], [1, 2, 0, 3], [2, 3, 1, 0], [3, 3, 2, 1]], jnp.int32)
    line = jnp.append(pick_row(rounds, z), PLANES - 1 - z) * plane + p
    blocks = jnp.arange(blocks_here, dtype=jnp.int32)
    wanted = line[:, None] * blocks_here + blocks[None, :]
    below = blocks[:, None] > blocks[None, :]
    seat = jnp.arange(capacity, dtype=jnp.int32)

    def seated(asking, wanted):
        need = jnp.any(asking[:, None, :, None] == wanted[None, :, None, :], axis=2).astype(jnp.int32)
        place = jnp.sum(jnp.where(below, need[:, :, None, :], 0), axis=3)
        taken = (need[:, :, None, :] == 1) & (place[:, :, None, :] == seat[:, None])
        return jnp.sum(jnp.where(taken, blocks, 0), axis=3)

    near = jnp.swapaxes(seated(asked, wanted), 0, 1)

    owners, within = columns // blocks_here, columns % blocks_here
    positions = jnp.arange(columns.shape[0], dtype=jnp.int32)
    same = columns[:, None] == columns[None, :]
    repeated = jnp.any(same & (positions[None, :] < positions[:, None]), axis=1)
    ahead = (owners[:, None] == owners[None, :]) & (columns[None, :] < columns[:, None])
    ranks = jnp.sum(ahead & ~repeated[None, :], axis=1, dtype=jnp.int32)
    rounds_of = jnp.array([[0, 2, 3, 1], [2, 0, 1, 3], [3, 2, 0, 1], [1, 3, 2, 0]], jnp.int32)
    their_plane = owners // plane
    among = their_plane[:, None] == jnp.arange(PLANES)
    turn = jnp.sum(jnp.where(among, pick_row(rounds_of, z)[None, :], 0), axis=1)
    seats = (owners % plane) * capacity + ranks
    nothing = blocks_here + 3 * seats_all
    final = (turn == 3) | (end & (turn == 1))
    slots = jnp.where(final, nothing, blocks_here + turn * seats_all + seats)
    slots = jnp.where(owners == myself, within, slots)
    seats = jnp.where(turn == 3, seats + seats_all, seats)

    last = final.reshape(blocks_here, per_block)
    counts = jnp.sum(last, axis=1, dtype=jnp.int32)
    order_in = jnp.cumsum(last, axis=1) - 1
    spots = jnp.arange(REM_PB, dtype=jnp.int32)
    chair = last[:, None, :] & (order_in[:, None, :] == spots[:, None])
    late = jnp.sum(jnp.where(chair, jnp.arange(per_block, dtype=jnp.int32), 0), axis=2, dtype=jnp.int32)
    late_slots = jnp.sum(
        jnp.where(chair, seats.reshape(blocks_here, 1, per_block), 0), axis=2, dtype=jnp.int32
    )

    always = jnp.zeros((1,), jnp.int32)
    inner = (~end).astype(jnp.int32)[None]
    picked = choose(always, [near], [0], [local], LIGHT)
    got = [exchange(picked)]
    opposite, _ = lax.optimization_barrier((near[PLANES:], picked))
    across = shift(opposite, [(0, PLANES - 1), (PLANES - 1, 0)])
    across, _, _ = lax.optimization_barrier((across, from_above, from_below))
    picked = choose(inner, [across, near], [0, 1], [local, from_above], LIGHT)
    leaving, _ = lax.optimization_barrier((picked, got[0]))
    got.append(exchange(leaving))
    second_down = shift(from_above, down[:-1])
    second_up = shift(from_below, up[1:])
    leaving, _, _ = lax.optimization_barrier((got[1], second_down, second_up))
    crossed = shift(leaving, [(0, PLANES - 1), (PLANES - 1, 0)])
    near, _ = lax.optimization_barrier((near, picked))
    outer = (z > 0).astype(jnp.int32)[None]
    got.append(exchange(choose(outer, [near], [2], [from_above, from_below], HEAVY)))
    beyond = (z >= PLANES // 2).astype(jnp.int32)[None]
    got.append(exchange(choose(beyond, [near], [3], [second_down, second_up], LIGHT)))

    sums, left, more = early(slots, late.reshape(-1), counts, [local] + got[:3], tile_masks)
    return layer(
        late_slots.reshape(-1),
        counts,
        [crossed, got[3]],
        sums,
        left,
        more,
        degree.reshape(blocks_here, tile),
        features,
        weight,
    )


def solution(mesh):
    in_specs = (P("rows", None), P("rows", None), P("rows", None, None, None), P("rows"), P())
    out_specs = P("rows", None)
    return jax.shard_map(
        on_device, mesh=mesh, in_specs=in_specs, out_specs=out_specs, check_vma=False
    )
```

```python
import functools

import jax
import jax.numpy as jnp
from jax import lax
from jax.experimental import pallas as pl
from jax.experimental.pallas import tpu as pltpu
from jax.sharding import PartitionSpec as P

REM_PB = 4
PLANES = 4
HEAVY = 3 * 10**10
LIGHT = 10**10

VMEM_LIMIT = 62 * 1024 * 1024


def pick_row(table, z):
    return jnp.sum(jnp.where(jnp.arange(table.shape[0])[:, None] == z, table, 0), axis=0)


def choose_kernel(which, *refs, turns):
    lists, (*froms, out, held, in_sems, out_sems) = refs[: len(turns)], refs[len(turns) :]
    count, seats = out.shape[0], lists[0].shape[2]
    groups = in_sems.shape[0]
    size = count // groups
    for j, source in enumerate(froms):
        ids, turn = lists[j % len(turns)], turns[j % len(turns)]

        @pl.when(which[0] == j)
        def _():
            for n in range(count):
                block = source.at[ids[turn, n // seats, n % seats]]
                pltpu.make_async_copy(block, held.at[n], in_sems.at[n // size]).start()

    leaving = []
    for g in range(groups):
        here = pl.ds(g * size, size)
        pltpu.make_async_copy(out.at[here], held.at[here], in_sems.at[g]).wait()
        leaving.append(pltpu.make_async_copy(held.at[here], out.at[here], out_sems.at[g]))
        leaving[-1].start()
    for copy in leaving:
        copy.wait()


def choose(which, lists, turns, froms, flops):
    out = (lists[0].shape[1] * lists[0].shape[2],) + froms[0].shape[1:]
    moved = out[0] * out[1] * out[2] * 2
    groups = 4 if out[0] % 4 == 0 else 1
    return pl.pallas_call(
        functools.partial(choose_kernel, turns=turns),
        grid_spec=pltpu.PrefetchScalarGridSpec(
            num_scalar_prefetch=1 + len(lists),
            grid=(1,),
            in_specs=[pl.BlockSpec(memory_space=pltpu.HBM)] * len(froms),
            out_specs=pl.BlockSpec(memory_space=pltpu.HBM),
            scratch_shapes=[
                pltpu.VMEM(out, froms[0].dtype),
                pltpu.SemaphoreType.DMA((groups,)),
                pltpu.SemaphoreType.DMA((groups,)),
            ],
        ),
        out_shape=jax.ShapeDtypeStruct(out, froms[0].dtype),
        compiler_params=pltpu.CompilerParams(vmem_limit_bytes=VMEM_LIMIT),
        cost_estimate=pl.CostEstimate(flops=flops, bytes_accessed=2 * moved, transcendentals=0),
        name="choose_blocks",
    )(which, *lists, *froms)


def fill(pieces, table, sems):
    copies, at = [], 0
    for n, piece in enumerate(pieces):
        here = table.at[pl.ds(at, piece.shape[0])]
        copies.append(pltpu.make_async_copy(piece, here, sems.at[n]))
        at += piece.shape[0]
    for copy in copies:
        copy.start()
    return copies


def early_kernel(slots, late, counts, *refs):
    *froms, masks, sums, left, table, sems = refs
    step = pl.program_id(0)
    rows, per_block = masks.shape[:2]
    tile, width = table.shape[1:]
    spare = left.shape[2] // tile

    @pl.when(step == 0)
    def _():
        table[table.shape[0] - 1] = jnp.zeros((tile, width), table.dtype)
        for copy in fill(froms, table, sems):
            copy.wait()

    for r in range(rows):
        row = step * rows + r
        here = pl.ds(r * tile, tile)
        mask = jnp.concatenate(
            [masks[r, t].astype(jnp.float32).astype(jnp.bfloat16) for t in range(per_block)], axis=1
        )
        picked = jnp.concatenate(
            [table[slots[row * per_block + t]] for t in range(per_block)], axis=0
        )
        sums[here, :] = jnp.dot(mask, picked, preferred_element_type=jnp.float32)
        for t in range(spare):
            kept = jnp.where(t < counts[row], masks[r, late[row * spare + t]], 0)
            left[r, :, t * tile : (t + 1) * tile] = kept.astype(jnp.int8)


def early(slots, late, counts, froms, tile_masks):
    blocks_here, per_block, tile, _ = tile_masks.shape
    width = froms[0].shape[2]
    spare = late.shape[0] // blocks_here
    rows = 4 if blocks_here % 4 == 0 else 1
    blocks_in_table = sum(piece.shape[0] for piece in froms) + 1
    return pl.pallas_call(
        early_kernel,
        grid_spec=pltpu.PrefetchScalarGridSpec(
            num_scalar_prefetch=3,
            grid=(blocks_here // rows,),
            in_specs=[pl.BlockSpec(memory_space=pl.ANY)] * len(froms)
            + [pl.BlockSpec((rows, per_block, tile, tile), lambda r, *_: (r, 0, 0, 0))],
            out_specs=[
                pl.BlockSpec((rows * tile, width), lambda r, *_: (r, 0)),
                pl.BlockSpec((rows, tile, spare * tile), lambda r, *_: (r, 0, 0)),
            ],
            scratch_shapes=[
                pltpu.VMEM((blocks_in_table, tile, width), jnp.bfloat16),
                pltpu.SemaphoreType.DMA((len(froms),)),
            ],
        ),
        out_shape=[
            jax.ShapeDtypeStruct((blocks_here * tile, width), jnp.float32),
            jax.ShapeDtypeStruct((blocks_here, tile, spare * tile), jnp.int8),
        ],
        compiler_params=pltpu.CompilerParams(vmem_limit_bytes=VMEM_LIMIT),
        cost_estimate=pl.CostEstimate(
            flops=2 * LIGHT,
            bytes_accessed=blocks_here * per_block * tile * tile * 6 + blocks_in_table * tile * width * 2,
            transcendentals=0,
        ),
        name="early_sums",
    )(slots, late, counts, *froms, tile_masks)


def layer_kernel(slots, counts, *refs):
    *froms, sums, left, degree, features, weight, out, table, totals, share, sems = refs
    step = pl.program_id(0)
    rows, tile = left.shape[:2]
    width = table.shape[2]
    spare = left.shape[2] // tile
    pair = min(2, spare)

    @pl.when(step == 0)
    def _():
        copies = fill(froms, table, sems)
        column = lax.broadcasted_iota(jnp.int32, (tile, tile), 1)
        diagonal = lax.broadcasted_iota(jnp.int32, (tile, tile), 0) == column
        ones = jnp.ones((2 * tile, tile), jnp.bfloat16)
        for first in range(0, degree.shape[0], rows):
            spread = []
            for row in range(first, first + rows):
                count = degree[row : row + 1, :]
                small = count & 7
                halves = [
                    jnp.where(diagonal, part.astype(jnp.float32), 0.0).astype(jnp.bfloat16)
                    for part in (count - small, small)
                ]
                spread.append(jnp.concatenate(halves, axis=1))
            share[first * tile : (first + rows) * tile, :] = 1.0 / jnp.dot(
                jnp.concatenate(spread, axis=0), ones, preferred_element_type=jnp.float32
            )
        for copy in copies:
            copy.wait()


    def added(r, first):
        ends = min(first + pair, spare)
        picked = [table[slots[(step * rows + r) * spare + t]] for t in range(first, ends)]
        mask = left[r, :, first * tile : ends * tile].astype(jnp.int32)
        mask = mask.astype(jnp.float32).astype(jnp.bfloat16)
        return jnp.dot(mask, jnp.concatenate(picked, axis=0), preferred_element_type=jnp.float32)

    for r in range(rows):
        here = pl.ds(r * tile, tile)
        totals[here, :] = sums[here, :] + added(r, 0)
    for r in range(rows):
        here = pl.ds(r * tile, tile)
        for first in range(pair, spare, pair):

            @pl.when(counts[step * rows + r] > first)
            def _():
                totals[here, :] += added(r, first)

    many = min(rows, 4) * tile
    for first in range(0, rows * tile, many):
        here = pl.ds(first, many)
        there = pl.ds(pl.multiple_of(step * rows * tile + first, tile), many)
        part = jnp.concatenate([share[there, :]] * (width // tile), axis=1)
        mean = (totals[here, :] * part).astype(jnp.bfloat16)
        joined = jnp.concatenate([features[here, :], mean], axis=1)
        hidden = jnp.dot(joined, weight[...], preferred_element_type=jnp.float32)
        hidden = jnp.maximum(hidden, 0.0)
        scale = lax.rsqrt(jnp.sum(hidden * hidden, axis=1, keepdims=True) + 1e-06)
        out[here, :] = (hidden * scale).astype(jnp.bfloat16)


def layer(slots, counts, froms, sums, left, degree, features, weight):
    blocks_here, tile, across = left.shape
    width = features.shape[1]
    out_width = weight.shape[1]
    rows = 8 if blocks_here % 8 == 0 else 1
    items = rows * tile
    blocks_in_table = sum(piece.shape[0] for piece in froms)
    return pl.pallas_call(
        layer_kernel,
        grid_spec=pltpu.PrefetchScalarGridSpec(
            num_scalar_prefetch=2,
            grid=(blocks_here // rows,),
            in_specs=[pl.BlockSpec(memory_space=pl.ANY)] * len(froms)
            + [
                pl.BlockSpec((items, width), lambda r, *_: (r, 0)),
                pl.BlockSpec((rows, tile, across), lambda r, *_: (r, 0, 0)),
                pl.BlockSpec((blocks_here, tile), lambda r, *_: (0, 0)),
                pl.BlockSpec((items, width), lambda r, *_: (r, 0)),
                pl.BlockSpec((2 * width, out_width), lambda r, *_: (0, 0)),
            ],
            out_specs=pl.BlockSpec((items, out_width), lambda r, *_: (r, 0)),
            scratch_shapes=[
                pltpu.VMEM((blocks_in_table, tile, width), jnp.bfloat16),
                pltpu.VMEM((items, width), jnp.float32),
                pltpu.VMEM((blocks_here * tile, tile), jnp.float32),
                pltpu.SemaphoreType.DMA((len(froms),)),
            ],
        ),
        out_shape=jax.ShapeDtypeStruct((blocks_here * tile, out_width), jnp.bfloat16),
        compiler_params=pltpu.CompilerParams(vmem_limit_bytes=VMEM_LIMIT),
        cost_estimate=pl.CostEstimate(
            flops=2 * blocks_here * tile * (across + 2 * width) * out_width,
            bytes_accessed=blocks_here * tile * (4 * width + across + 2 * width + 2 * out_width),
            transcendentals=blocks_here * tile,
        ),
        name="sage_layer",
    )(slots, counts, *froms, sums, left, degree, features, weight)


def on_device(features, tile_cols, tile_masks, degree, weight):
    blocks_here, per_block = tile_cols.shape
    tile = tile_masks.shape[2]
    width = features.shape[1]
    peers = lax.axis_size("rows")
    plane = peers // PLANES
    myself = lax.axis_index("rows")
    z, p = myself // plane, myself % plane
    end = (z == 0) | (z == PLANES - 1)
    capacity = max(2, (REM_PB * blocks_here + peers - 2) // (peers - 1))
    seats_all = plane * capacity
    local = features.reshape(blocks_here, tile, width)
    columns = tile_cols.reshape(-1)
    groups = [[a * plane + q for q in range(plane)] for a in range(PLANES)]

    def exchange(x):
        return lax.all_to_all(
            x, "rows", split_axis=0, concat_axis=0, axis_index_groups=groups, tiled=True
        )

    def shift(x, moves):
        pairs = [(a * plane + q, b * plane + q) for a, b in moves for q in range(plane)]
        return lax.ppermute(x, "rows", pairs)

    asked = exchange(jnp.broadcast_to(columns, (plane,) + columns.shape))
    swap, outward, inward = [(1, 2), (2, 1)], [(1, 0), (2, 3)], [(0, 1), (3, 2)]
    beyond, near_out, near_in = shift(local, swap), shift(local, outward), shift(local, inward)

    rounds = jnp.array([[0, 0, 1, 2], [1, 2, 0, 3], [2, 1, 3, 0], [3, 3, 2, 1]], jnp.int32)
    line = jnp.append(pick_row(rounds, z), PLANES - 1 - z) * plane + p
    blocks = jnp.arange(blocks_here, dtype=jnp.int32)
    wanted = line[:, None] * blocks_here + blocks[None, :]
    below = blocks[:, None] > blocks[None, :]
    seat = jnp.arange(capacity, dtype=jnp.int32)

    def seated(asking, wanted):
        need = jnp.any(asking[:, None, :, None] == wanted[None, :, None, :], axis=2).astype(jnp.int32)
        place = jnp.sum(jnp.where(below, need[:, :, None, :], 0), axis=3)
        taken = (need[:, :, None, :] == 1) & (place[:, :, None, :] == seat[:, None])
        return jnp.sum(jnp.where(taken, blocks, 0), axis=3)

    near = jnp.swapaxes(seated(asked, wanted), 0, 1)

    owners, within = columns // blocks_here, columns % blocks_here
    positions = jnp.arange(columns.shape[0], dtype=jnp.int32)
    same = columns[:, None] == columns[None, :]
    repeated = jnp.any(same & (positions[None, :] < positions[:, None]), axis=1)
    ahead = (owners[:, None] == owners[None, :]) & (columns[None, :] < columns[:, None])
    ranks = jnp.sum(ahead & ~repeated[None, :], axis=1, dtype=jnp.int32)
    rounds_of = jnp.array([[0, 2, 3, 1], [2, 0, 1, 3], [3, 1, 0, 2], [1, 3, 2, 0]], jnp.int32)
    their_plane = owners // plane
    among = their_plane[:, None] == jnp.arange(PLANES)
    turn = jnp.sum(jnp.where(among, pick_row(rounds_of, z)[None, :], 0), axis=1)
    seats = (owners % plane) * capacity + ranks
    nothing = blocks_here + 3 * seats_all
    final = (turn == 3) | (end & (turn == 1))
    slots = jnp.where(final, nothing, blocks_here + turn * seats_all + seats)
    slots = jnp.where(owners == myself, within, slots)
    seats = jnp.where(turn == 3, seats + seats_all, seats)

    last = final.reshape(blocks_here, per_block)
    counts = jnp.sum(last, axis=1, dtype=jnp.int32)
    order_in = jnp.cumsum(last, axis=1) - 1
    spots = jnp.arange(REM_PB, dtype=jnp.int32)
    chair = last[:, None, :] & (order_in[:, None, :] == spots[:, None])
    late = jnp.sum(jnp.where(chair, jnp.arange(per_block, dtype=jnp.int32), 0), axis=2, dtype=jnp.int32)
    late_slots = jnp.sum(
        jnp.where(chair, seats.reshape(blocks_here, 1, per_block), 0), axis=2, dtype=jnp.int32
    )

    always = jnp.zeros((1,), jnp.int32)
    inner = (~end).astype(jnp.int32)[None]
    picked = choose(always, [near], [0], [local], LIGHT)
    got = [exchange(picked)]
    opposite, _ = lax.optimization_barrier((near[PLANES:], picked))
    across = shift(opposite, [(0, PLANES - 1), (PLANES - 1, 0)])
    across, _, _, _ = lax.optimization_barrier((across, beyond, near_out, near_in))
    picked = choose(inner, [across, near], [0, 1], [local, beyond], LIGHT)
    leaving, _ = lax.optimization_barrier((picked, got[0]))
    got.append(exchange(leaving))
    far_out, far_in = shift(beyond, outward), shift(near_in, swap)
    leaving, _, _ = lax.optimization_barrier((got[1], far_out, far_in))
    crossed = shift(leaving, [(0, PLANES - 1), (PLANES - 1, 0)])
    near, _ = lax.optimization_barrier((near, picked))
    got.append(exchange(choose(inner, [near], [2], [near_out, near_in], HEAVY)))
    got.append(exchange(choose(inner, [near], [3], [far_out, far_in], LIGHT)))

    sums, left = early(slots, late.reshape(-1), counts, [local] + got[:3], tile_masks)
    return layer(
        late_slots.reshape(-1),
        counts,
        [crossed, got[3]],
        sums,
        left,
        degree.reshape(blocks_here, tile),
        features,
        weight,
    )


def solution(mesh):
    in_specs = (P("rows", None), P("rows", None), P("rows", None, None, None), P("rows"), P())
    out_specs = P("rows", None)
    return jax.shard_map(
        on_device, mesh=mesh, in_specs=in_specs, out_specs=out_specs, check_vma=False
    )
```

```python
import functools

import jax
import jax.numpy as jnp
from jax import lax
from jax.experimental import pallas as pl
from jax.experimental.pallas import tpu as pltpu
from jax.sharding import PartitionSpec as P

REM_PB = 4
PLANES = 4
HEAVY = 3 * 10**10
LIGHT = 10**10

VMEM_LIMIT = 62 * 1024 * 1024


def pick_row(table, z):
    return jnp.sum(jnp.where(jnp.arange(table.shape[0])[:, None] == z, table, 0), axis=0)


def choose_kernel(which, *refs, turns):
    lists, (*froms, out, held, in_sems, out_sems) = refs[: len(turns)], refs[len(turns) :]
    count, seats = out.shape[0], lists[0].shape[2]
    groups = in_sems.shape[0]
    size = count // groups
    for j, source in enumerate(froms):
        ids, turn = lists[j % len(turns)], turns[j % len(turns)]

        @pl.when(which[0] == j)
        def _():
            for n in range(count):
                block = source.at[ids[turn, n // seats, n % seats]]
                pltpu.make_async_copy(block, held.at[n], in_sems.at[n // size]).start()

    leaving = []
    for g in range(groups):
        here = pl.ds(g * size, size)
        pltpu.make_async_copy(out.at[here], held.at[here], in_sems.at[g]).wait()
        leaving.append(pltpu.make_async_copy(held.at[here], out.at[here], out_sems.at[g]))
        leaving[-1].start()
    for copy in leaving:
        copy.wait()


def choose(which, lists, turns, froms, flops):
    out = (lists[0].shape[1] * lists[0].shape[2],) + froms[0].shape[1:]
    moved = out[0] * out[1] * out[2] * 2
    groups = 4 if out[0] % 4 == 0 else 1
    return pl.pallas_call(
        functools.partial(choose_kernel, turns=turns),
        grid_spec=pltpu.PrefetchScalarGridSpec(
            num_scalar_prefetch=1 + len(lists),
            grid=(1,),
            in_specs=[pl.BlockSpec(memory_space=pltpu.HBM)] * len(froms),
            out_specs=pl.BlockSpec(memory_space=pltpu.HBM),
            scratch_shapes=[
                pltpu.VMEM(out, froms[0].dtype),
                pltpu.SemaphoreType.DMA((groups,)),
                pltpu.SemaphoreType.DMA((groups,)),
            ],
        ),
        out_shape=jax.ShapeDtypeStruct(out, froms[0].dtype),
        compiler_params=pltpu.CompilerParams(vmem_limit_bytes=VMEM_LIMIT),
        cost_estimate=pl.CostEstimate(flops=flops, bytes_accessed=2 * moved, transcendentals=0),
        name="choose_blocks",
    )(which, *lists, *froms)


def fill(pieces, table, sems):
    copies, at = [], 0
    for n, piece in enumerate(pieces):
        here = table.at[pl.ds(at, piece.shape[0])]
        copies.append(pltpu.make_async_copy(piece, here, sems.at[n]))
        at += piece.shape[0]
    for copy in copies:
        copy.start()
    return copies


def early_kernel(slots, late, counts, *refs):
    *froms, masks, sums, left, table, sems = refs
    step = pl.program_id(0)
    rows, per_block = masks.shape[:2]
    tile, width = table.shape[1:]
    spare = left.shape[2] // tile

    @pl.when(step == 0)
    def _():
        table[table.shape[0] - 1] = jnp.zeros((tile, width), table.dtype)
        for copy in fill(froms, table, sems):
            copy.wait()

    for r in range(rows):
        row = step * rows + r
        here = pl.ds(r * tile, tile)
        mask = jnp.concatenate(
            [masks[r, t].astype(jnp.float32).astype(jnp.bfloat16) for t in range(per_block)], axis=1
        )
        picked = jnp.concatenate(
            [table[slots[row * per_block + t]] for t in range(per_block)], axis=0
        )
        sums[here, :] = jnp.dot(mask, picked, preferred_element_type=jnp.float32)
        for t in range(spare):
            kept = jnp.where(t < counts[row], masks[r, late[row * spare + t]], 0)
            left[r, :, t * tile : (t + 1) * tile] = kept.astype(jnp.int8)


def early(slots, late, counts, froms, tile_masks):
    blocks_here, per_block, tile, _ = tile_masks.shape
    width = froms[0].shape[2]
    spare = late.shape[0] // blocks_here
    rows = 4 if blocks_here % 4 == 0 else 1
    blocks_in_table = sum(piece.shape[0] for piece in froms) + 1
    return pl.pallas_call(
        early_kernel,
        grid_spec=pltpu.PrefetchScalarGridSpec(
            num_scalar_prefetch=3,
            grid=(blocks_here // rows,),
            in_specs=[pl.BlockSpec(memory_space=pl.ANY)] * len(froms)
            + [pl.BlockSpec((rows, per_block, tile, tile), lambda r, *_: (r, 0, 0, 0))],
            out_specs=[
                pl.BlockSpec((rows * tile, width), lambda r, *_: (r, 0)),
                pl.BlockSpec((rows, tile, spare * tile), lambda r, *_: (r, 0, 0)),
            ],
            scratch_shapes=[
                pltpu.VMEM((blocks_in_table, tile, width), jnp.bfloat16),
                pltpu.SemaphoreType.DMA((len(froms),)),
            ],
        ),
        out_shape=[
            jax.ShapeDtypeStruct((blocks_here * tile, width), jnp.float32),
            jax.ShapeDtypeStruct((blocks_here, tile, spare * tile), jnp.int8),
        ],
        compiler_params=pltpu.CompilerParams(vmem_limit_bytes=VMEM_LIMIT),
        cost_estimate=pl.CostEstimate(
            flops=2 * LIGHT,
            bytes_accessed=blocks_here * per_block * tile * tile * 6 + blocks_in_table * tile * width * 2,
            transcendentals=0,
        ),
        name="early_sums",
    )(slots, late, counts, *froms, tile_masks)


def layer_kernel(slots, counts, *refs):
    *froms, sums, left, degree, features, weight, out, table, totals, share, sems = refs
    step = pl.program_id(0)
    rows, tile = left.shape[:2]
    width = table.shape[2]
    spare = left.shape[2] // tile
    pair = min(2, spare)

    @pl.when(step == 0)
    def _():
        copies = fill(froms, table, sems)
        column = lax.broadcasted_iota(jnp.int32, (tile, tile), 1)
        diagonal = lax.broadcasted_iota(jnp.int32, (tile, tile), 0) == column
        ones = jnp.ones((2 * tile, tile), jnp.bfloat16)
        for first in range(0, degree.shape[0], rows):
            spread = []
            for row in range(first, first + rows):
                count = degree[row : row + 1, :]
                small = count & 7
                halves = [
                    jnp.where(diagonal, part.astype(jnp.float32), 0.0).astype(jnp.bfloat16)
                    for part in (count - small, small)
                ]
                spread.append(jnp.concatenate(halves, axis=1))
            share[first * tile : (first + rows) * tile, :] = 1.0 / jnp.dot(
                jnp.concatenate(spread, axis=0), ones, preferred_element_type=jnp.float32
            )
        for copy in copies:
            copy.wait()


    def added(r, first):
        ends = min(first + pair, spare)
        picked = [table[slots[(step * rows + r) * spare + t]] for t in range(first, ends)]
        mask = left[r, :, first * tile : ends * tile].astype(jnp.int32)
        mask = mask.astype(jnp.float32).astype(jnp.bfloat16)
        return jnp.dot(mask, jnp.concatenate(picked, axis=0), preferred_element_type=jnp.float32)

    for r in range(rows):
        here = pl.ds(r * tile, tile)
        totals[here, :] = sums[here, :] + added(r, 0)
    for r in range(rows):
        here = pl.ds(r * tile, tile)
        for first in range(pair, spare, pair):

            @pl.when(counts[step * rows + r] > first)
            def _():
                totals[here, :] += added(r, first)

    many = min(rows, 4) * tile
    for first in range(0, rows * tile, many):
        here = pl.ds(first, many)
        there = pl.ds(pl.multiple_of(step * rows * tile + first, tile), many)
        part = jnp.concatenate([share[there, :]] * (width // tile), axis=1)
        mean = (totals[here, :] * part).astype(jnp.bfloat16)
        joined = jnp.concatenate([features[here, :], mean], axis=1)
        hidden = jnp.dot(joined, weight[...], preferred_element_type=jnp.float32)
        hidden = jnp.maximum(hidden, 0.0)
        scale = lax.rsqrt(jnp.sum(hidden * hidden, axis=1, keepdims=True) + 1e-06)
        out[here, :] = (hidden * scale).astype(jnp.bfloat16)


def layer(slots, counts, froms, sums, left, degree, features, weight):
    blocks_here, tile, across = left.shape
    width = features.shape[1]
    out_width = weight.shape[1]
    rows = 8 if blocks_here % 8 == 0 else 1
    items = rows * tile
    blocks_in_table = sum(piece.shape[0] for piece in froms)
    return pl.pallas_call(
        layer_kernel,
        grid_spec=pltpu.PrefetchScalarGridSpec(
            num_scalar_prefetch=2,
            grid=(blocks_here // rows,),
            in_specs=[pl.BlockSpec(memory_space=pl.ANY)] * len(froms)
            + [
                pl.BlockSpec((items, width), lambda r, *_: (r, 0)),
                pl.BlockSpec((rows, tile, across), lambda r, *_: (r, 0, 0)),
                pl.BlockSpec((blocks_here, tile), lambda r, *_: (0, 0)),
                pl.BlockSpec((items, width), lambda r, *_: (r, 0)),
                pl.BlockSpec((2 * width, out_width), lambda r, *_: (0, 0)),
            ],
            out_specs=pl.BlockSpec((items, out_width), lambda r, *_: (r, 0)),
            scratch_shapes=[
                pltpu.VMEM((blocks_in_table, tile, width), jnp.bfloat16),
                pltpu.VMEM((items, width), jnp.float32),
                pltpu.VMEM((blocks_here * tile, tile), jnp.float32),
                pltpu.SemaphoreType.DMA((len(froms),)),
            ],
        ),
        out_shape=jax.ShapeDtypeStruct((blocks_here * tile, out_width), jnp.bfloat16),
        compiler_params=pltpu.CompilerParams(vmem_limit_bytes=VMEM_LIMIT),
        cost_estimate=pl.CostEstimate(
            flops=2 * blocks_here * tile * (across + 2 * width) * out_width,
            bytes_accessed=blocks_here * tile * (4 * width + across + 2 * width + 2 * out_width),
            transcendentals=blocks_here * tile,
        ),
        name="sage_layer",
    )(slots, counts, *froms, sums, left, degree, features, weight)


def on_device(features, tile_cols, tile_masks, degree, weight):
    blocks_here, per_block = tile_cols.shape
    tile = tile_masks.shape[2]
    width = features.shape[1]
    peers = lax.axis_size("rows")
    plane = peers // PLANES
    myself = lax.axis_index("rows")
    z, p = myself // plane, myself % plane
    end = (z == 0) | (z == PLANES - 1)
    capacity = max(2, (REM_PB * blocks_here + peers - 2) // (peers - 1))
    seats_all = plane * capacity
    local = features.reshape(blocks_here, tile, width)
    columns = tile_cols.reshape(-1)
    groups = [[a * plane + q for q in range(plane)] for a in range(PLANES)]

    def exchange(x):
        return lax.all_to_all(
            x, "rows", split_axis=0, concat_axis=0, axis_index_groups=groups, tiled=True
        )

    def shift(x, moves):
        pairs = [(a * plane + q, b * plane + q) for a, b in moves for q in range(plane)]
        return lax.ppermute(x, "rows", pairs)

    asked = exchange(jnp.broadcast_to(columns, (plane,) + columns.shape))
    swap, outward, beside = [(1, 2), (2, 1)], [(1, 0), (2, 3)], [(0, 1), (1, 0), (2, 3), (3, 2)]
    near_by, beyond = shift(local, beside), shift(local, swap)

    rounds = jnp.array([[0, 0, 1, 2], [1, 2, 0, 3], [2, 1, 3, 0], [3, 3, 2, 1]], jnp.int32)
    line = jnp.append(pick_row(rounds, z), PLANES - 1 - z) * plane + p
    blocks = jnp.arange(blocks_here, dtype=jnp.int32)
    wanted = line[:, None] * blocks_here + blocks[None, :]
    below = blocks[:, None] > blocks[None, :]
    seat = jnp.arange(capacity, dtype=jnp.int32)

    def seated(asking, wanted):
        need = jnp.any(asking[:, None, :, None] == wanted[None, :, None, :], axis=2).astype(jnp.int32)
        place = jnp.sum(jnp.where(below, need[:, :, None, :], 0), axis=3)
        taken = (need[:, :, None, :] == 1) & (place[:, :, None, :] == seat[:, None])
        return jnp.sum(jnp.where(taken, blocks, 0), axis=3)

    near = jnp.swapaxes(seated(asked, wanted), 0, 1)

    owners, within = columns // blocks_here, columns % blocks_here
    positions = jnp.arange(columns.shape[0], dtype=jnp.int32)
    same = columns[:, None] == columns[None, :]
    repeated = jnp.any(same & (positions[None, :] < positions[:, None]), axis=1)
    ahead = (owners[:, None] == owners[None, :]) & (columns[None, :] < columns[:, None])
    ranks = jnp.sum(ahead & ~repeated[None, :], axis=1, dtype=jnp.int32)
    rounds_of = jnp.array([[0, 2, 3, 1], [2, 0, 1, 3], [3, 1, 0, 2], [1, 3, 2, 0]], jnp.int32)
    their_plane = owners // plane
    among = their_plane[:, None] == jnp.arange(PLANES)
    turn = jnp.sum(jnp.where(among, pick_row(rounds_of, z)[None, :], 0), axis=1)
    seats = (owners % plane) * capacity + ranks
    nothing = blocks_here + 3 * seats_all
    final = (turn == 3) | (end & (turn == 1))
    slots = jnp.where(final, nothing, blocks_here + turn * seats_all + seats)
    slots = jnp.where(owners == myself, within, slots)
    seats = jnp.where(turn == 3, seats + seats_all, seats)

    last = final.reshape(blocks_here, per_block)
    counts = jnp.sum(last, axis=1, dtype=jnp.int32)
    order_in = jnp.cumsum(last, axis=1) - 1
    spots = jnp.arange(REM_PB, dtype=jnp.int32)
    chair = last[:, None, :] & (order_in[:, None, :] == spots[:, None])
    late = jnp.sum(jnp.where(chair, jnp.arange(per_block, dtype=jnp.int32), 0), axis=2, dtype=jnp.int32)
    late_slots = jnp.sum(
        jnp.where(chair, seats.reshape(blocks_here, 1, per_block), 0), axis=2, dtype=jnp.int32
    )

    always = jnp.zeros((1,), jnp.int32)
    inner = (~end).astype(jnp.int32)[None]
    picked = choose(always, [near], [0], [local], LIGHT)
    got = [exchange(picked)]
    opposite, _ = lax.optimization_barrier((near[PLANES:], picked))
    across = shift(opposite, [(0, PLANES - 1), (PLANES - 1, 0)])
    across, _, _ = lax.optimization_barrier((across, beyond, near_by))
    picked = choose(inner, [across, near], [0, 1], [local, beyond], LIGHT)
    leaving, _ = lax.optimization_barrier((picked, got[0]))
    got.append(exchange(leaving))
    far_out, far_in = shift(beyond, outward), shift(near_by, swap)
    leaving, _, _ = lax.optimization_barrier((got[1], far_out, far_in))
    crossed = shift(leaving, [(0, PLANES - 1), (PLANES - 1, 0)])
    near, _ = lax.optimization_barrier((near, picked))
    got.append(exchange(choose(always, [near], [2], [near_by], HEAVY)))
    got.append(exchange(choose(inner, [near], [3], [far_out, far_in], LIGHT)))

    sums, left = early(slots, late.reshape(-1), counts, [local] + got[:3], tile_masks)
    return layer(
        late_slots.reshape(-1),
        counts,
        [crossed, got[3]],
        sums,
        left,
        degree.reshape(blocks_here, tile),
        features,
        weight,
    )


def solution(mesh):
    in_specs = (P("rows", None), P("rows", None), P("rows", None, None, None), P("rows"), P())
    out_specs = P("rows", None)
    return jax.shard_map(
        on_device, mesh=mesh, in_specs=in_specs, out_specs=out_specs, check_vma=False
    )
```

```python
import functools

import jax
import jax.numpy as jnp
from jax import lax
from jax.experimental import pallas as pl
from jax.experimental.pallas import tpu as pltpu
from jax.sharding import PartitionSpec as P

REM_PB = 4
PLANES = 4
HEAVY = 3 * 10**10
LIGHT = 10**10
CUT = 4

VMEM_LIMIT = 62 * 1024 * 1024


def pick_row(table, z):
    return jnp.sum(jnp.where(jnp.arange(table.shape[0])[:, None] == z, table, 0), axis=0)


def choose_kernel(which, *refs, turns):
    lists, (*froms, out, held, in_sems, out_sems) = refs[: len(turns)], refs[len(turns) :]
    count, seats = out.shape[0], lists[0].shape[2]
    groups = in_sems.shape[0]
    size = count // groups
    for j, source in enumerate(froms):
        ids, turn = lists[j % len(turns)], turns[j % len(turns)]

        @pl.when(which[0] == j)
        def _():
            for n in range(count):
                block = source.at[ids[turn, n // seats, n % seats]]
                pltpu.make_async_copy(block, held.at[n], in_sems.at[n // size]).start()

    leaving = []
    for g in range(groups):
        here = pl.ds(g * size, size)
        pltpu.make_async_copy(out.at[here], held.at[here], in_sems.at[g]).wait()
        leaving.append(pltpu.make_async_copy(held.at[here], out.at[here], out_sems.at[g]))
        leaving[-1].start()
    for copy in leaving:
        copy.wait()


def choose(which, lists, turns, froms, flops):
    out = (lists[0].shape[1] * lists[0].shape[2],) + froms[0].shape[1:]
    moved = out[0] * out[1] * out[2] * 2
    groups = 4 if out[0] % 4 == 0 else 1
    return pl.pallas_call(
        functools.partial(choose_kernel, turns=turns),
        grid_spec=pltpu.PrefetchScalarGridSpec(
            num_scalar_prefetch=1 + len(lists),
            grid=(1,),
            in_specs=[pl.BlockSpec(memory_space=pltpu.HBM)] * len(froms),
            out_specs=pl.BlockSpec(memory_space=pltpu.HBM),
            scratch_shapes=[
                pltpu.VMEM(out, froms[0].dtype),
                pltpu.SemaphoreType.DMA((groups,)),
                pltpu.SemaphoreType.DMA((groups,)),
            ],
        ),
        out_shape=jax.ShapeDtypeStruct(out, froms[0].dtype),
        compiler_params=pltpu.CompilerParams(vmem_limit_bytes=VMEM_LIMIT),
        cost_estimate=pl.CostEstimate(flops=flops, bytes_accessed=2 * moved, transcendentals=0),
        name="choose_blocks",
    )(which, *lists, *froms)


def fill(pieces, table, sems, at=0):
    copies, cut = [], sems.shape[1]
    for n, piece in enumerate(pieces):
        size = piece.shape[0] // cut
        for c in range(cut):
            here = table.at[pl.ds(at + c * size, size)]
            copies.append(pltpu.make_async_copy(piece.at[pl.ds(c * size, size)], here, sems.at[n, c]))
        at += piece.shape[0]
    for copy in copies:
        copy.start()
    return copies


def early_kernel(slots, late, counts, *refs):
    *froms, masks, sums, left, table, sems = refs
    step = pl.program_id(0)
    rows, per_block = masks.shape[:2]
    tile, width = table.shape[1:]
    spare = left.shape[2] // tile

    @pl.when(step == 0)
    def _():
        table[table.shape[0] - 1] = jnp.zeros((tile, width), table.dtype)
        for copy in fill(froms, table, sems):
            copy.wait()

    for r in range(rows):
        row = step * rows + r
        here = pl.ds(r * tile, tile)
        mask = jnp.concatenate(
            [masks[r, t].astype(jnp.float32).astype(jnp.bfloat16) for t in range(per_block)], axis=1
        )
        picked = jnp.concatenate(
            [table[slots[row * per_block + t]] for t in range(per_block)], axis=0
        )
        sums[here, :] = jnp.dot(mask, picked, preferred_element_type=jnp.float32)
        for t in range(spare):
            kept = jnp.where(t < counts[row], masks[r, late[row * spare + t]], 0)
            left[r, :, t * tile : (t + 1) * tile] = kept.astype(jnp.int8)


def early(slots, late, counts, froms, tile_masks):
    blocks_here, per_block, tile, _ = tile_masks.shape
    width = froms[0].shape[2]
    spare = late.shape[0] // blocks_here
    rows = 4 if blocks_here % 4 == 0 else 1
    blocks_in_table = sum(piece.shape[0] for piece in froms) + 1
    return pl.pallas_call(
        early_kernel,
        grid_spec=pltpu.PrefetchScalarGridSpec(
            num_scalar_prefetch=3,
            grid=(blocks_here // rows,),
            in_specs=[pl.BlockSpec(memory_space=pl.ANY)] * len(froms)
            + [pl.BlockSpec((rows, per_block, tile, tile), lambda r, *_: (r, 0, 0, 0))],
            out_specs=[
                pl.BlockSpec((rows * tile, width), lambda r, *_: (r, 0)),
                pl.BlockSpec((rows, tile, spare * tile), lambda r, *_: (r, 0, 0)),
            ],
            scratch_shapes=[
                pltpu.VMEM((blocks_in_table, tile, width), jnp.bfloat16),
                pltpu.SemaphoreType.DMA((len(froms), CUT)),
            ],
        ),
        out_shape=[
            jax.ShapeDtypeStruct((blocks_here * tile, width), jnp.float32),
            jax.ShapeDtypeStruct((blocks_here, tile, spare * tile), jnp.int8),
        ],
        compiler_params=pltpu.CompilerParams(vmem_limit_bytes=VMEM_LIMIT),
        cost_estimate=pl.CostEstimate(
            flops=2 * LIGHT,
            bytes_accessed=blocks_here * per_block * tile * tile * 6 + blocks_in_table * tile * width * 2,
            transcendentals=0,
        ),
        name="early_sums",
    )(slots, late, counts, *froms, tile_masks)


def layer_kernel(slots, counts, end, crossed, last, *refs):
    sums, left, degree, features, weight, out, table, totals, share, sems, far_sems = refs
    step = pl.program_id(0)
    rows, tile = left.shape[:2]
    width = table.shape[2]
    spare = left.shape[2] // tile
    pair = min(2, spare)

    @pl.when(step == 0)
    def _():
        size = crossed.shape[0]
        copies = fill([last], table, sems, size)

        @pl.when(end[0] == 1)
        def _():
            fill([crossed], table, far_sems)

        @pl.when(end[0] == 0)
        def _():
            table[0] = jnp.zeros((tile, width), table.dtype)

        column = lax.broadcasted_iota(jnp.int32, (tile, tile), 1)
        diagonal = lax.broadcasted_iota(jnp.int32, (tile, tile), 0) == column
        ones = jnp.ones((2 * tile, tile), jnp.bfloat16)
        for first in range(0, degree.shape[0], rows):
            spread = []
            for row in range(first, first + rows):
                count = degree[row : row + 1, :]
                small = count & 7
                halves = [
                    jnp.where(diagonal, part.astype(jnp.float32), 0.0).astype(jnp.bfloat16)
                    for part in (count - small, small)
                ]
                spread.append(jnp.concatenate(halves, axis=1))
            share[first * tile : (first + rows) * tile, :] = 1.0 / jnp.dot(
                jnp.concatenate(spread, axis=0), ones, preferred_element_type=jnp.float32
            )
        for copy in copies:
            copy.wait()

        @pl.when(end[0] == 1)
        def _():
            for c in range(CUT):
                here = pl.ds(c * (size // CUT), size // CUT)
                pltpu.make_async_copy(crossed.at[here], table.at[here], far_sems.at[0, c]).wait()

    def added(r, first):
        ends = min(first + pair, spare)
        picked = [table[slots[(step * rows + r) * spare + t]] for t in range(first, ends)]
        mask = left[r, :, first * tile : ends * tile].astype(jnp.int32)
        mask = mask.astype(jnp.float32).astype(jnp.bfloat16)
        return jnp.dot(mask, jnp.concatenate(picked, axis=0), preferred_element_type=jnp.float32)

    for r in range(rows):
        here = pl.ds(r * tile, tile)
        totals[here, :] = sums[here, :] + added(r, 0)
    for r in range(rows):
        here = pl.ds(r * tile, tile)
        for first in range(pair, spare, pair):

            @pl.when(counts[step * rows + r] > first)
            def _():
                totals[here, :] += added(r, first)

    many = rows * tile
    for first in range(0, rows * tile, many):
        here = pl.ds(first, many)
        there = pl.ds(pl.multiple_of(step * rows * tile + first, tile), many)
        part = jnp.concatenate([share[there, :]] * (width // tile), axis=1)
        mean = (totals[here, :] * part).astype(jnp.bfloat16)
        joined = jnp.concatenate([features[here, :], mean], axis=1)
        hidden = jnp.dot(joined, weight[...], preferred_element_type=jnp.float32)
        hidden = jnp.maximum(hidden, 0.0)
        scale = lax.rsqrt(jnp.sum(hidden * hidden, axis=1, keepdims=True) + 1e-06)
        out[here, :] = (hidden * scale).astype(jnp.bfloat16)


def layer(slots, counts, end, froms, sums, left, degree, features, weight):
    blocks_here, tile, across = left.shape
    width = features.shape[1]
    out_width = weight.shape[1]
    rows = 8 if blocks_here % 8 == 0 else 1
    items = rows * tile
    blocks_in_table = sum(piece.shape[0] for piece in froms)
    return pl.pallas_call(
        layer_kernel,
        grid_spec=pltpu.PrefetchScalarGridSpec(
            num_scalar_prefetch=3,
            grid=(blocks_here // rows,),
            in_specs=[pl.BlockSpec(memory_space=pl.ANY)] * len(froms)
            + [
                pl.BlockSpec((items, width), lambda r, *_: (r, 0)),
                pl.BlockSpec((rows, tile, across), lambda r, *_: (r, 0, 0)),
                pl.BlockSpec((blocks_here, tile), lambda r, *_: (0, 0)),
                pl.BlockSpec((items, width), lambda r, *_: (r, 0)),
                pl.BlockSpec((2 * width, out_width), lambda r, *_: (0, 0)),
            ],
            out_specs=pl.BlockSpec((items, out_width), lambda r, *_: (r, 0)),
            scratch_shapes=[
                pltpu.VMEM((blocks_in_table, tile, width), jnp.bfloat16),
                pltpu.VMEM((items, width), jnp.float32),
                pltpu.VMEM((blocks_here * tile, tile), jnp.float32),
                pltpu.SemaphoreType.DMA((1, CUT)),
                pltpu.SemaphoreType.DMA((1, CUT)),
            ],
        ),
        out_shape=jax.ShapeDtypeStruct((blocks_here * tile, out_width), jnp.bfloat16),
        compiler_params=pltpu.CompilerParams(vmem_limit_bytes=VMEM_LIMIT),
        cost_estimate=pl.CostEstimate(
            flops=2 * blocks_here * tile * (across + 2 * width) * out_width,
            bytes_accessed=blocks_here * tile * (4 * width + across + 2 * width + 2 * out_width),
            transcendentals=blocks_here * tile,
        ),
        name="sage_layer",
    )(slots, counts, end, *froms, sums, left, degree, features, weight)


def on_device(features, tile_cols, tile_masks, degree, weight):
    blocks_here, per_block = tile_cols.shape
    tile = tile_masks.shape[2]
    width = features.shape[1]
    peers = lax.axis_size("rows")
    plane = peers // PLANES
    myself = lax.axis_index("rows")
    z, p = myself // plane, myself % plane
    end = (z == 0) | (z == PLANES - 1)
    capacity = max(2, (REM_PB * blocks_here + peers - 2) // (peers - 1))
    seats_all = plane * capacity
    local = features.reshape(blocks_here, tile, width)
    columns = tile_cols.reshape(-1)
    groups = [[a * plane + q for q in range(plane)] for a in range(PLANES)]

    def exchange(x):
        return lax.all_to_all(
            x, "rows", split_axis=0, concat_axis=0, axis_index_groups=groups, tiled=True
        )

    def shift(x, moves):
        pairs = [(a * plane + q, b * plane + q) for a, b in moves for q in range(plane)]
        return lax.ppermute(x, "rows", pairs)

    asked = exchange(jnp.broadcast_to(columns, (plane,) + columns.shape))
    swap, outward, beside = [(1, 2), (2, 1)], [(1, 0), (2, 3)], [(0, 1), (1, 0), (2, 3), (3, 2)]
    near_by, beyond = shift(local, beside), shift(local, swap)

    rounds = jnp.array([[0, 0, 1, 2], [1, 2, 0, 3], [2, 1, 3, 0], [3, 3, 2, 1]], jnp.int32)
    line = jnp.append(pick_row(rounds, z), PLANES - 1 - z) * plane + p
    blocks = jnp.arange(blocks_here, dtype=jnp.int32)
    wanted = line[:, None] * blocks_here + blocks[None, :]
    below = blocks[:, None] > blocks[None, :]
    seat = jnp.arange(capacity, dtype=jnp.int32)

    def seated(asking, wanted):
        need = jnp.any(asking[:, None, :, None] == wanted[None, :, None, :], axis=2).astype(jnp.int32)
        place = jnp.sum(jnp.where(below, need[:, :, None, :], 0), axis=3)
        taken = (need[:, :, None, :] == 1) & (place[:, :, None, :] == seat[:, None])
        return jnp.sum(jnp.where(taken, blocks, 0), axis=3)

    near = jnp.swapaxes(seated(asked, wanted), 0, 1)

    owners, within = columns // blocks_here, columns % blocks_here
    positions = jnp.arange(columns.shape[0], dtype=jnp.int32)
    same = columns[:, None] == columns[None, :]
    repeated = jnp.any(same & (positions[None, :] < positions[:, None]), axis=1)
    ahead = (owners[:, None] == owners[None, :]) & (columns[None, :] < columns[:, None])
    ranks = jnp.sum(ahead & ~repeated[None, :], axis=1, dtype=jnp.int32)
    rounds_of = jnp.array([[0, 2, 3, 1], [2, 0, 1, 3], [3, 1, 0, 2], [1, 3, 2, 0]], jnp.int32)
    their_plane = owners // plane
    among = their_plane[:, None] == jnp.arange(PLANES)
    turn = jnp.sum(jnp.where(among, pick_row(rounds_of, z)[None, :], 0), axis=1)
    seats = (owners % plane) * capacity + ranks
    nothing = blocks_here + 3 * seats_all
    final = (turn == 3) | (end & (turn == 1))
    slots = jnp.where(final, nothing, blocks_here + turn * seats_all + seats)
    slots = jnp.where(owners == myself, within, slots)
    seats = jnp.where(turn == 3, seats + seats_all, seats)

    last = final.reshape(blocks_here, per_block)
    counts = jnp.sum(last, axis=1, dtype=jnp.int32)
    order_in = jnp.cumsum(last, axis=1) - 1
    spots = jnp.arange(REM_PB, dtype=jnp.int32)
    chair = last[:, None, :] & (order_in[:, None, :] == spots[:, None])
    late = jnp.sum(jnp.where(chair, jnp.arange(per_block, dtype=jnp.int32), 0), axis=2, dtype=jnp.int32)
    late_slots = jnp.sum(
        jnp.where(chair, seats.reshape(blocks_here, 1, per_block), 0), axis=2, dtype=jnp.int32
    )

    always = jnp.zeros((1,), jnp.int32)
    inner = (~end).astype(jnp.int32)[None]
    picked = choose(always, [near], [0], [local], LIGHT)
    got = [exchange(picked)]
    opposite, _ = lax.optimization_barrier((near[PLANES:], picked))
    across = shift(opposite, [(0, PLANES - 1), (PLANES - 1, 0)])
    across, _, _ = lax.optimization_barrier((across, beyond, near_by))
    picked = choose(inner, [across, near], [0, 1], [local, beyond], LIGHT)
    leaving, _ = lax.optimization_barrier((picked, got[0]))
    got.append(exchange(leaving))
    far_out, far_in = shift(beyond, outward), shift(near_by, swap)
    leaving, _, _ = lax.optimization_barrier((got[1], far_out, far_in))
    crossed = shift(leaving, [(0, PLANES - 1), (PLANES - 1, 0)])
    near, _ = lax.optimization_barrier((near, picked))
    got.append(exchange(choose(always, [near], [2], [near_by], HEAVY)))
    got.append(exchange(choose(inner, [near], [3], [far_out, far_in], LIGHT)))

    sums, left = early(slots, late.reshape(-1), counts, [local] + got[:3], tile_masks)
    return layer(
        late_slots.reshape(-1),
        counts,
        end.astype(jnp.int32)[None],
        [crossed, got[3]],
        sums,
        left,
        degree.reshape(blocks_here, tile),
        features,
        weight,
    )


def solution(mesh):
    in_specs = (P("rows", None), P("rows", None), P("rows", None, None, None), P("rows"), P())
    out_specs = P("rows", None)
    return jax.shard_map(
        on_device, mesh=mesh, in_specs=in_specs, out_specs=out_specs, check_vma=False
    )
```

```python
import functools

import jax
import jax.numpy as jnp
from jax import lax
from jax.experimental import pallas as pl
from jax.experimental.pallas import tpu as pltpu
from jax.sharding import PartitionSpec as P

REM_PB = 4
PLANES = 4
HEAVY = 3 * 10**10
LIGHT = 10**10
CUT = 4

VMEM_LIMIT = 62 * 1024 * 1024


def pick_row(table, z):
    return jnp.sum(jnp.where(jnp.arange(table.shape[0])[:, None] == z, table, 0), axis=0)


def choose_kernel(which, *refs, turns):
    lists, (*froms, out, held, in_sems, out_sems) = refs[: len(turns)], refs[len(turns) :]
    count, seats = out.shape[0], lists[0].shape[2]
    groups = in_sems.shape[0]
    size = count // groups
    for j, source in enumerate(froms):
        ids, turn = lists[j % len(turns)], turns[j % len(turns)]

        @pl.when(which[0] == j)
        def _():
            for n in range(count):
                block = source.at[ids[turn, n // seats, n % seats]]
                pltpu.make_async_copy(block, held.at[n], in_sems.at[n // size]).start()

    leaving = []
    for g in range(groups):
        here = pl.ds(g * size, size)
        pltpu.make_async_copy(out.at[here], held.at[here], in_sems.at[g]).wait()
        leaving.append(pltpu.make_async_copy(held.at[here], out.at[here], out_sems.at[g]))
        leaving[-1].start()
    for copy in leaving:
        copy.wait()


def choose(which, lists, turns, froms, flops):
    out = (lists[0].shape[1] * lists[0].shape[2],) + froms[0].shape[1:]
    moved = out[0] * out[1] * out[2] * 2
    groups = 4 if out[0] % 4 == 0 else 1
    return pl.pallas_call(
        functools.partial(choose_kernel, turns=turns),
        grid_spec=pltpu.PrefetchScalarGridSpec(
            num_scalar_prefetch=1 + len(lists),
            grid=(1,),
            in_specs=[pl.BlockSpec(memory_space=pltpu.HBM)] * len(froms),
            out_specs=pl.BlockSpec(memory_space=pltpu.HBM),
            scratch_shapes=[
                pltpu.VMEM(out, froms[0].dtype),
                pltpu.SemaphoreType.DMA((groups,)),
                pltpu.SemaphoreType.DMA((groups,)),
            ],
        ),
        out_shape=jax.ShapeDtypeStruct(out, froms[0].dtype),
        compiler_params=pltpu.CompilerParams(vmem_limit_bytes=VMEM_LIMIT),
        cost_estimate=pl.CostEstimate(flops=flops, bytes_accessed=2 * moved, transcendentals=0),
        name="choose_blocks",
    )(which, *lists, *froms)


def fill(pieces, table, sems, at=0):
    copies, cut = [], sems.shape[1]
    for n, piece in enumerate(pieces):
        size = piece.shape[0] // cut
        for c in range(cut):
            here = table.at[pl.ds(at + c * size, size)]
            copies.append(pltpu.make_async_copy(piece.at[pl.ds(c * size, size)], here, sems.at[n, c]))
        at += piece.shape[0]
    for copy in copies:
        copy.start()
    return copies


def early_kernel(slots, late, counts, *refs):
    *froms, masks, sums, left, table, sems = refs
    step = pl.program_id(0)
    rows, per_block = masks.shape[:2]
    tile, width = table.shape[1:]
    spare = left.shape[2] // tile

    @pl.when(step == 0)
    def _():
        table[table.shape[0] - 1] = jnp.zeros((tile, width), table.dtype)
        for copy in fill(froms, table, sems):
            copy.wait()

    for r in range(rows):
        row = step * rows + r
        here = pl.ds(r * tile, tile)
        mask = jnp.concatenate(
            [masks[r, t].astype(jnp.float32).astype(jnp.bfloat16) for t in range(per_block)], axis=1
        )
        picked = jnp.concatenate(
            [table[slots[row * per_block + t]] for t in range(per_block)], axis=0
        )
        sums[here, :] = jnp.dot(mask, picked, preferred_element_type=jnp.float32)
        for t in range(spare):
            kept = masks[r, late[row * spare + t]].astype(jnp.float32)
            kept = jnp.where(t < counts[row], kept, 0.0).astype(jnp.bfloat16)
            left[r, :, t * tile : (t + 1) * tile] = kept


def early(slots, late, counts, froms, tile_masks):
    blocks_here, per_block, tile, _ = tile_masks.shape
    width = froms[0].shape[2]
    spare = late.shape[0] // blocks_here
    rows = 4 if blocks_here % 4 == 0 else 1
    blocks_in_table = sum(piece.shape[0] for piece in froms) + 1
    return pl.pallas_call(
        early_kernel,
        grid_spec=pltpu.PrefetchScalarGridSpec(
            num_scalar_prefetch=3,
            grid=(blocks_here // rows,),
            in_specs=[pl.BlockSpec(memory_space=pl.ANY)] * len(froms)
            + [pl.BlockSpec((rows, per_block, tile, tile), lambda r, *_: (r, 0, 0, 0))],
            out_specs=[
                pl.BlockSpec((rows * tile, width), lambda r, *_: (r, 0)),
                pl.BlockSpec((rows, tile, spare * tile), lambda r, *_: (r, 0, 0)),
            ],
            scratch_shapes=[
                pltpu.VMEM((blocks_in_table, tile, width), jnp.bfloat16),
                pltpu.SemaphoreType.DMA((len(froms), CUT)),
            ],
        ),
        out_shape=[
            jax.ShapeDtypeStruct((blocks_here * tile, width), jnp.float32),
            jax.ShapeDtypeStruct((blocks_here, tile, spare * tile), jnp.bfloat16),
        ],
        compiler_params=pltpu.CompilerParams(vmem_limit_bytes=VMEM_LIMIT),
        cost_estimate=pl.CostEstimate(
            flops=2 * LIGHT,
            bytes_accessed=blocks_here * per_block * tile * tile * 6 + blocks_in_table * tile * width * 2,
            transcendentals=0,
        ),
        name="early_sums",
    )(slots, late, counts, *froms, tile_masks)


def layer_kernel(slots, counts, end, crossed, last, *refs):
    sums, left, degree, features, weight, out, table, totals, share, sems, far_sems = refs
    step = pl.program_id(0)
    rows, tile = left.shape[:2]
    width = table.shape[2]
    spare = left.shape[2] // tile
    pair = min(2, spare)

    @pl.when(step == 0)
    def _():
        size = crossed.shape[0]
        copies = fill([last], table, sems, size)

        @pl.when(end[0] == 1)
        def _():
            fill([crossed], table, far_sems)

        @pl.when(end[0] == 0)
        def _():
            table[0] = jnp.zeros((tile, width), table.dtype)

        column = lax.broadcasted_iota(jnp.int32, (tile, tile), 1)
        diagonal = lax.broadcasted_iota(jnp.int32, (tile, tile), 0) == column
        ones = jnp.ones((2 * tile, tile), jnp.bfloat16)
        for first in range(0, degree.shape[0], rows):
            spread = []
            for row in range(first, first + rows):
                count = degree[row : row + 1, :]
                small = count & 7
                halves = [
                    jnp.where(diagonal, part.astype(jnp.float32), 0.0).astype(jnp.bfloat16)
                    for part in (count - small, small)
                ]
                spread.append(jnp.concatenate(halves, axis=1))
            share[first * tile : (first + rows) * tile, :] = 1.0 / jnp.dot(
                jnp.concatenate(spread, axis=0), ones, preferred_element_type=jnp.float32
            )
        for copy in copies:
            copy.wait()

        @pl.when(end[0] == 1)
        def _():
            for c in range(CUT):
                here = pl.ds(c * (size // CUT), size // CUT)
                pltpu.make_async_copy(crossed.at[here], table.at[here], far_sems.at[0, c]).wait()

    def added(r, first):
        ends = min(first + pair, spare)
        picked = [table[slots[(step * rows + r) * spare + t]] for t in range(first, ends)]
        mask = left[r, :, first * tile : ends * tile]
        return jnp.dot(mask, jnp.concatenate(picked, axis=0), preferred_element_type=jnp.float32)

    for r in range(rows):
        here = pl.ds(r * tile, tile)
        totals[here, :] = sums[here, :] + added(r, 0)
    for r in range(rows):
        here = pl.ds(r * tile, tile)
        for first in range(pair, spare, pair):

            @pl.when(counts[step * rows + r] > first)
            def _():
                totals[here, :] += added(r, first)

    many = rows * tile
    for first in range(0, rows * tile, many):
        here = pl.ds(first, many)
        there = pl.ds(pl.multiple_of(step * rows * tile + first, tile), many)
        part = jnp.concatenate([share[there, :]] * (width // tile), axis=1)
        mean = (totals[here, :] * part).astype(jnp.bfloat16)
        joined = jnp.concatenate([features[here, :], mean], axis=1)
        hidden = jnp.dot(joined, weight[...], preferred_element_type=jnp.float32)
        hidden = jnp.maximum(hidden, 0.0)
        scale = lax.rsqrt(jnp.sum(hidden * hidden, axis=1, keepdims=True) + 1e-06)
        out[here, :] = (hidden * scale).astype(jnp.bfloat16)


def layer(slots, counts, end, froms, sums, left, degree, features, weight):
    blocks_here, tile, across = left.shape
    width = features.shape[1]
    out_width = weight.shape[1]
    rows = 8 if blocks_here % 8 == 0 else 1
    items = rows * tile
    blocks_in_table = sum(piece.shape[0] for piece in froms)
    return pl.pallas_call(
        layer_kernel,
        grid_spec=pltpu.PrefetchScalarGridSpec(
            num_scalar_prefetch=3,
            grid=(blocks_here // rows,),
            in_specs=[pl.BlockSpec(memory_space=pl.ANY)] * len(froms)
            + [
                pl.BlockSpec((items, width), lambda r, *_: (r, 0)),
                pl.BlockSpec((rows, tile, across), lambda r, *_: (r, 0, 0)),
                pl.BlockSpec((blocks_here, tile), lambda r, *_: (0, 0)),
                pl.BlockSpec((items, width), lambda r, *_: (r, 0)),
                pl.BlockSpec((2 * width, out_width), lambda r, *_: (0, 0)),
            ],
            out_specs=pl.BlockSpec((items, out_width), lambda r, *_: (r, 0)),
            scratch_shapes=[
                pltpu.VMEM((blocks_in_table, tile, width), jnp.bfloat16),
                pltpu.VMEM((items, width), jnp.float32),
                pltpu.VMEM((blocks_here * tile, tile), jnp.float32),
                pltpu.SemaphoreType.DMA((1, CUT)),
                pltpu.SemaphoreType.DMA((1, CUT)),
            ],
        ),
        out_shape=jax.ShapeDtypeStruct((blocks_here * tile, out_width), jnp.bfloat16),
        compiler_params=pltpu.CompilerParams(vmem_limit_bytes=VMEM_LIMIT),
        cost_estimate=pl.CostEstimate(
            flops=2 * blocks_here * tile * (across + 2 * width) * out_width,
            bytes_accessed=blocks_here * tile * (4 * width + 2 * across + 2 * width + 2 * out_width),
            transcendentals=blocks_here * tile,
        ),
        name="sage_layer",
    )(slots, counts, end, *froms, sums, left, degree, features, weight)


def on_device(features, tile_cols, tile_masks, degree, weight):
    blocks_here, per_block = tile_cols.shape
    tile = tile_masks.shape[2]
    width = features.shape[1]
    peers = lax.axis_size("rows")
    plane = peers // PLANES
    myself = lax.axis_index("rows")
    z, p = myself // plane, myself % plane
    end = (z == 0) | (z == PLANES - 1)
    capacity = max(2, (REM_PB * blocks_here + peers - 2) // (peers - 1))
    seats_all = plane * capacity
    local = features.reshape(blocks_here, tile, width)
    columns = tile_cols.reshape(-1)
    groups = [[a * plane + q for q in range(plane)] for a in range(PLANES)]

    def exchange(x):
        return lax.all_to_all(
            x, "rows", split_axis=0, concat_axis=0, axis_index_groups=groups, tiled=True
        )

    def shift(x, moves):
        pairs = [(a * plane + q, b * plane + q) for a, b in moves for q in range(plane)]
        return lax.ppermute(x, "rows", pairs)

    asked = exchange(jnp.broadcast_to(columns, (plane,) + columns.shape))
    swap, outward, beside = [(1, 2), (2, 1)], [(1, 0), (2, 3)], [(0, 1), (1, 0), (2, 3), (3, 2)]
    near_by, beyond = shift(local, beside), shift(local, swap)

    rounds = jnp.array([[0, 0, 1, 2], [1, 2, 0, 3], [2, 1, 3, 0], [3, 3, 2, 1]], jnp.int32)
    line = jnp.append(pick_row(rounds, z), PLANES - 1 - z) * plane + p
    blocks = jnp.arange(blocks_here, dtype=jnp.int32)
    wanted = line[:, None] * blocks_here + blocks[None, :]
    below = blocks[:, None] > blocks[None, :]
    seat = jnp.arange(capacity, dtype=jnp.int32)

    def seated(asking, wanted):
        need = jnp.any(asking[:, None, :, None] == wanted[None, :, None, :], axis=2).astype(jnp.int32)
        place = jnp.sum(jnp.where(below, need[:, :, None, :], 0), axis=3)
        taken = (need[:, :, None, :] == 1) & (place[:, :, None, :] == seat[:, None])
        return jnp.sum(jnp.where(taken, blocks, 0), axis=3)

    near = jnp.swapaxes(seated(asked, wanted), 0, 1)

    owners, within = columns // blocks_here, columns % blocks_here
    positions = jnp.arange(columns.shape[0], dtype=jnp.int32)
    same = columns[:, None] == columns[None, :]
    repeated = jnp.any(same & (positions[None, :] < positions[:, None]), axis=1)
    ahead = (owners[:, None] == owners[None, :]) & (columns[None, :] < columns[:, None])
    ranks = jnp.sum(ahead & ~repeated[None, :], axis=1, dtype=jnp.int32)
    rounds_of = jnp.array([[0, 2, 3, 1], [2, 0, 1, 3], [3, 1, 0, 2], [1, 3, 2, 0]], jnp.int32)
    their_plane = owners // plane
    among = their_plane[:, None] == jnp.arange(PLANES)
    turn = jnp.sum(jnp.where(among, pick_row(rounds_of, z)[None, :], 0), axis=1)
    seats = (owners % plane) * capacity + ranks
    nothing = blocks_here + 3 * seats_all
    final = (turn == 3) | (end & (turn == 1))
    slots = jnp.where(final, nothing, blocks_here + turn * seats_all + seats)
    slots = jnp.where(owners == myself, within, slots)
    seats = jnp.where(turn == 3, seats + seats_all, seats)

    last = final.reshape(blocks_here, per_block)
    counts = jnp.sum(last, axis=1, dtype=jnp.int32)
    order_in = jnp.cumsum(last, axis=1) - 1
    spots = jnp.arange(REM_PB, dtype=jnp.int32)
    chair = last[:, None, :] & (order_in[:, None, :] == spots[:, None])
    late = jnp.sum(jnp.where(chair, jnp.arange(per_block, dtype=jnp.int32), 0), axis=2, dtype=jnp.int32)
    late_slots = jnp.sum(
        jnp.where(chair, seats.reshape(blocks_here, 1, per_block), 0), axis=2, dtype=jnp.int32
    )

    always = jnp.zeros((1,), jnp.int32)
    inner = (~end).astype(jnp.int32)[None]
    picked = choose(always, [near], [0], [local], LIGHT)
    got = [exchange(picked)]
    opposite, _ = lax.optimization_barrier((near[PLANES:], picked))
    across = shift(opposite, [(0, PLANES - 1), (PLANES - 1, 0)])
    across, _, _ = lax.optimization_barrier((across, beyond, near_by))
    picked = choose(inner, [across, near], [0, 1], [local, beyond], LIGHT)
    leaving, _ = lax.optimization_barrier((picked, got[0]))
    got.append(exchange(leaving))
    far_out, far_in = shift(beyond, outward), shift(near_by, swap)
    leaving, _, _ = lax.optimization_barrier((got[1], far_out, far_in))
    crossed = shift(leaving, [(0, PLANES - 1), (PLANES - 1, 0)])
    near, _ = lax.optimization_barrier((near, picked))
    got.append(exchange(choose(always, [near], [2], [near_by], HEAVY)))
    got.append(exchange(choose(inner, [near], [3], [far_out, far_in], LIGHT)))

    sums, left = early(slots, late.reshape(-1), counts, [local] + got[:3], tile_masks)
    return layer(
        late_slots.reshape(-1),
        counts,
        end.astype(jnp.int32)[None],
        [crossed, got[3]],
        sums,
        left,
        degree.reshape(blocks_here, tile),
        features,
        weight,
    )


def solution(mesh):
    in_specs = (P("rows", None), P("rows", None), P("rows", None, None, None), P("rows"), P())
    out_specs = P("rows", None)
    return jax.shard_map(
        on_device, mesh=mesh, in_specs=in_specs, out_specs=out_specs, check_vma=False
    )
```

```python
import functools

import jax
import jax.numpy as jnp
from jax import lax
from jax.experimental import pallas as pl
from jax.experimental.pallas import tpu as pltpu
from jax.sharding import PartitionSpec as P

REM_PB = 4
PLANES = 4
HEAVY = 3 * 10**10
LIGHT = 10**10
CUT = 4

VMEM_LIMIT = 62 * 1024 * 1024


def pick_row(table, z):
    return jnp.sum(jnp.where(jnp.arange(table.shape[0])[:, None] == z, table, 0), axis=0)


def choose_kernel(which, *refs, turns):
    lists, (*froms, out, held, in_sems, out_sems) = refs[: len(turns)], refs[len(turns) :]
    count, seats = out.shape[0], lists[0].shape[2]
    groups = in_sems.shape[0]
    size = count // groups
    for j, source in enumerate(froms):
        ids, turn = lists[j % len(turns)], turns[j % len(turns)]

        @pl.when(which[0] == j)
        def _():
            for n in range(count):
                block = source.at[ids[turn, n // seats, n % seats]]
                pltpu.make_async_copy(block, held.at[n], in_sems.at[n // size]).start()

    leaving = []
    for g in range(groups):
        here = pl.ds(g * size, size)
        pltpu.make_async_copy(out.at[here], held.at[here], in_sems.at[g]).wait()
        leaving.append(pltpu.make_async_copy(held.at[here], out.at[here], out_sems.at[g]))
        leaving[-1].start()
    for copy in leaving:
        copy.wait()


def choose(which, lists, turns, froms, flops):
    out = (lists[0].shape[1] * lists[0].shape[2],) + froms[0].shape[1:]
    moved = out[0] * out[1] * out[2] * 2
    groups = 4 if out[0] % 4 == 0 else 1
    return pl.pallas_call(
        functools.partial(choose_kernel, turns=turns),
        grid_spec=pltpu.PrefetchScalarGridSpec(
            num_scalar_prefetch=1 + len(lists),
            grid=(1,),
            in_specs=[pl.BlockSpec(memory_space=pltpu.HBM)] * len(froms),
            out_specs=pl.BlockSpec(memory_space=pltpu.HBM),
            scratch_shapes=[
                pltpu.VMEM(out, froms[0].dtype),
                pltpu.SemaphoreType.DMA((groups,)),
                pltpu.SemaphoreType.DMA((groups,)),
            ],
        ),
        out_shape=jax.ShapeDtypeStruct(out, froms[0].dtype),
        compiler_params=pltpu.CompilerParams(vmem_limit_bytes=VMEM_LIMIT),
        cost_estimate=pl.CostEstimate(flops=flops, bytes_accessed=2 * moved, transcendentals=0),
        name="choose_blocks",
    )(which, *lists, *froms)


def fill(pieces, table, sems, at=0):
    copies, cut = [], sems.shape[1]
    for n, piece in enumerate(pieces):
        size = piece.shape[0] // cut
        for c in range(cut):
            here = table.at[pl.ds(at + c * size, size)]
            copies.append(pltpu.make_async_copy(piece.at[pl.ds(c * size, size)], here, sems.at[n, c]))
        at += piece.shape[0]
    for copy in copies:
        copy.start()
    return copies


def early_kernel(slots, late, counts, *refs):
    *froms, masks, sums, left, table, sems = refs
    step = pl.program_id(0)
    rows, per_block = masks.shape[:2]
    tile, width = table.shape[1:]
    spare = left.shape[2] // tile

    @pl.when(step == 0)
    def _():
        table[table.shape[0] - 1] = jnp.zeros((tile, width), table.dtype)
        for copy in fill(froms, table, sems):
            copy.wait()

    for r in range(rows):
        row = step * rows + r
        here = pl.ds(r * tile, tile)
        mask = jnp.concatenate(
            [masks[r, t].astype(jnp.float32).astype(jnp.bfloat16) for t in range(per_block)], axis=1
        )
        picked = jnp.concatenate(
            [table[slots[row * per_block + t]] for t in range(per_block)], axis=0
        )
        sums[here, :] = jnp.dot(mask, picked, preferred_element_type=jnp.float32)
        for t in range(spare):
            kept = jnp.where(t < counts[row], masks[r, late[row * spare + t]], 0)
            left[r, :, t * tile : (t + 1) * tile] = kept.astype(jnp.int8)


def early(slots, late, counts, froms, tile_masks):
    blocks_here, per_block, tile, _ = tile_masks.shape
    width = froms[0].shape[2]
    spare = late.shape[0] // blocks_here
    rows = 4 if blocks_here % 4 == 0 else 1
    blocks_in_table = sum(piece.shape[0] for piece in froms) + 1
    return pl.pallas_call(
        early_kernel,
        grid_spec=pltpu.PrefetchScalarGridSpec(
            num_scalar_prefetch=3,
            grid=(blocks_here // rows,),
            in_specs=[pl.BlockSpec(memory_space=pl.ANY)] * len(froms)
            + [pl.BlockSpec((rows, per_block, tile, tile), lambda r, *_: (r, 0, 0, 0))],
            out_specs=[
                pl.BlockSpec((rows * tile, width), lambda r, *_: (r, 0)),
                pl.BlockSpec((rows, tile, spare * tile), lambda r, *_: (r, 0, 0)),
            ],
            scratch_shapes=[
                pltpu.VMEM((blocks_in_table, tile, width), jnp.bfloat16),
                pltpu.SemaphoreType.DMA((len(froms), CUT)),
            ],
        ),
        out_shape=[
            jax.ShapeDtypeStruct((blocks_here * tile, width), jnp.float32),
            jax.ShapeDtypeStruct((blocks_here, tile, spare * tile), jnp.int8),
        ],
        compiler_params=pltpu.CompilerParams(vmem_limit_bytes=VMEM_LIMIT),
        cost_estimate=pl.CostEstimate(
            flops=2 * LIGHT,
            bytes_accessed=blocks_here * per_block * tile * tile * 6 + blocks_in_table * tile * width * 2,
            transcendentals=0,
        ),
        name="early_sums",
    )(slots, late, counts, *froms, tile_masks)


def layer_kernel(slots, counts, end, crossed, last, *refs):
    sums, left, degree, features, weight, out, table, totals, share, sems, far_sems = refs
    step = pl.program_id(0)
    rows, tile = left.shape[:2]
    width = table.shape[2]
    spare = left.shape[2] // tile
    pair = min(2, spare)

    @pl.when(step == 0)
    def _():
        size = crossed.shape[0]
        copies = fill([last], table, sems, size)

        @pl.when(end[0] == 1)
        def _():
            fill([crossed], table, far_sems)

        @pl.when(end[0] == 0)
        def _():
            table[0] = jnp.zeros((tile, width), table.dtype)

        column = lax.broadcasted_iota(jnp.int32, (tile, tile), 1)
        diagonal = lax.broadcasted_iota(jnp.int32, (tile, tile), 0) == column
        ones = jnp.ones((2 * tile, tile), jnp.bfloat16)
        for first in range(0, degree.shape[0], rows):
            spread = []
            for row in range(first, first + rows):
                count = degree[row : row + 1, :]
                small = count & 7
                halves = [
                    jnp.where(diagonal, part.astype(jnp.float32), 0.0).astype(jnp.bfloat16)
                    for part in (count - small, small)
                ]
                spread.append(jnp.concatenate(halves, axis=1))
            share[first * tile : (first + rows) * tile, :] = 1.0 / jnp.dot(
                jnp.concatenate(spread, axis=0), ones, preferred_element_type=jnp.float32
            )
        for copy in copies:
            copy.wait()

        @pl.when(end[0] == 1)
        def _():
            for c in range(CUT):
                here = pl.ds(c * (size // CUT), size // CUT)
                pltpu.make_async_copy(crossed.at[here], table.at[here], far_sems.at[0, c]).wait()

    def added(r, first):
        ends = min(first + pair, spare)
        picked = [table[slots[(step * rows + r) * spare + t]] for t in range(first, ends)]
        mask = left[r, :, first * tile : ends * tile].astype(jnp.int32)
        mask = mask.astype(jnp.float32).astype(jnp.bfloat16)
        return jnp.dot(mask, jnp.concatenate(picked, axis=0), preferred_element_type=jnp.float32)

    for r in range(rows):
        here = pl.ds(r * tile, tile)
        totals[here, :] = sums[here, :] + added(r, 0)
    for r in range(rows):
        here = pl.ds(r * tile, tile)
        for first in range(pair, spare, pair):

            @pl.when(counts[step * rows + r] > first)
            def _():
                totals[here, :] += added(r, first)

    many = rows * tile
    for first in range(0, rows * tile, many):
        here = pl.ds(first, many)
        there = pl.ds(pl.multiple_of(step * rows * tile + first, tile), many)
        part = jnp.concatenate([share[there, :]] * (width // tile), axis=1)
        mean = (totals[here, :] * part).astype(jnp.bfloat16)
        joined = jnp.concatenate([features[here, :], mean], axis=1)
        hidden = jnp.dot(joined, weight[...], preferred_element_type=jnp.float32)
        hidden = jnp.maximum(hidden, 0.0)
        scale = lax.rsqrt(jnp.sum(hidden * hidden, axis=1, keepdims=True) + 1e-06)
        out[here, :] = (hidden * scale).astype(jnp.bfloat16)


def layer(slots, counts, end, froms, sums, left, degree, features, weight):
    blocks_here, tile, across = left.shape
    width = features.shape[1]
    out_width = weight.shape[1]
    rows = 8 if blocks_here % 8 == 0 else 1
    items = rows * tile
    blocks_in_table = sum(piece.shape[0] for piece in froms)
    return pl.pallas_call(
        layer_kernel,
        grid_spec=pltpu.PrefetchScalarGridSpec(
            num_scalar_prefetch=3,
            grid=(blocks_here // rows,),
            in_specs=[pl.BlockSpec(memory_space=pl.ANY)] * len(froms)
            + [
                pl.BlockSpec((items, width), lambda r, *_: (r, 0)),
                pl.BlockSpec((rows, tile, across), lambda r, *_: (r, 0, 0)),
                pl.BlockSpec((blocks_here, tile), lambda r, *_: (0, 0)),
                pl.BlockSpec((items, width), lambda r, *_: (r, 0)),
                pl.BlockSpec((2 * width, out_width), lambda r, *_: (0, 0)),
            ],
            out_specs=pl.BlockSpec((items, out_width), lambda r, *_: (r, 0)),
            scratch_shapes=[
                pltpu.VMEM((blocks_in_table, tile, width), jnp.bfloat16),
                pltpu.VMEM((items, width), jnp.float32),
                pltpu.VMEM((blocks_here * tile, tile), jnp.float32),
                pltpu.SemaphoreType.DMA((1, CUT)),
                pltpu.SemaphoreType.DMA((1, CUT)),
            ],
        ),
        out_shape=jax.ShapeDtypeStruct((blocks_here * tile, out_width), jnp.bfloat16),
        compiler_params=pltpu.CompilerParams(vmem_limit_bytes=VMEM_LIMIT),
        cost_estimate=pl.CostEstimate(
            flops=2 * blocks_here * tile * (across + 2 * width) * out_width,
            bytes_accessed=blocks_here * tile * (4 * width + across + 2 * width + 2 * out_width),
            transcendentals=blocks_here * tile,
        ),
        name="sage_layer",
    )(slots, counts, end, *froms, sums, left, degree, features, weight)


def on_device(features, tile_cols, tile_masks, degree, weight):
    blocks_here, per_block = tile_cols.shape
    tile = tile_masks.shape[2]
    width = features.shape[1]
    peers = lax.axis_size("rows")
    plane = peers // PLANES
    myself = lax.axis_index("rows")
    z, p = myself // plane, myself % plane
    end = (z == 0) | (z == PLANES - 1)
    capacity = max(2, (REM_PB * blocks_here + peers - 2) // (peers - 1))
    seats_all = plane * capacity
    local = features.reshape(blocks_here, tile, width)
    columns = tile_cols.reshape(-1)
    groups = [[a * plane + q for q in range(plane)] for a in range(PLANES)]

    def exchange(x):
        return lax.all_to_all(
            x, "rows", split_axis=0, concat_axis=0, axis_index_groups=groups, tiled=True
        )

    def shift(x, moves):
        pairs = [(a * plane + q, b * plane + q) for a, b in moves for q in range(plane)]
        return lax.ppermute(x, "rows", pairs)

    asked = exchange(jnp.broadcast_to(columns, (plane,) + columns.shape))
    swap, outward, beside = [(1, 2), (2, 1)], [(1, 0), (2, 3)], [(0, 1), (1, 0), (2, 3), (3, 2)]
    near_by, beyond = shift(local, beside), shift(local, swap)

    rounds = jnp.array([[0, 0, 1, 2], [1, 2, 0, 3], [2, 1, 3, 0], [3, 3, 2, 1]], jnp.int32)
    line = jnp.append(pick_row(rounds, z), PLANES - 1 - z) * plane + p
    blocks = jnp.arange(blocks_here, dtype=jnp.int32)
    wanted = line[:, None] * blocks_here + blocks[None, :]
    below = blocks[:, None] > blocks[None, :]
    seat = jnp.arange(capacity, dtype=jnp.int32)

    def seated(asking, wanted):
        need = jnp.any(asking[:, None, :, None] == wanted[None, :, None, :], axis=2).astype(jnp.int32)
        place = jnp.sum(jnp.where(below, need[:, :, None, :], 0), axis=3)
        taken = (need[:, :, None, :] == 1) & (place[:, :, None, :] == seat[:, None])
        return jnp.sum(jnp.where(taken, blocks, 0), axis=3)

    near = jnp.swapaxes(seated(asked, wanted), 0, 1)

    owners, within = columns // blocks_here, columns % blocks_here
    positions = jnp.arange(columns.shape[0], dtype=jnp.int32)
    same = columns[:, None] == columns[None, :]
    repeated = jnp.any(same & (positions[None, :] < positions[:, None]), axis=1)
    ahead = (owners[:, None] == owners[None, :]) & (columns[None, :] < columns[:, None])
    ranks = jnp.sum(ahead & ~repeated[None, :], axis=1, dtype=jnp.int32)
    rounds_of = jnp.array([[0, 2, 3, 1], [2, 0, 1, 3], [3, 1, 0, 2], [1, 3, 2, 0]], jnp.int32)
    their_plane = owners // plane
    among = their_plane[:, None] == jnp.arange(PLANES)
    turn = jnp.sum(jnp.where(among, pick_row(rounds_of, z)[None, :], 0), axis=1)
    seats = (owners % plane) * capacity + ranks
    nothing = blocks_here + 3 * seats_all
    final = (turn == 3) | (end & (turn == 1))
    slots = jnp.where(final, nothing, blocks_here + turn * seats_all + seats)
    slots = jnp.where(owners == myself, within, slots)
    seats = jnp.where(turn == 3, seats + seats_all, seats)

    last = final.reshape(blocks_here, per_block)
    counts = jnp.sum(last, axis=1, dtype=jnp.int32)
    order_in = jnp.cumsum(last, axis=1) - 1
    spots = jnp.arange(REM_PB, dtype=jnp.int32)
    chair = last[:, None, :] & (order_in[:, None, :] == spots[:, None])
    late = jnp.sum(jnp.where(chair, jnp.arange(per_block, dtype=jnp.int32), 0), axis=2, dtype=jnp.int32)
    late_slots = jnp.sum(
        jnp.where(chair, seats.reshape(blocks_here, 1, per_block), 0), axis=2, dtype=jnp.int32
    )

    always = jnp.zeros((1,), jnp.int32)
    inner = (~end).astype(jnp.int32)[None]
    picked = choose(always, [near], [0], [local], LIGHT)
    got = [exchange(picked)]
    opposite, _ = lax.optimization_barrier((near[PLANES:], picked))
    across = shift(opposite, [(0, PLANES - 1), (PLANES - 1, 0)])
    across, _, _ = lax.optimization_barrier((across, beyond, near_by))
    picked = choose(inner, [across, near], [0, 1], [local, beyond], LIGHT)
    leaving, _ = lax.optimization_barrier((picked, got[0]))
    got.append(exchange(leaving))
    second, _ = lax.optimization_barrier((near_by, got[0]))
    far_out, far_in = shift(beyond, outward), shift(second, swap)
    leaving, _, _ = lax.optimization_barrier((got[1], far_out, far_in))
    crossed = shift(leaving, [(0, PLANES - 1), (PLANES - 1, 0)])
    near, _ = lax.optimization_barrier((near, picked))
    got.append(exchange(choose(always, [near], [2], [near_by], HEAVY)))
    got.append(exchange(choose(inner, [near], [3], [far_out, far_in], LIGHT)))

    sums, left = early(slots, late.reshape(-1), counts, [local] + got[:3], tile_masks)
    return layer(
        late_slots.reshape(-1),
        counts,
        end.astype(jnp.int32)[None],
        [crossed, got[3]],
        sums,
        left,
        degree.reshape(blocks_here, tile),
        features,
        weight,
    )


def solution(mesh):
    in_specs = (P("rows", None), P("rows", None), P("rows", None, None, None), P("rows"), P())
    out_specs = P("rows", None)
    return jax.shard_map(
        on_device, mesh=mesh, in_specs=in_specs, out_specs=out_specs, check_vma=False
    )
```

```python
import functools

import jax
import jax.numpy as jnp
from jax import lax
from jax.experimental import pallas as pl
from jax.experimental.pallas import tpu as pltpu
from jax.sharding import PartitionSpec as P

REM_PB = 4
PLANES = 4
HEAVY = 3 * 10**10
LIGHT = 10**10
CUT = 4

VMEM_LIMIT = 62 * 1024 * 1024


def pick_row(table, z):
    return jnp.sum(jnp.where(jnp.arange(table.shape[0])[:, None] == z, table, 0), axis=0)


def choose_kernel(which, *refs, turns):
    lists, (*froms, out, held, in_sems, out_sems) = refs[: len(turns)], refs[len(turns) :]
    count, seats = out.shape[0], lists[0].shape[2]
    groups = in_sems.shape[0]
    size = count // groups
    for j, source in enumerate(froms):
        ids, turn = lists[j % len(turns)], turns[j % len(turns)]

        @pl.when(which[0] == j)
        def _():
            for n in range(count):
                block = source.at[ids[turn, n // seats, n % seats]]
                pltpu.make_async_copy(block, held.at[n], in_sems.at[n // size]).start()

    leaving = []
    for g in range(groups):
        here = pl.ds(g * size, size)
        pltpu.make_async_copy(out.at[here], held.at[here], in_sems.at[g]).wait()
        leaving.append(pltpu.make_async_copy(held.at[here], out.at[here], out_sems.at[g]))
        leaving[-1].start()
    for copy in leaving:
        copy.wait()


def choose(which, lists, turns, froms, flops):
    out = (lists[0].shape[1] * lists[0].shape[2],) + froms[0].shape[1:]
    moved = out[0] * out[1] * out[2] * 2
    groups = 1
    return pl.pallas_call(
        functools.partial(choose_kernel, turns=turns),
        grid_spec=pltpu.PrefetchScalarGridSpec(
            num_scalar_prefetch=1 + len(lists),
            grid=(1,),
            in_specs=[pl.BlockSpec(memory_space=pltpu.HBM)] * len(froms),
            out_specs=pl.BlockSpec(memory_space=pltpu.HBM),
            scratch_shapes=[
                pltpu.VMEM(out, froms[0].dtype),
                pltpu.SemaphoreType.DMA((groups,)),
                pltpu.SemaphoreType.DMA((groups,)),
            ],
        ),
        out_shape=jax.ShapeDtypeStruct(out, froms[0].dtype),
        compiler_params=pltpu.CompilerParams(vmem_limit_bytes=VMEM_LIMIT),
        cost_estimate=pl.CostEstimate(flops=flops, bytes_accessed=2 * moved, transcendentals=0),
        name="choose_blocks",
    )(which, *lists, *froms)


def fill(pieces, table, sems, at=0):
    copies, cut = [], sems.shape[1]
    for n, piece in enumerate(pieces):
        size = piece.shape[0] // cut
        for c in range(cut):
            here = table.at[pl.ds(at + c * size, size)]
            copies.append(pltpu.make_async_copy(piece.at[pl.ds(c * size, size)], here, sems.at[n, c]))
        at += piece.shape[0]
    for copy in copies:
        copy.start()
    return copies


def early_kernel(slots, late, counts, *refs):
    *froms, masks, sums, left, table, sems = refs
    step = pl.program_id(0)
    rows, per_block = masks.shape[:2]
    tile, width = table.shape[1:]
    spare = left.shape[2] // tile

    @pl.when(step == 0)
    def _():
        table[table.shape[0] - 1] = jnp.zeros((tile, width), table.dtype)
        for copy in fill(froms, table, sems):
            copy.wait()

    for r in range(rows):
        row = step * rows + r
        here = pl.ds(r * tile, tile)
        mask = jnp.concatenate(
            [masks[r, t].astype(jnp.float32).astype(jnp.bfloat16) for t in range(per_block)], axis=1
        )
        picked = jnp.concatenate(
            [table[slots[row * per_block + t]] for t in range(per_block)], axis=0
        )
        sums[here, :] = jnp.dot(mask, picked, preferred_element_type=jnp.float32)
        for t in range(spare):
            kept = jnp.where(t < counts[row], masks[r, late[row * spare + t]], 0)
            left[r, :, t * tile : (t + 1) * tile] = kept.astype(jnp.int8)


def early(slots, late, counts, froms, tile_masks):
    blocks_here, per_block, tile, _ = tile_masks.shape
    width = froms[0].shape[2]
    spare = late.shape[0] // blocks_here
    rows = 4 if blocks_here % 4 == 0 else 1
    blocks_in_table = sum(piece.shape[0] for piece in froms) + 1
    return pl.pallas_call(
        early_kernel,
        grid_spec=pltpu.PrefetchScalarGridSpec(
            num_scalar_prefetch=3,
            grid=(blocks_here // rows,),
            in_specs=[pl.BlockSpec(memory_space=pl.ANY)] * len(froms)
            + [pl.BlockSpec((rows, per_block, tile, tile), lambda r, *_: (r, 0, 0, 0))],
            out_specs=[
                pl.BlockSpec((rows * tile, width), lambda r, *_: (r, 0)),
                pl.BlockSpec((rows, tile, spare * tile), lambda r, *_: (r, 0, 0)),
            ],
            scratch_shapes=[
                pltpu.VMEM((blocks_in_table, tile, width), jnp.bfloat16),
                pltpu.SemaphoreType.DMA((len(froms), CUT)),
            ],
        ),
        out_shape=[
            jax.ShapeDtypeStruct((blocks_here * tile, width), jnp.float32),
            jax.ShapeDtypeStruct((blocks_here, tile, spare * tile), jnp.int8),
        ],
        compiler_params=pltpu.CompilerParams(vmem_limit_bytes=VMEM_LIMIT),
        cost_estimate=pl.CostEstimate(
            flops=2 * LIGHT,
            bytes_accessed=blocks_here * per_block * tile * tile * 6 + blocks_in_table * tile * width * 2,
            transcendentals=0,
        ),
        name="early_sums",
    )(slots, late, counts, *froms, tile_masks)


def layer_kernel(slots, counts, end, crossed, last, *refs):
    sums, left, degree, features, weight, out, table, totals, share, sems, far_sems = refs
    step = pl.program_id(0)
    rows, tile = left.shape[:2]
    width = table.shape[2]
    spare = left.shape[2] // tile
    pair = min(2, spare)

    @pl.when(step == 0)
    def _():
        size = crossed.shape[0]
        copies = fill([last], table, sems, size)

        @pl.when(end[0] == 1)
        def _():
            fill([crossed], table, far_sems)

        @pl.when(end[0] == 0)
        def _():
            table[0] = jnp.zeros((tile, width), table.dtype)

        column = lax.broadcasted_iota(jnp.int32, (tile, tile), 1)
        diagonal = lax.broadcasted_iota(jnp.int32, (tile, tile), 0) == column
        ones = jnp.ones((2 * tile, tile), jnp.bfloat16)
        for first in range(0, degree.shape[0], rows):
            spread = []
            for row in range(first, first + rows):
                count = degree[row : row + 1, :]
                small = count & 7
                halves = [
                    jnp.where(diagonal, part.astype(jnp.float32), 0.0).astype(jnp.bfloat16)
                    for part in (count - small, small)
                ]
                spread.append(jnp.concatenate(halves, axis=1))
            share[first * tile : (first + rows) * tile, :] = 1.0 / jnp.dot(
                jnp.concatenate(spread, axis=0), ones, preferred_element_type=jnp.float32
            )
        for copy in copies:
            copy.wait()

        @pl.when(end[0] == 1)
        def _():
            for c in range(CUT):
                here = pl.ds(c * (size // CUT), size // CUT)
                pltpu.make_async_copy(crossed.at[here], table.at[here], far_sems.at[0, c]).wait()

    def added(r, first):
        ends = min(first + pair, spare)
        picked = [table[slots[(step * rows + r) * spare + t]] for t in range(first, ends)]
        mask = left[r, :, first * tile : ends * tile].astype(jnp.int32)
        mask = mask.astype(jnp.float32).astype(jnp.bfloat16)
        return jnp.dot(mask, jnp.concatenate(picked, axis=0), preferred_element_type=jnp.float32)

    for r in range(rows):
        here = pl.ds(r * tile, tile)
        totals[here, :] = sums[here, :] + added(r, 0)
    for r in range(rows):
        here = pl.ds(r * tile, tile)
        for first in range(pair, spare, pair):

            @pl.when(counts[step * rows + r] > first)
            def _():
                totals[here, :] += added(r, first)

    many = rows * tile
    for first in range(0, rows * tile, many):
        here = pl.ds(first, many)
        there = pl.ds(pl.multiple_of(step * rows * tile + first, tile), many)
        part = jnp.concatenate([share[there, :]] * (width // tile), axis=1)
        mean = (totals[here, :] * part).astype(jnp.bfloat16)
        joined = jnp.concatenate([features[here, :], mean], axis=1)
        hidden = jnp.dot(joined, weight[...], preferred_element_type=jnp.float32)
        hidden = jnp.maximum(hidden, 0.0)
        scale = lax.rsqrt(jnp.sum(hidden * hidden, axis=1, keepdims=True) + 1e-06)
        out[here, :] = (hidden * scale).astype(jnp.bfloat16)


def layer(slots, counts, end, froms, sums, left, degree, features, weight):
    blocks_here, tile, across = left.shape
    width = features.shape[1]
    out_width = weight.shape[1]
    rows = 8 if blocks_here % 8 == 0 else 1
    items = rows * tile
    blocks_in_table = sum(piece.shape[0] for piece in froms)
    return pl.pallas_call(
        layer_kernel,
        grid_spec=pltpu.PrefetchScalarGridSpec(
            num_scalar_prefetch=3,
            grid=(blocks_here // rows,),
            in_specs=[pl.BlockSpec(memory_space=pl.ANY)] * len(froms)
            + [
                pl.BlockSpec((items, width), lambda r, *_: (r, 0)),
                pl.BlockSpec((rows, tile, across), lambda r, *_: (r, 0, 0)),
                pl.BlockSpec((blocks_here, tile), lambda r, *_: (0, 0)),
                pl.BlockSpec((items, width), lambda r, *_: (r, 0)),
                pl.BlockSpec((2 * width, out_width), lambda r, *_: (0, 0)),
            ],
            out_specs=pl.BlockSpec((items, out_width), lambda r, *_: (r, 0)),
            scratch_shapes=[
                pltpu.VMEM((blocks_in_table, tile, width), jnp.bfloat16),
                pltpu.VMEM((items, width), jnp.float32),
                pltpu.VMEM((blocks_here * tile, tile), jnp.float32),
                pltpu.SemaphoreType.DMA((1, CUT)),
                pltpu.SemaphoreType.DMA((1, CUT)),
            ],
        ),
        out_shape=jax.ShapeDtypeStruct((blocks_here * tile, out_width), jnp.bfloat16),
        compiler_params=pltpu.CompilerParams(vmem_limit_bytes=VMEM_LIMIT),
        cost_estimate=pl.CostEstimate(
            flops=2 * blocks_here * tile * (across + 2 * width) * out_width,
            bytes_accessed=blocks_here * tile * (4 * width + across + 2 * width + 2 * out_width),
            transcendentals=blocks_here * tile,
        ),
        name="sage_layer",
    )(slots, counts, end, *froms, sums, left, degree, features, weight)


def on_device(features, tile_cols, tile_masks, degree, weight):
    blocks_here, per_block = tile_cols.shape
    tile = tile_masks.shape[2]
    width = features.shape[1]
    peers = lax.axis_size("rows")
    plane = peers // PLANES
    myself = lax.axis_index("rows")
    z, p = myself // plane, myself % plane
    end = (z == 0) | (z == PLANES - 1)
    capacity = max(2, (REM_PB * blocks_here + peers - 2) // (peers - 1))
    seats_all = plane * capacity
    local = features.reshape(blocks_here, tile, width)
    columns = tile_cols.reshape(-1)
    groups = [[a * plane + q for q in range(plane)] for a in range(PLANES)]

    def exchange(x):
        return lax.all_to_all(
            x, "rows", split_axis=0, concat_axis=0, axis_index_groups=groups, tiled=True
        )

    def shift(x, moves):
        pairs = [(a * plane + q, b * plane + q) for a, b in moves for q in range(plane)]
        return lax.ppermute(x, "rows", pairs)

    asked = exchange(jnp.broadcast_to(columns, (plane,) + columns.shape))
    swap, outward, beside = [(1, 2), (2, 1)], [(1, 0), (2, 3)], [(0, 1), (1, 0), (2, 3), (3, 2)]
    near_by, beyond = shift(local, beside), shift(local, swap)

    rounds = jnp.array([[0, 0, 1, 2], [1, 2, 0, 3], [2, 1, 3, 0], [3, 3, 2, 1]], jnp.int32)
    line = jnp.append(pick_row(rounds, z), PLANES - 1 - z) * plane + p
    blocks = jnp.arange(blocks_here, dtype=jnp.int32)
    wanted = line[:, None] * blocks_here + blocks[None, :]
    below = blocks[:, None] > blocks[None, :]
    seat = jnp.arange(capacity, dtype=jnp.int32)

    def seated(asking, wanted):
        need = jnp.any(asking[:, None, :, None] == wanted[None, :, None, :], axis=2).astype(jnp.int32)
        place = jnp.sum(jnp.where(below, need[:, :, None, :], 0), axis=3)
        taken = (need[:, :, None, :] == 1) & (place[:, :, None, :] == seat[:, None])
        return jnp.sum(jnp.where(taken, blocks, 0), axis=3)

    near = jnp.swapaxes(seated(asked, wanted), 0, 1)

    owners, within = columns // blocks_here, columns % blocks_here
    positions = jnp.arange(columns.shape[0], dtype=jnp.int32)
    same = columns[:, None] == columns[None, :]
    repeated = jnp.any(same & (positions[None, :] < positions[:, None]), axis=1)
    ahead = (owners[:, None] == owners[None, :]) & (columns[None, :] < columns[:, None])
    ranks = jnp.sum(ahead & ~repeated[None, :], axis=1, dtype=jnp.int32)
    rounds_of = jnp.array([[0, 2, 3, 1], [2, 0, 1, 3], [3, 1, 0, 2], [1, 3, 2, 0]], jnp.int32)
    their_plane = owners // plane
    among = their_plane[:, None] == jnp.arange(PLANES)
    turn = jnp.sum(jnp.where(among, pick_row(rounds_of, z)[None, :], 0), axis=1)
    seats = (owners % plane) * capacity + ranks
    nothing = blocks_here + 3 * seats_all
    final = (turn == 3) | (end & (turn == 1))
    slots = jnp.where(final, nothing, blocks_here + turn * seats_all + seats)
    slots = jnp.where(owners == myself, within, slots)
    seats = jnp.where(turn == 3, seats + seats_all, seats)

    last = final.reshape(blocks_here, per_block)
    counts = jnp.sum(last, axis=1, dtype=jnp.int32)
    order_in = jnp.cumsum(last, axis=1) - 1
    spots = jnp.arange(REM_PB, dtype=jnp.int32)
    chair = last[:, None, :] & (order_in[:, None, :] == spots[:, None])
    late = jnp.sum(jnp.where(chair, jnp.arange(per_block, dtype=jnp.int32), 0), axis=2, dtype=jnp.int32)
    late_slots = jnp.sum(
        jnp.where(chair, seats.reshape(blocks_here, 1, per_block), 0), axis=2, dtype=jnp.int32
    )

    always = jnp.zeros((1,), jnp.int32)
    inner = (~end).astype(jnp.int32)[None]
    picked = choose(always, [near], [0], [local], LIGHT)
    got = [exchange(picked)]
    opposite, _ = lax.optimization_barrier((near[PLANES:], picked))
    across = shift(opposite, [(0, PLANES - 1), (PLANES - 1, 0)])
    across, _, _ = lax.optimization_barrier((across, beyond, near_by))
    picked = choose(inner, [across, near], [0, 1], [local, beyond], LIGHT)
    leaving, _ = lax.optimization_barrier((picked, got[0]))
    got.append(exchange(leaving))
    far_out, far_in = shift(beyond, outward), shift(near_by, swap)
    leaving, _, _ = lax.optimization_barrier((got[1], far_out, far_in))
    crossed = shift(leaving, [(0, PLANES - 1), (PLANES - 1, 0)])
    near, _ = lax.optimization_barrier((near, picked))
    got.append(exchange(choose(always, [near], [2], [near_by], HEAVY)))
    got.append(exchange(choose(inner, [near], [3], [far_out, far_in], LIGHT)))

    sums, left = early(slots, late.reshape(-1), counts, [local] + got[:3], tile_masks)
    return layer(
        late_slots.reshape(-1),
        counts,
        end.astype(jnp.int32)[None],
        [crossed, got[3]],
        sums,
        left,
        degree.reshape(blocks_here, tile),
        features,
        weight,
    )


def solution(mesh):
    in_specs = (P("rows", None), P("rows", None), P("rows", None, None, None), P("rows"), P())
    out_specs = P("rows", None)
    return jax.shard_map(
        on_device, mesh=mesh, in_specs=in_specs, out_specs=out_specs, check_vma=False
    )
```
